256 devices in a mesh: az: 8 (over y, x_lo), ax: 32 (over z, x_hi, core).
Axes of the slice: x: 4 (x_hi: 2, x_lo: 2; x = x_hi * 2 + x_lo), y: 4, z: 8, core: 2. Of those that a mesh axis runs over, the one named last changes fastest.
Arguments:
- velocity: float32 [3, 512, 64, 256], P(None, 'az', 'ax'), may hold values from -5 to 5
- viscosity: bfloat16 [512, 64, 256], P('az', 'ax'), may hold values from 0.5 to 2
- bfield: bfloat16 [3, 512, 64, 256], P(None, 'az', 'ax'), may hold values from -4 to 4
- particle_velocity: float32 [3, 2097152], P(None, ('az', 'ax')), may hold values from -5 to 5
- particle_cell: int32 [3, 2097152], P(None, ('az', 'ax')), may hold values from 0 to 511, as said below
- send_rows: int32 [256, 8, 128], P(('az', 'ax')), may hold values from 0 to 8191, as said below
- send_counts: int32 [8, 32, 8], P(None, 'ax'), may hold values from 0 to 128, as said below
Outputs:
- new_velocity: float32 [3, 512, 64, 256], P(None, 'az', 'ax')
- kept_velocity: float32 [3, 2097152], P(None, ('az', 'ax'))
- arrival_velocity: float32 [256, 3, 1024], P(('az', 'ax'))
The draws below stay inside these ranges and needn't reach their ends.
Inputs may be any that keep to these rules, and one draw needn't show every extreme that they name: `send_counts`: zero toward the device's own sector, exactly 128 toward each of the two neighbouring sectors, 0 to 64 toward the others. `send_rows`: within one device's lists all rows are distinct; rows in slots at or beyond the count stay and are ignored for leaving. `particle_cell`: row 0 lies in 0 to 511, row 1 in 0 to 255, row 2 in 0 to 63. A leaving inclusion's cell lies in the target sector, every other in its own device's sector; the axial cell always lies in the device's own slab.
All inputs are finite; a program needn't handle non-finite values.
Results may differ from the reference program's by a relative error of at most 0.0003.
Values sent between devices are 32-bit elements; how exact they have to be, the bound alone decides.
No kernel may reach another device: no remote copies, remote signals or barrier semaphores. Data moves between devices by JAX's collectives and lax.ppermute only.
A program may use at most 128 MiB of HBM per device.

```python
import math
import jax
import jax.numpy as jnp

NA = 512
NR = 256
KR = 32
ZDEV = 2
P_DEV = 8192
CAP = 128
NZ = 64
PTOTAL = 2097152
N_AZ = 8
N_AX = 32


def shuffle_rows(order_key):
    return jax.random.permutation(order_key, P_DEV)


def place_device(sector, list_rows, chosen_sector, far_slot):
    owner_sector = jnp.full((P_DEV,), sector, jnp.int32).at[list_rows.reshape(-1)].set(chosen_sector.reshape(-1))
    far_flag = jnp.zeros((P_DEV,), jnp.int32).at[list_rows.reshape(-1)].set(far_slot.reshape(-1))
    return (owner_sector, far_flag)


def migration_plan(key):
    devices = N_AZ * N_AX
    key_count, key_order, key_theta, key_radial, key_near, key_axial = jax.random.split(key, 6)
    device_sector = jnp.arange(devices, dtype=jnp.int32) // N_AX
    device_slab = jnp.arange(devices, dtype=jnp.int32) % N_AX
    target_sector = jnp.arange(N_AZ, dtype=jnp.int32)
    offset = (target_sector[None, :] - device_sector[:, None]) % N_AZ
    partial_count = jax.random.randint(key_count, (devices, N_AZ), 0, CAP // 2 + 1)
    neighbour = (offset == 1) | (offset == N_AZ - 1)
    counts = jnp.where(offset == 0, 0, jnp.where(neighbour, CAP, partial_count)).astype(jnp.int32)
    orders = jax.vmap(shuffle_rows)(jax.random.split(key_order, devices))
    send_list = orders[:, :N_AZ * CAP].reshape(devices, N_AZ, CAP).astype(jnp.int32)
    slot_index = jnp.arange(CAP, dtype=jnp.int32)
    used_slot = slot_index[None, None, :] < counts[:, :, None]
    chosen_sector = jnp.where(used_slot, target_sector[None, :, None], device_sector[:, None, None]).astype(jnp.int32)
    far_slot = (used_slot & jnp.logical_not(neighbour)[:, :, None]).astype(jnp.int32)
    owner_sector, far_flag = jax.vmap(place_device)(device_sector, send_list, chosen_sector, far_slot)
    theta_cell = owner_sector * (NA // N_AZ) + jax.random.randint(key_theta, (devices, P_DEV), 0, NA // N_AZ)
    radial_cell = jnp.where(far_flag == 1, jax.random.randint(key_near, (devices, P_DEV), 0, 8), jax.random.randint(key_radial, (devices, P_DEV), 0, NR))
    axial_cell = device_slab[:, None] * ZDEV + jax.random.randint(key_axial, (devices, P_DEV), 0, ZDEV)
    every_cell = jnp.stack([theta_cell, radial_cell, axial_cell]).astype(jnp.int32).reshape(3, devices * P_DEV)
    return (counts, send_list, every_cell)


def draw_particle_cell(key, part):
    counts, send_list, every_cell = migration_plan(key)
    return every_cell


def draw_send_rows(key, part):
    counts, send_list, every_cell = migration_plan(key)
    return send_list


def draw_send_counts(key, part):
    counts, send_list, every_cell = migration_plan(key)
    return counts.reshape(N_AZ, N_AX, N_AZ)


def block_scale(stream_key, dims, pieces, smallest, high):
    gain = 1.0
    for dim, blocks in pieces:
        draws = jax.random.uniform(jax.random.fold_in(jax.random.fold_in(stream_key, 6), dim), (blocks,), jnp.float32, smallest / len(pieces), high / len(pieces))
        gain = gain * jnp.repeat(jnp.exp(draws), dims[dim] // blocks).reshape((-1,) + (1,) * (len(dims) - 1 - dim))
    return gain


def scatter_about(stream_key, dims, deviation, bound, cuts=(), held_as=jnp.bfloat16):
    entries = deviation * jax.random.normal(stream_key, dims, jnp.float32)
    if cuts:
        entries = entries * block_scale(stream_key, dims, cuts, -0.22, 0.18)
    return jnp.clip(entries, -bound, bound).astype(held_as)


def setup_inputs(seed: int = 0) -> dict:
    seeds = jax.random.split(jax.random.key(seed), 8)
    return {
        "velocity": scatter_about(seeds[0], (3, NA, NZ, NR), 1.0, 5.0, ((1, 8), (2, 32)), jnp.float32),
        "viscosity": jnp.clip(jnp.exp(math.log(2.0) - 1.3862944 * jax.random.uniform(seeds[1], (NA, NZ, NR), jnp.float32) ** block_scale(seeds[1], (NA, NZ, NR), ((0, 8), (1, 32)), -0.2, 0.2)), 0.5, 2.0).astype(jnp.bfloat16),
        "bfield": scatter_about(seeds[2], (3, NA, NZ, NR), 1.0, 4.0, ((1, 8), (2, 32))),
        "particle_velocity": scatter_about(seeds[3], (3, PTOTAL), 1.0, 5.0, ((1, 256),), jnp.float32),
        "particle_cell": draw_particle_cell(jax.random.fold_in(seeds[7], 71), 0),
        "send_rows": draw_send_rows(jax.random.fold_in(seeds[7], 71), 0),
        "send_counts": draw_send_counts(jax.random.fold_in(seeds[7], 71), 0),
    }


TIME_STEP = 0.02
RELAX_TIME = 0.1
COUPLING = 2.0
CONDUCTIVITY = 0.5
STIR_RATE = 2.0
POLE_SIGNS = (-1.0, -1.0, 1.0)


def cycle_radius(cycle_count):
    return jnp.arange(cycle_count).astype(jnp.float32) + 0.5


def damping(mode_count, cycle_count, total_az):
    mode_index = jnp.arange(mode_count).astype(jnp.float32)
    folded = jnp.minimum(mode_index, total_az - mode_index)
    cutoff = 4.0 * cycle_radius(cycle_count)
    mode_ratio = folded[:, None] / cutoff[None, :]
    return 1.0 / (1.0 + mode_ratio ** 4)


def cross_product(left_vector, right_vector):
    return jnp.stack([left_vector[1] * right_vector[2] - left_vector[2] * right_vector[1],
                      left_vector[2] * right_vector[0] - left_vector[0] * right_vector[2],
                      left_vector[0] * right_vector[1] - left_vector[1] * right_vector[0]])


def split_terms(flow_field, theta_prev, theta_next, axial_prev, axial_next, radial_prev, radial_next, viscosity, bfield, dtheta, outer_radius):
    radius = cycle_radius(flow_field.shape[3])
    outer_face = radius + 0.5
    inner_face = radius - 0.5
    eddy_nu = viscosity.astype(jnp.float32)
    lap_radial = (outer_face * (radial_next - flow_field) - inner_face * (flow_field - radial_prev)) / radius
    lap_axial = axial_next - 2.0 * flow_field + axial_prev
    lap_theta = (theta_next - 2.0 * flow_field + theta_prev) / (radius * radius * dtheta * dtheta)
    grad_radial = 0.5 * (radial_next - radial_prev)
    grad_axial = 0.5 * (axial_next - axial_prev)
    grad_theta = (theta_next - theta_prev) / (2.0 * dtheta * radius)
    radial_flow = flow_field[0]
    swirl_flow = flow_field[1]
    axial_flow = flow_field[2]
    no_flow = jnp.zeros_like(radial_flow)
    metric_terms = jnp.stack([-eddy_nu * radial_flow / (radius * radius) + swirl_flow * swirl_flow / radius,
                              -eddy_nu * swirl_flow / (radius * radius) - radial_flow * swirl_flow / radius,
                              no_flow])
    stirring = jnp.stack([no_flow, no_flow + STIR_RATE * radius / outer_radius, no_flow])
    magnetic = bfield.astype(jnp.float32)
    lorentz = CONDUCTIVITY * cross_product(cross_product(stirring - flow_field, magnetic), magnetic)
    radial_part = eddy_nu * (lap_radial + lap_axial) - (radial_flow * grad_radial + axial_flow * grad_axial) + metric_terms + lorentz
    coupling_terms = jnp.stack([-2.0 * eddy_nu * grad_theta[1] / radius, 2.0 * eddy_nu * grad_theta[0] / radius, no_flow])
    azimuth_part = eddy_nu * lap_theta - swirl_flow * grad_theta + coupling_terms
    return radial_part, azimuth_part


def polar_filter(inner_cycles):
    spectrum = jnp.fft.rfft(inner_cycles, axis=1)
    mode_weights = damping(NA // 2 + 1, KR, NA)
    spectrum = spectrum * mode_weights[None, :, None, :]
    return jnp.fft.irfft(spectrum, n=NA, axis=1)


def tendency(flow_field, particle_rates, flat_cell, viscosity, bfield):
    dtheta = 2.0 * math.pi / NA
    theta_prev = jnp.roll(flow_field, 1, axis=1)
    theta_next = jnp.roll(flow_field, -1, axis=1)
    no_slab = jnp.zeros_like(flow_field[:, :, :1])
    axial_prev = jnp.concatenate([no_slab, flow_field[:, :, :-1]], axis=2)
    axial_next = jnp.concatenate([flow_field[:, :, 1:], no_slab], axis=2)
    pole_signs = jnp.array(POLE_SIGNS, dtype=jnp.float32)
    pole_ghost = pole_signs[:, None, None] * jnp.roll(flow_field[:, :, :, 0], NA // 2, axis=1)
    no_cycle = jnp.zeros_like(flow_field[:, :, :, :1])
    radial_prev = jnp.concatenate([pole_ghost[..., None], flow_field[..., :-1]], axis=3)
    radial_next = jnp.concatenate([flow_field[..., 1:], no_cycle], axis=3)
    radial_part, azimuth_part = split_terms(flow_field, theta_prev, theta_next, axial_prev, axial_next,
                                            radial_prev, radial_next, viscosity, bfield, dtheta, float(NR))
    filtered = jnp.concatenate([polar_filter(azimuth_part[..., :KR]), azimuth_part[..., KR:]], axis=3)
    flat_flow = flow_field.reshape(3, -1)
    mismatch = particle_rates - flat_flow[:, flat_cell]
    drag_force = jnp.zeros_like(flat_flow).at[:, flat_cell].add(COUPLING * mismatch)
    return radial_part + filtered + drag_force.reshape(flow_field.shape), -mismatch / RELAX_TIME


def reference(velocity, viscosity, bfield, particle_velocity, particle_cell, send_rows, send_counts):
    flat_cell = (particle_cell[0] * NZ + particle_cell[2]) * NR + particle_cell[1]
    first_flow, first_parts = tendency(velocity, particle_velocity, flat_cell, viscosity, bfield)
    mid_flow = velocity + TIME_STEP * first_flow
    mid_parts = particle_velocity + TIME_STEP * first_parts
    second_flow, second_parts = tendency(mid_flow, mid_parts, flat_cell, viscosity, bfield)
    new_flow = 0.5 * (velocity + mid_flow + TIME_STEP * second_flow)
    new_parts = 0.5 * (particle_velocity + mid_parts + TIME_STEP * second_parts)
    device_rows = send_rows + (jnp.arange(N_AZ * N_AX, dtype=jnp.int32) * P_DEV)[:, None, None]
    slot_index = jnp.arange(CAP, dtype=jnp.int32)
    used_slot = (slot_index[None, None, :] < send_counts.reshape(N_AZ * N_AX, N_AZ)[:, :, None]).astype(jnp.float32)
    leaving = jnp.zeros((N_AZ * N_AX * P_DEV,), jnp.float32).at[device_rows.reshape(-1)].add(used_slot.reshape(-1))
    kept_parts = new_parts * (1.0 - leaving)
    moved_parts = new_parts[:, device_rows] * used_slot
    moved_parts = moved_parts.reshape(3, N_AZ, N_AX, N_AZ, CAP).transpose(3, 2, 0, 1, 4)
    moved_parts = moved_parts.reshape(N_AZ * N_AX, 3, N_AZ * CAP)
    return new_flow, kept_parts, moved_parts
```

```python
import math

import jax
import jax.numpy as jnp
import numpy as np
from jax import lax
from jax.experimental import pallas as pl
from jax.experimental.pallas import tpu as pltpu
from jax.sharding import PartitionSpec as P

NA = 512
NR = 256
KR = 32
SECT = 8
TH = NA // SECT
CAP = 128
NP = 8192
DTHETA = 2.0 * math.pi / NA
DT = 0.02
POLE_SIGNS = (-1.0, -1.0, 1.0)
HIGHEST = lax.Precision.HIGHEST
f32 = jnp.float32
bf16 = jnp.bfloat16
i32 = jnp.int32
VMEM_LIMIT = 32 * 1024 * 1024

ROW_B = 64
ROW_HALO = 128
ROW_PART = 144
MSG1 = 152
MSG2 = 144
CHUNK = 2048


def filter_tables():
    a = np.arange(NA // 2)
    even, odd, even_mode, odd_mode = [], [], [], []
    for m in range(NA // 2 + 1):
        scale = math.sqrt((1.0 if m in (0, NA // 2) else 2.0) / NA)
        phase = 2.0 * math.pi * (m * a % NA) / NA
        rows = [scale * np.cos(phase)]
        if m not in (0, NA // 2):
            rows.append(scale * np.sin(phase))
        for row in rows:
            (odd if m % 2 else even).append(row)
            (odd_mode if m % 2 else even_mode).append(m)
    basis = np.stack([np.stack(even), np.stack(odd)]).astype(np.float32)
    modes = np.stack([np.array(even_mode), np.array(odd_mode)]).astype(np.float64)
    cutoff = 4.0 * (np.arange(KR) + 0.5)
    weight = 1.0 / (1.0 + (modes[:, :, None] / cutoff) ** 4)
    weight = np.tile(weight, (1, 1, 256 // KR)).astype(np.float32)
    return basis, np.ascontiguousarray(basis.transpose(0, 2, 1)), weight


BASIS, BASIS_T, MODE_WEIGHT = filter_tables()


def lane_iota(shape):
    return lax.broadcasted_iota(i32, shape, len(shape) - 1)


def row_iota(shape):
    return lax.broadcasted_iota(i32, shape, len(shape) - 2)


def strided(c, z, h):
    return pl.ds(c * 256 + h * 2 + z, TH, stride=4)


def block(c, z, h):
    return pl.ds(((c * 2 + z) * 2 + h) * TH, TH)


def lanes(x, by):
    by %= 128
    return x if by == 0 else pltpu.roll(x, by, 1)


def split2(x):
    hi = x.astype(bf16)
    return hi, (x - hi.astype(f32)).astype(bf16)


def split3(x):
    hi = x.astype(bf16)
    rest = x - hi.astype(f32)
    mid = rest.astype(bf16)
    return hi, mid, (rest - mid.astype(f32)).astype(bf16)


def pack_inner(field, nu):
    lane = lane_iota((TH, 128))

    def four(p, q, r, s):
        low = jnp.where(lane < 32, p, lanes(q, 32))
        high = jnp.where(lane < 96, lanes(r, 64), lanes(s, 96))
        return jnp.where(lane < 64, low, high)

    first = four(field[0][0][0], field[0][1][0], field[1][0][0], field[1][1][0])
    second = four(field[2][0][0], field[2][1][0], nu[0], nu[1])
    return first, second


def write_message(msg_ref, field, nu, me):
    first, second = pack_inner(field, nu)
    up = (me + 1) % SECT
    for t in range(SECT):
        msg_ref[t, 0:TH, :] = first
        msg_ref[t, ROW_B : ROW_B + TH, :] = second
        for c in range(3):
            for z in range(2):
                for h in range(2):
                    x = field[c][z][h]
                    edge = jnp.where(t == up, x[TH - 1 : TH], x[0:1])
                    row = ROW_HALO + (c * 2 + z) * 2 + h
                    msg_ref[t, row : row + 1, :] = edge


def write_axial(up_ref, down_ref, field):
    for c in range(3):
        for h in range(2):
            rows = pl.ds((c * 2 + h) * TH, TH)
            up_ref[rows, :] = field[c][1][h]
            down_ref[rows, :] = field[c][0][h]


def pack_kernel(vel_ref, nu_ref, pv_ref, pc_ref, rows_ref, cnt_ref, msg_ref, up_ref, down_ref, stay_ref, tmp_ref, nu_s):
    me = lax.axis_index("az")
    field = [[[vel_ref[strided(c, z, h), :] for h in range(2)] for z in range(2)] for c in range(3)]
    nu_s[...] = nu_ref[...].astype(f32)
    nu = [nu_s[pl.ds(z, TH, stride=4), :] for z in range(2)]
    write_message(msg_ref, field, nu, me)
    write_axial(up_ref, down_ref, field)
    for i in range(64):
        tmp_ref[i * 8 : i * 8 + 3, :] = pv_ref[:, i * 128 : (i + 1) * 128]
        tmp_ref[512 + i * 8 : 512 + i * 8 + 3, :] = pc_ref[:, i * 128 : (i + 1) * 128].astype(f32)
    parts = []
    for k in range(2):
        for c in range(3):
            parts.append(split3(tmp_ref[pl.ds(k * 512 + c, 64, stride=8), :]))
    stack = jnp.concatenate([jnp.concatenate([p[s] for p in parts], axis=1) for s in range(3)], axis=0)
    high_iota = row_iota((64, 128))
    low_iota = row_iota((128, 128))
    highs, lows, used_lows = [], [], []
    lane = lane_iota((1, 128))
    for t in range(SECT):
        row = rows_ref[0, t : t + 1, :]
        used = (lane < cnt_ref[me, 0, t]).astype(f32)
        highs.append((high_iota == row // 128).astype(f32).astype(bf16))
        low = (low_iota == row % 128).astype(f32)
        lows.append(low)
        used_lows.append((low * used).astype(bf16))
    high = jnp.concatenate(highs, axis=1)
    leaving = lax.dot_general(
        high, jnp.concatenate(used_lows, axis=1), (((1,), (1,)), ((), ())), preferred_element_type=f32
    )
    stay = 1.0 - leaving
    for i in range(64):
        stay_ref[0:1, i * 128 : (i + 1) * 128] = stay[i : i + 1, :]
    picked = lax.dot_general(
        stack, jnp.concatenate([high, high, high], axis=0), (((0,), (0,)), ((), ())), preferred_element_type=f32
    )
    for t in range(SECT):
        for q in range(6):
            value = picked[q * 128 : (q + 1) * 128, t * 128 : (t + 1) * 128] * lows[t]
            msg_ref[t, ROW_PART + q : ROW_PART + q + 1, :] = jnp.sum(value, axis=0, keepdims=True)


def local_row(theta, r, z, me, slab):
    return ((z - 2 * slab) * 2 + r // 128) * TH + theta - me * TH


def one_hot_pair(row, col, n):
    rows = (row_iota((256, n)) == row).astype(f32).astype(bf16)
    cols = row_iota((128, n)) == col
    return rows, cols


def deposit(row, col, velocity, n):
    rows, cols = one_hot_pair(row, col, n)
    pieces = []
    for c in range(3):
        for part in split2(velocity[c]):
            pieces.append(jnp.where(cols, part.astype(f32), 0.0).astype(bf16))
    pieces.append(cols.astype(f32).astype(bf16))
    return lax.dot_general(
        rows, jnp.concatenate(pieces, axis=0), (((1,), (1,)), ((), ())), preferred_element_type=f32
    )


def add_deposit(acc):
    out = [acc[:, c * 256 : c * 256 + 128] + acc[:, c * 256 + 128 : c * 256 + 256] for c in range(3)]
    out.append(acc[:, 768:896])
    return out


def scatter_kernel(pv_ref, pc_ref, stay_ref, sum_ref, acc_ref):
    me = lax.axis_index("az")
    slab = lax.axis_index("ax")
    for k in range(NP // CHUNK):
        part = pl.ds(k * CHUNK, CHUNK)
        row = local_row(pc_ref[0:1, part], pc_ref[1:2, part], pc_ref[2:3, part], me, slab)
        row = jnp.where(stay_ref[0:1, part] > 0.5, row, -1)
        col = pc_ref[1:2, part] % 128
        more = deposit(row, col, [pv_ref[c : c + 1, part] for c in range(3)], CHUNK)
        if k == 0:
            acc_ref[...] = more
        else:
            acc_ref[...] += more
    for c, x in enumerate(add_deposit(acc_ref[...])):
        sum_ref[c * 256 : (c + 1) * 256, :] = x


def arrivals(recv_ref, cnt_ref, me, slab):
    lane = lane_iota((1, CAP))
    live = jnp.concatenate([(lane < cnt_ref[s, 0, me]).astype(i32) for s in range(SECT)], axis=1)

    def channel(q):
        return jnp.concatenate([recv_ref[s, ROW_PART + q : ROW_PART + q + 1, :] for s in range(SECT)], axis=1)

    velocity = [channel(c) for c in range(3)]
    theta, r, z = [channel(3 + c).astype(i32) for c in range(3)]
    row = jnp.where(live > 0, local_row(theta, r, z, me, slab), -1)
    return live, row, r % 128, velocity


def filtered_inner(recv_ref, basis_ref, basis_t_ref, weight_ref, me):
    first = recv_ref[:, 0:TH, :].reshape(NA, 128)
    second = recv_ref[:, ROW_B : ROW_B + TH, :].reshape(NA, 128)
    lane = lane_iota((1, 128))
    radius = (lane % KR).astype(f32) + 0.5
    left = lane < 64
    first_swap = pltpu.roll(first, 64, 1)
    second_swap = pltpu.roll(second, 64, 1)
    nu = jnp.where(left, second_swap, second)
    swirl = jnp.where(left, first_swap, first)

    def differences(x):
        after = pltpu.roll(x, NA - 1, 0)
        before = pltpu.roll(x, 1, 0)
        lap = (after - 2.0 * x + before) * (1.0 / (radius * radius * (DTHETA * DTHETA)))
        return lap, (after - before) * (1.0 / (2.0 * DTHETA * radius))

    lap, grad = differences(first)
    cross = jnp.where(left, -2.0, 2.0) / radius
    part_first = nu * lap - swirl * grad + cross * nu * pltpu.roll(grad, 64, 1)
    lap, grad = differences(second)
    part_second = jnp.where(left, nu * lap - swirl * grad, 0.0)
    part = jnp.concatenate([part_first, part_second], axis=1)
    low, high = part[: NA // 2], part[NA // 2 :]
    own = pl.ds(pl.multiple_of((me % 4) * TH, TH), TH)
    out = 0.0
    for parity, x in enumerate((low + high, low - high)):
        spectrum = jnp.dot(basis_ref[parity], x, precision=HIGHEST, preferred_element_type=f32)
        spectrum = spectrum * weight_ref[parity]
        back = jnp.dot(basis_t_ref[parity, own, :], spectrum, precision=HIGHEST, preferred_element_type=f32)
        if parity:
            back = jnp.where(me < 4, back, -back)
        out = out + back
    return out[:, :128], out[:, 128:]


def fluid_rate(field, nu, magnetic, recv_ref, above_ref, below_ref, tables, me):
    filtered = filtered_inner(recv_ref, *tables, me)
    before_sector = (me + SECT - 1) % SECT
    after_sector = (me + 1) % SECT
    opposite = (me + SECT // 2) % SECT
    lane = lane_iota((TH, 128))
    row = row_iota((TH, 128))
    poles = [recv_ref[opposite, 0:TH, :], recv_ref[opposite, ROW_B : ROW_B + TH, :]]
    rates = [[[None, None], [None, None]] for _ in range(3)]
    for z in range(2):
        ghosts = []
        for c in range(3):
            ghosts.append(POLE_SIGNS[c] * lanes(poles[c // 2], -((c % 2) * 64 + z * 32)))
        rolled = [[(pltpu.roll(field[c][z][h], 1, 1), pltpu.roll(field[c][z][h], 127, 1)) for h in range(2)] for c in range(3)]
        for h in range(2):
            radius = lane_iota((1, 128)).astype(f32) + (h * 128 + 0.5)
            inverse = 1.0 / radius
            eddy = nu[z][h]
            u = [field[c][z][h] for c in range(3)]
            lap_ax, lap_rad, grad_rad, grad_ax, lap_th, grad_th = [], [], [], [], [], []
            for c in range(3):
                x = u[c]
                if h == 0:
                    prev_r = jnp.where(lane == 0, ghosts[c], rolled[c][0][0])
                    next_r = jnp.where(lane == 127, rolled[c][1][1], rolled[c][0][1])
                else:
                    prev_r = jnp.where(lane == 0, rolled[c][0][0], rolled[c][1][0])
                    next_r = jnp.where(lane == 127, 0.0, rolled[c][1][1])
                face = pl.ds((c * 2 + h) * TH, TH)
                prev_z = below_ref[face, :] if z == 0 else field[c][0][h]
                next_z = field[c][1][h] if z == 0 else above_ref[face, :]
                halo = ROW_HALO + (c * 2 + z) * 2 + h
                prev_t = jnp.where(row == 0, recv_ref[before_sector, halo : halo + 1, :], pltpu.roll(x, 1, 0))
                next_t = jnp.where(row == TH - 1, recv_ref[after_sector, halo : halo + 1, :], pltpu.roll(x, TH - 1, 0))
                lap_rad.append(((radius + 0.5) * (next_r - x) - (radius - 0.5) * (x - prev_r)) * inverse)
                lap_ax.append(next_z - 2.0 * x + prev_z)
                grad_rad.append(0.5 * (next_r - prev_r))
                grad_ax.append(0.5 * (next_z - prev_z))
                lap_th.append((next_t - 2.0 * x + prev_t) * (1.0 / (radius * radius * (DTHETA * DTHETA))))
                grad_th.append((next_t - prev_t) * (1.0 / (2.0 * DTHETA * radius)))
            b = [magnetic[c][z][h] for c in range(3)]
            slip = [-u[0], radius * (2.0 / NR) - u[1], -u[2]]
            current = [slip[1] * b[2] - slip[2] * b[1], slip[2] * b[0] - slip[0] * b[2], slip[0] * b[1] - slip[1] * b[0]]
            force = [
                current[1] * b[2] - current[2] * b[1],
                current[2] * b[0] - current[0] * b[2],
                current[0] * b[1] - current[1] * b[0],
            ]
            inverse2 = inverse * inverse
            metric = [
                u[1] * u[1] * inverse - eddy * u[0] * inverse2,
                -eddy * u[1] * inverse2 - u[0] * u[1] * inverse,
                0.0,
            ]
            coupling = [-2.0 * eddy * grad_th[1] * inverse, 2.0 * eddy * grad_th[0] * inverse, 0.0]
            for c in range(3):
                azimuth = eddy * lap_th[c] - u[1] * grad_th[c] + coupling[c]
                if h == 0:
                    inner = lanes(filtered[c // 2], -((c % 2) * 64 + z * 32))
                    azimuth = jnp.where(lane < KR, inner, azimuth)
                rates[c][z][h] = (
                    eddy * (lap_rad[c] + lap_ax[c])
                    - (u[0] * grad_rad[c] + u[2] * grad_ax[c])
                    + metric[c]
                    + 0.5 * force[c]
                    + azimuth
                )
    return rates


def materials(nu_ref, mag_ref, nu_s, mag_s):
    nu_s[...] = nu_ref[...].astype(f32)
    mag_s[...] = mag_ref[...].astype(f32)
    nu = [[nu_s[strided(0, z, h), :] for h in range(2)] for z in range(2)]
    magnetic = [[[mag_s[strided(c, z, h), :] for h in range(2)] for z in range(2)] for c in range(3)]
    return nu, magnetic


def first_kernel(
    recv_ref, above_ref, below_ref, vel_ref, nu_ref, mag_ref, sum_ref, cnt_ref, basis_ref, basis_t_ref, weight_ref,
    msg_ref, up_ref, down_ref, mid_ref, rest_ref, pick_ref, nu_s, mag_s,
):
    me = lax.axis_index("az")
    slab = lax.axis_index("ax")
    live, row, col, velocity = arrivals(recv_ref, cnt_ref, me, slab)
    arrived = add_deposit(deposit(row, col, velocity, SECT * CAP))
    total = [sum_ref[c * 256 : (c + 1) * 256, :] + arrived[c] for c in range(4)]
    nu, magnetic = materials(nu_ref, mag_ref, nu_s, mag_s)
    field = [[[vel_ref[strided(c, z, h), :] for h in range(2)] for z in range(2)] for c in range(3)]
    tables = (basis_ref, basis_t_ref, weight_ref)
    rates = fluid_rate(field, nu, magnetic, recv_ref, above_ref, below_ref, tables, me)
    mid = [[[None, None], [None, None]] for _ in range(3)]
    for c in range(3):
        halves = []
        for z in range(2):
            for h in range(2):
                at = slice((z * 2 + h) * TH, (z * 2 + h + 1) * TH)
                x, s, n = field[c][z][h], total[c][at], total[3][at]
                u1 = x + DT * (rates[c][z][h] + 2.0 * (s - n * x))
                mid[c][z][h] = u1
                mid_ref[block(c, z, h), :] = u1
                rest_ref[block(c, z, h), :] = 0.5 * (x + u1) + DT * (0.8 * s + 0.2 * n * x - n * u1)
                halves.append(0.08 * x + 0.1 * u1)
        pick = jnp.concatenate(halves, axis=0).T
        hi, lo = split2(pick)
        pick_ref[c * 128 : (c + 1) * 128, 0:256] = hi
        pick_ref[c * 128 : (c + 1) * 128, 256:512] = lo
    write_message(msg_ref, mid, [nu[z][0] for z in range(2)], me)
    write_axial(up_ref, down_ref, mid)


def take(pick, row, col, n):
    rows, cols = one_hot_pair(row, col, n)
    got = jnp.dot(pick, jnp.concatenate([rows, rows], axis=0), preferred_element_type=f32)
    return [jnp.sum(jnp.where(cols, got[c * 128 : (c + 1) * 128], 0.0), axis=0, keepdims=True) for c in range(3)]


def gather_kernel(pv_ref, pc_ref, stay_ref, recv_ref, cnt_ref, pick_ref, kept_ref, arr_ref):
    me = lax.axis_index("az")
    slab = lax.axis_index("ax")
    pick = pick_ref[...]
    for k in range(NP // CHUNK):
        part = pl.ds(k * CHUNK, CHUNK)
        row = local_row(pc_ref[0:1, part], pc_ref[1:2, part], pc_ref[2:3, part], me, slab)
        stay = stay_ref[0:1, part] > 0.5
        row = jnp.where(stay, row, -1)
        got = take(pick, row, pc_ref[1:2, part] % 128, CHUNK)
        for c in range(3):
            kept_ref[c : c + 1, part] = jnp.where(stay, 0.82 * pv_ref[c : c + 1, part] + got[c], 0.0)
    live, row, col, velocity = arrivals(recv_ref, cnt_ref, me, slab)
    got = take(pick, row, col, SECT * CAP)
    for c in range(3):
        arr_ref[0, c : c + 1, :] = jnp.where(live > 0, 0.82 * velocity[c] + got[c], 0.0)


def last_kernel(
    recv_ref, above_ref, below_ref, mid_ref, rest_ref, nu_ref, mag_ref, basis_ref, basis_t_ref, weight_ref,
    out_ref, nu_s, mag_s,
):
    me = lax.axis_index("az")
    nu, magnetic = materials(nu_ref, mag_ref, nu_s, mag_s)
    field = [[[mid_ref[block(c, z, h), :] for h in range(2)] for z in range(2)] for c in range(3)]
    tables = (basis_ref, basis_t_ref, weight_ref)
    rates = fluid_rate(field, nu, magnetic, recv_ref, above_ref, below_ref, tables, me)
    for c in range(3):
        for z in range(2):
            for h in range(2):
                out_ref[strided(c, z, h), :] = rest_ref[block(c, z, h), :] + (0.5 * DT) * rates[c][z][h]


def call(kernel, outs, ins, scratch, name, flops=0, smem=()):
    vmem = pl.BlockSpec(memory_space=pltpu.VMEM)
    return pl.pallas_call(
        kernel,
        out_shape=[jax.ShapeDtypeStruct(s, t) for s, t in outs],
        in_specs=[pl.BlockSpec(memory_space=pltpu.SMEM) if i in smem else vmem for i in range(len(ins))],
        out_specs=[vmem] * len(outs),
        scratch_shapes=[pltpu.VMEM(s, t) for s, t in scratch],
        compiler_params=pltpu.CompilerParams(vmem_limit_bytes=VMEM_LIMIT),
        cost_estimate=pl.CostEstimate(flops=flops, bytes_accessed=2 * 1024 * 1024, transcendentals=0),
        name=name,
    )(*ins)


def rows_of(x):
    lead = x.shape[:-2]
    x = x.reshape(*lead, 2, 2, 128)
    return jnp.swapaxes(x, -3, -2).reshape(-1, 128)


def per_device(velocity, viscosity, bfield, particle_velocity, particle_cell, send_rows, send_counts):
    ax = lax.axis_size("ax")
    vel, nu, mag = rows_of(velocity), rows_of(viscosity), rows_of(bfield)
    pv, pc = particle_velocity, particle_cell
    tables = (jnp.asarray(BASIS), jnp.asarray(BASIS_T), jnp.asarray(MODE_WEIGHT))
    scratch = [((256, 128), f32), ((768, 128), f32)]

    def exchange(msg, up, down):
        below = lax.ppermute(up, "ax", [(i, i + 1) for i in range(ax - 1)])
        above = lax.ppermute(down, "ax", [(i + 1, i) for i in range(ax - 1)])
        recv = lax.all_to_all(msg, "az", split_axis=0, concat_axis=0, tiled=True)
        return recv, above, below

    face = ((384, 128), f32)
    msg, up, down, stay = call(
        pack_kernel,
        [((SECT, MSG1, 128), f32), face, face, ((1, NP), f32)],
        [vel, nu, pv, pc, send_rows, send_counts],
        [((1024, 128), f32), ((256, 128), f32)],
        "pack",
        smem=(5,),
    )
    recv, above, below = exchange(msg, up, down)
    (sums,) = call(
        scatter_kernel, [((1024, 128), f32)], [pv, pc, stay], [((256, 896), f32)], "deposit", flops=2 * NP * 256 * 896
    )
    msg2, up, down, mid, rest, pick = call(
        first_kernel,
        [((SECT, MSG2, 128), f32), face, face, ((768, 128), f32), ((768, 128), f32), ((384, 512), bf16)],
        [recv, above, below, vel, nu, mag, sums, send_counts, *tables],
        scratch,
        "first_section",
        smem=(7,),
    )
    recv2, above2, below2 = exchange(msg2, up, down)
    kept, arrived = call(
        gather_kernel,
        [((3, NP), f32), ((1, 3, SECT * CAP), f32)],
        [pv, pc, stay, recv, send_counts, pick],
        [],
        "take",
        flops=2 * NP * 512 * 384,
        smem=(4,),
    )
    (new,) = call(
        last_kernel,
        [((768, 128), f32)],
        [recv2, above2, below2, mid, rest, nu, mag, *tables],
        scratch,
        "second_section",
    )
    new = jnp.swapaxes(new.reshape(3, TH, 2, 2, 128), 2, 3).reshape(3, TH, 2, NR)
    return new, kept, arrived


def solution(mesh):
    return jax.shard_map(
        per_device,
        mesh=mesh,
        in_specs=(
            P(None, "az", "ax", None),
            P("az", "ax", None),
            P(None, "az", "ax", None),
            P(None, ("az", "ax")),
            P(None, ("az", "ax")),
            P(("az", "ax"), None, None),
            P(None, "ax", None),
        ),
        out_specs=(P(None, "az", "ax", None), P(None, ("az", "ax")), P(("az", "ax"), None, None)),
        check_vma=False,
    )
```

```python
import math

import jax
import jax.numpy as jnp
import numpy as np
from jax import lax
from jax.experimental import pallas as pl
from jax.experimental.pallas import tpu as pltpu
from jax.sharding import PartitionSpec as P

NA = 512
NR = 256
KR = 32
SECT = 8
TH = NA // SECT
CAP = 128
NP = 8192
DTHETA = 2.0 * math.pi / NA
DT = 0.02
POLE_SIGNS = (-1.0, -1.0, 1.0)
HIGHEST = lax.Precision.HIGHEST
f32 = jnp.float32
bf16 = jnp.bfloat16
i32 = jnp.int32
VMEM_LIMIT = 32 * 1024 * 1024

ROW_B = 64
ROW_EDGE = 128
EDGE_PART = 16
EDGE1 = 24
EDGE2 = 16
CHUNK = 2048


def filter_tables():
    a = np.arange(NA // 2)
    even, odd, even_mode, odd_mode = [], [], [], []
    for m in range(NA // 2 + 1):
        scale = math.sqrt((1.0 if m in (0, NA // 2) else 2.0) / NA)
        phase = 2.0 * math.pi * (m * a % NA) / NA
        rows = [scale * np.cos(phase)]
        if m not in (0, NA // 2):
            rows.append(scale * np.sin(phase))
        for row in rows:
            (odd if m % 2 else even).append(row)
            (odd_mode if m % 2 else even_mode).append(m)
    basis = np.stack([np.stack(even), np.stack(odd)]).astype(np.float32)
    modes = np.stack([np.array(even_mode), np.array(odd_mode)]).astype(np.float64)
    cutoff = 4.0 * (np.arange(KR) + 0.5)
    weight = 1.0 / (1.0 + (modes[:, :, None] / cutoff) ** 4)
    weight = np.tile(weight, (1, 1, 256 // KR)).astype(np.float32)
    return basis, np.ascontiguousarray(basis.transpose(0, 2, 1)), weight


BASIS, BASIS_T, MODE_WEIGHT = filter_tables()


def lane_iota(shape):
    return lax.broadcasted_iota(i32, shape, len(shape) - 1)


def row_iota(shape):
    return lax.broadcasted_iota(i32, shape, len(shape) - 2)


def strided(c, z, h):
    return pl.ds(c * 256 + h * 2 + z, TH, stride=4)


def block(c, z, h):
    return pl.ds(((c * 2 + z) * 2 + h) * TH, TH)


def lanes(x, by):
    by %= 128
    return x if by == 0 else pltpu.roll(x, by, 1)


def split2(x):
    hi = x.astype(bf16)
    return hi, (x - hi.astype(f32)).astype(bf16)


def split3(x):
    hi = x.astype(bf16)
    rest = x - hi.astype(f32)
    mid = rest.astype(bf16)
    return hi, mid, (rest - mid.astype(f32)).astype(bf16)


def pack_inner(field, nu):
    lane = lane_iota((TH, 128))

    def four(p, q, r, s):
        low = jnp.where(lane < 32, p, lanes(q, 32))
        high = jnp.where(lane < 96, lanes(r, 64), lanes(s, 96))
        return jnp.where(lane < 64, low, high)

    first = four(field[0][0][0], field[0][1][0], field[1][0][0], field[1][1][0])
    second = four(field[2][0][0], field[2][1][0], nu[0], nu[1])
    return first, second


def write_message(inner_ref, edge_ref, field, nu, me):
    first, second = pack_inner(field, nu)
    inner_ref[0:TH, :] = first
    inner_ref[TH : 2 * TH, :] = second
    up = (me + 1) % SECT
    for c in range(3):
        for z in range(2):
            for h in range(2):
                x = field[c][z][h]
                row = (c * 2 + z) * 2 + h
                for t in range(SECT):
                    edge_ref[t, row : row + 1, :] = jnp.where(t == up, x[TH - 1 : TH], x[0:1])


def send_message(out, edges):
    inner = out.vmem("inner")
    for t in range(SECT):
        out.copy(inner, out.hbm("msg").at[t, 0:ROW_EDGE, :])
    out.copy(edges, out.hbm("msg").at[:, ROW_EDGE:, :])


def write_axial(one_ref, two_ref, field, slab):
    odd = slab % 2 == 1
    for c in range(3):
        for h in range(2):
            rows = pl.ds((c * 2 + h) * TH, TH)
            low, high = field[c][0][h], field[c][1][h]
            one_ref[rows, :] = jnp.where(odd, low, high)
            two_ref[rows, :] = jnp.where(odd, high, low)


class Inputs:
    def __init__(self, names, refs, bufs, sems):
        self.refs = dict(zip(names, bufs))
        self.copies = {}
        for i, (name, ref, buf) in enumerate(zip(names, refs, bufs)):
            if name == "inner":
                ref = ref.at[:, 0:ROW_EDGE, :]
            if name == "edge":
                ref = ref.at[:, ROW_EDGE:, :]
            self.copies[name] = [pltpu.make_async_copy(ref, buf, sems.at[i])]
            self.copies[name][0].start()

    def __call__(self, name):
        for copy in self.copies.pop(name, ()):
            copy.wait()
        return self.refs[name]


class Outputs:
    def __init__(self, names, refs, bufs, sems):
        self.refs, self.bufs, self.sems, self.started = dict(zip(names, refs)), bufs, sems, []

    def hbm(self, name):
        return self.refs[name]

    def vmem(self, name):
        return self.bufs[name]

    def copy(self, src, dst):
        copy = pltpu.make_async_copy(src, dst, self.sems.at[len(self.started)])
        copy.start()
        self.started.append(copy)

    def send(self, name):
        self.copy(self.bufs[name], self.refs[name])

    def finish(self):
        for copy in self.started:
            copy.wait()


def pack_kernel(inp, out):
    me = lax.axis_index("az")
    slab = lax.axis_index("ax")
    pv_ref, pc_ref = inp("pv"), inp("pc")
    tmp_ref, nu_s, edge_ref, stay_ref = out.vmem("tmp"), out.vmem("nu"), out.vmem("edge"), out.vmem("stay")
    for i in range(64):
        tmp_ref[i * 8 : i * 8 + 3, :] = pv_ref[:, i * 128 : (i + 1) * 128]
        tmp_ref[512 + i * 8 : 512 + i * 8 + 3, :] = pc_ref[:, i * 128 : (i + 1) * 128].astype(f32)
    parts = []
    for k in range(2):
        for c in range(3):
            parts.append(split3(tmp_ref[pl.ds(k * 512 + c, 64, stride=8), :]))
    stack = jnp.concatenate([jnp.concatenate([p[s] for p in parts], axis=1) for s in range(3)], axis=0)
    rows_ref, cnt_ref = inp("rows"), inp("cnt")
    high_iota = row_iota((64, 128))
    low_iota = row_iota((128, 128))
    highs, lows, used_lows = [], [], []
    lane = lane_iota((1, 128))
    for t in range(SECT):
        row = rows_ref[0, t : t + 1, :]
        used = (lane < cnt_ref[me, 0, t]).astype(f32)
        highs.append((high_iota == row // 128).astype(f32).astype(bf16))
        low = (low_iota == row % 128).astype(f32)
        lows.append(low)
        used_lows.append((low * used).astype(bf16))
    high = jnp.concatenate(highs, axis=1)
    leaving = lax.dot_general(
        high, jnp.concatenate(used_lows, axis=1), (((1,), (1,)), ((), ())), preferred_element_type=f32
    )
    stay = 1.0 - leaving
    for i in range(64):
        stay_ref[0:1, i * 128 : (i + 1) * 128] = stay[i : i + 1, :]
    out.send("stay")
    picked = lax.dot_general(
        stack, jnp.concatenate([high, high, high], axis=0), (((0,), (0,)), ((), ())), preferred_element_type=f32
    )
    for t in range(SECT):
        for q in range(6):
            value = picked[q * 128 : (q + 1) * 128, t * 128 : (t + 1) * 128] * lows[t]
            edge_ref[t, EDGE_PART + q : EDGE_PART + q + 1, :] = jnp.sum(value, axis=0, keepdims=True)
    vel_ref, nu_ref = inp("vel"), inp("nu")
    field = [[[vel_ref[strided(c, z, h), :] for h in range(2)] for z in range(2)] for c in range(3)]
    nu_s[...] = nu_ref[...].astype(f32)
    nu = [nu_s[pl.ds(z, TH, stride=4), :] for z in range(2)]
    write_message(out.vmem("inner"), edge_ref, field, nu, me)
    send_message(out, edge_ref)
    write_axial(out.vmem("one"), out.vmem("two"), field, slab)
    out.send("one")
    out.send("two")


def local_row(theta, r, z, me, slab):
    return ((z - 2 * slab) * 2 + r // 128) * TH + theta - me * TH


def one_hot_pair(row, col, n):
    rows = (row_iota((256, n)) == row).astype(f32).astype(bf16)
    cols = row_iota((128, n)) == col
    return rows, cols


def deposit(row, col, velocity, n):
    rows, cols = one_hot_pair(row, col, n)
    pieces = []
    for c in range(3):
        for part in split2(velocity[c]):
            pieces.append(jnp.where(cols, part.astype(f32), 0.0).astype(bf16))
    pieces.append(cols.astype(f32).astype(bf16))
    return lax.dot_general(
        rows, jnp.concatenate(pieces, axis=0), (((1,), (1,)), ((), ())), preferred_element_type=f32
    )


def add_deposit(acc):
    out = [acc[:, c * 256 : c * 256 + 128] + acc[:, c * 256 + 128 : c * 256 + 256] for c in range(3)]
    out.append(acc[:, 768:896])
    return out


def scatter_kernel(inp, out):
    me = lax.axis_index("az")
    slab = lax.axis_index("ax")
    pc_ref, stay_ref, pv_ref = inp("pc"), inp("stay"), inp("pv")
    sum_ref, acc_ref = out.vmem("sums"), out.vmem("acc")
    for k in range(NP // CHUNK):
        part = pl.ds(k * CHUNK, CHUNK)
        row = local_row(pc_ref[0:1, part], pc_ref[1:2, part], pc_ref[2:3, part], me, slab)
        row = jnp.where(stay_ref[0:1, part] > 0.5, row, -1)
        col = pc_ref[1:2, part] % 128
        more = deposit(row, col, [pv_ref[c : c + 1, part] for c in range(3)], CHUNK)
        if k == 0:
            acc_ref[...] = more
        else:
            acc_ref[...] += more
    for c, x in enumerate(add_deposit(acc_ref[...])):
        sum_ref[c * 256 : (c + 1) * 256, :] = x
    out.send("sums")


def arrivals(edge_ref, cnt_ref, me, slab):
    lane = lane_iota((1, CAP))
    live = jnp.concatenate([(lane < cnt_ref[s, 0, me]).astype(i32) for s in range(SECT)], axis=1)

    def channel(q):
        return jnp.concatenate([edge_ref[s, EDGE_PART + q : EDGE_PART + q + 1, :] for s in range(SECT)], axis=1)

    velocity = [channel(c) for c in range(3)]
    theta, r, z = [channel(3 + c).astype(i32) for c in range(3)]
    row = jnp.where(live > 0, local_row(theta, r, z, me, slab), -1)
    return live, row, r % 128, velocity


def filtered_inner(inp, me):
    recv_ref = inp("inner")
    first = recv_ref[:, 0:TH, :].reshape(NA, 128)
    second = recv_ref[:, ROW_B : ROW_B + TH, :].reshape(NA, 128)
    lane = lane_iota((1, 128))
    radius = (lane % KR).astype(f32) + 0.5
    left = lane < 64
    first_swap = pltpu.roll(first, 64, 1)
    second_swap = pltpu.roll(second, 64, 1)
    nu = jnp.where(left, second_swap, second)
    swirl = jnp.where(left, first_swap, first)

    def differences(x):
        after = pltpu.roll(x, NA - 1, 0)
        before = pltpu.roll(x, 1, 0)
        lap = (after - 2.0 * x + before) * (1.0 / (radius * radius * (DTHETA * DTHETA)))
        return lap, (after - before) * (1.0 / (2.0 * DTHETA * radius))

    lap, grad = differences(first)
    cross = jnp.where(left, -2.0, 2.0) / radius
    part_first = nu * lap - swirl * grad + cross * nu * pltpu.roll(grad, 64, 1)
    lap, grad = differences(second)
    part_second = jnp.where(left, nu * lap - swirl * grad, 0.0)
    part = jnp.concatenate([part_first, part_second], axis=1)
    low, high = part[: NA // 2], part[NA // 2 :]
    basis_ref, weight_ref, basis_t_ref = inp("basis"), inp("weight"), inp("basis_t")
    own = pl.ds(pl.multiple_of((me % 4) * TH, TH), TH)
    out = 0.0
    for parity, x in enumerate((low + high, low - high)):
        spectrum = jnp.dot(basis_ref[parity], x, precision=HIGHEST, preferred_element_type=f32)
        spectrum = spectrum * weight_ref[parity]
        back = jnp.dot(basis_t_ref[parity, own, :], spectrum, precision=HIGHEST, preferred_element_type=f32)
        if parity:
            back = jnp.where(me < 4, back, -back)
        out = out + back
    return out[:, :128], out[:, 128:]


def fluid_rate(field, nu, magnetic, inp, me, slab):
    filtered = filtered_inner(inp, me)
    recv_ref, edge_ref, one_ref, two_ref = inp("inner"), inp("edge"), inp("one"), inp("two")
    odd = slab % 2 == 1
    before_sector = (me + SECT - 1) % SECT
    after_sector = (me + 1) % SECT
    opposite = (me + SECT // 2) % SECT
    lane = lane_iota((TH, 128))
    row = row_iota((TH, 128))
    poles = [recv_ref[opposite, 0:TH, :], recv_ref[opposite, ROW_B : ROW_B + TH, :]]
    rates = [[[None, None], [None, None]] for _ in range(3)]
    for z in range(2):
        ghosts = []
        for c in range(3):
            ghosts.append(POLE_SIGNS[c] * lanes(poles[c // 2], -((c % 2) * 64 + z * 32)))
        rolled = [[(pltpu.roll(field[c][z][h], 1, 1), pltpu.roll(field[c][z][h], 127, 1)) for h in range(2)] for c in range(3)]
        for h in range(2):
            radius = lane_iota((1, 128)).astype(f32) + (h * 128 + 0.5)
            inverse = 1.0 / radius
            eddy = nu[z][h]
            u = [field[c][z][h] for c in range(3)]
            lap_ax, lap_rad, grad_rad, grad_ax, lap_th, grad_th = [], [], [], [], [], []
            for c in range(3):
                x = u[c]
                if h == 0:
                    prev_r = jnp.where(lane == 0, ghosts[c], rolled[c][0][0])
                    next_r = jnp.where(lane == 127, rolled[c][1][1], rolled[c][0][1])
                else:
                    prev_r = jnp.where(lane == 0, rolled[c][0][0], rolled[c][1][0])
                    next_r = jnp.where(lane == 127, 0.0, rolled[c][1][1])
                face = pl.ds((c * 2 + h) * TH, TH)
                if z == 0:
                    prev_z = jnp.where(odd, one_ref[face, :], two_ref[face, :])
                    next_z = field[c][1][h]
                else:
                    prev_z = field[c][0][h]
                    next_z = jnp.where(odd, two_ref[face, :], one_ref[face, :])
                halo = (c * 2 + z) * 2 + h
                prev_t = jnp.where(row == 0, edge_ref[before_sector, halo : halo + 1, :], pltpu.roll(x, 1, 0))
                next_t = jnp.where(row == TH - 1, edge_ref[after_sector, halo : halo + 1, :], pltpu.roll(x, TH - 1, 0))
                lap_rad.append(((radius + 0.5) * (next_r - x) - (radius - 0.5) * (x - prev_r)) * inverse)
                lap_ax.append(next_z - 2.0 * x + prev_z)
                grad_rad.append(0.5 * (next_r - prev_r))
                grad_ax.append(0.5 * (next_z - prev_z))
                lap_th.append((next_t - 2.0 * x + prev_t) * (1.0 / (radius * radius * (DTHETA * DTHETA))))
                grad_th.append((next_t - prev_t) * (1.0 / (2.0 * DTHETA * radius)))
            b = [magnetic[c][z][h] for c in range(3)]
            slip = [-u[0], radius * (2.0 / NR) - u[1], -u[2]]
            current = [slip[1] * b[2] - slip[2] * b[1], slip[2] * b[0] - slip[0] * b[2], slip[0] * b[1] - slip[1] * b[0]]
            force = [
                current[1] * b[2] - current[2] * b[1],
                current[2] * b[0] - current[0] * b[2],
                current[0] * b[1] - current[1] * b[0],
            ]
            inverse2 = inverse * inverse
            metric = [
                u[1] * u[1] * inverse - eddy * u[0] * inverse2,
                -eddy * u[1] * inverse2 - u[0] * u[1] * inverse,
                0.0,
            ]
            coupling = [-2.0 * eddy * grad_th[1] * inverse, 2.0 * eddy * grad_th[0] * inverse, 0.0]
            for c in range(3):
                azimuth = eddy * lap_th[c] - u[1] * grad_th[c] + coupling[c]
                if h == 0:
                    inner = lanes(filtered[c // 2], -((c % 2) * 64 + z * 32))
                    azimuth = jnp.where(lane < KR, inner, azimuth)
                rates[c][z][h] = (
                    eddy * (lap_rad[c] + lap_ax[c])
                    - (u[0] * grad_rad[c] + u[2] * grad_ax[c])
                    + metric[c]
                    + 0.5 * force[c]
                    + azimuth
                )
    return rates


def materials(inp, out):
    nu_s, mag_s = out.vmem("nu"), out.vmem("mag")
    nu_s[...] = inp("nu")[...].astype(f32)
    mag_s[...] = inp("mag")[...].astype(f32)
    nu = [[nu_s[strided(0, z, h), :] for h in range(2)] for z in range(2)]
    magnetic = [[[mag_s[strided(c, z, h), :] for h in range(2)] for z in range(2)] for c in range(3)]
    return nu, magnetic


def first_kernel(inp, out):
    me = lax.axis_index("az")
    slab = lax.axis_index("ax")
    live, row, col, velocity = arrivals(inp("edge"), inp("cnt"), me, slab)
    arrived = add_deposit(deposit(row, col, velocity, SECT * CAP))
    sum_ref = inp("sums")
    total = [sum_ref[c * 256 : (c + 1) * 256, :] + arrived[c] for c in range(4)]
    nu, magnetic = materials(inp, out)
    vel_ref = inp("vel")
    field = [[[vel_ref[strided(c, z, h), :] for h in range(2)] for z in range(2)] for c in range(3)]
    rates = fluid_rate(field, nu, magnetic, inp, me, slab)
    mid_ref, rest_ref, pick_ref = out.vmem("mid"), out.vmem("rest"), out.vmem("pick")
    mid = [[[None, None], [None, None]] for _ in range(3)]
    picks = []
    for c in range(3):
        halves = []
        for z in range(2):
            for h in range(2):
                at = slice((z * 2 + h) * TH, (z * 2 + h + 1) * TH)
                x, s, n = field[c][z][h], total[c][at], total[3][at]
                u1 = x + DT * (rates[c][z][h] + 2.0 * (s - n * x))
                mid[c][z][h] = u1
                mid_ref[block(c, z, h), :] = u1
                rest_ref[block(c, z, h), :] = 0.5 * (x + u1) + DT * (0.8 * s + 0.2 * n * x - n * u1)
                halves.append(0.08 * x + 0.1 * u1)
        picks.append(jnp.concatenate(halves, axis=0))
    write_message(out.vmem("inner"), out.vmem("edge"), mid, [nu[z][0] for z in range(2)], me)
    send_message(out, out.vmem("edge"))
    write_axial(out.vmem("one"), out.vmem("two"), mid, slab)
    out.send("one")
    out.send("two")
    out.send("mid")
    out.send("rest")
    for c in range(3):
        hi, lo = split2(picks[c].T)
        pick_ref[c * 128 : (c + 1) * 128, 0:256] = hi
        pick_ref[c * 128 : (c + 1) * 128, 256:512] = lo
    out.send("pick")


def take(pick, row, col, n):
    rows, cols = one_hot_pair(row, col, n)
    got = jnp.dot(pick, jnp.concatenate([rows, rows], axis=0), preferred_element_type=f32)
    return [jnp.sum(jnp.where(cols, got[c * 128 : (c + 1) * 128], 0.0), axis=0, keepdims=True) for c in range(3)]


def gather_kernel(inp, out):
    me = lax.axis_index("az")
    slab = lax.axis_index("ax")
    pc_ref, stay_ref, pv_ref = inp("pc"), inp("stay"), inp("pv")
    kept_ref, arr_ref = out.vmem("kept"), out.vmem("arrived")
    pick = inp("pick")[...]
    for k in range(NP // CHUNK):
        part = pl.ds(k * CHUNK, CHUNK)
        row = local_row(pc_ref[0:1, part], pc_ref[1:2, part], pc_ref[2:3, part], me, slab)
        stay = stay_ref[0:1, part] > 0.5
        row = jnp.where(stay, row, -1)
        got = take(pick, row, pc_ref[1:2, part] % 128, CHUNK)
        for c in range(3):
            kept_ref[c : c + 1, part] = jnp.where(stay, 0.82 * pv_ref[c : c + 1, part] + got[c], 0.0)
    out.send("kept")
    live, row, col, velocity = arrivals(inp("edge"), inp("cnt"), me, slab)
    got = take(pick, row, col, SECT * CAP)
    for c in range(3):
        arr_ref[c, 0:1, :] = jnp.where(live > 0, 0.82 * velocity[c] + got[c], 0.0)
    out.send("arrived")


def last_kernel(inp, out):
    me = lax.axis_index("az")
    slab = lax.axis_index("ax")
    mid_ref = inp("mid")
    field = [[[mid_ref[block(c, z, h), :] for h in range(2)] for z in range(2)] for c in range(3)]
    nu, magnetic = materials(inp, out)
    rates = fluid_rate(field, nu, magnetic, inp, me, slab)
    rest_ref, out_ref = inp("rest"), out.vmem("new")
    for c in range(3):
        for z in range(2):
            for h in range(2):
                out_ref[strided(c, z, h), :] = rest_ref[block(c, z, h), :] + (0.5 * DT) * rates[c][z][h]
    out.send("new")


def call(kernel, name, ins, outs, bufs, copies, flops=0, in_smem=()):
    in_names, out_names, buf_names = list(ins), list(outs), list(bufs)
    arrays = [ins[n] for n in in_names]
    n_in, n_out = len(in_names), len(out_names)

    def body(*refs):
        in_refs, refs = refs[:n_in], refs[n_in:]
        out_refs, refs = refs[:n_out], refs[n_out:]
        in_bufs, refs = refs[:n_in], refs[n_in:]
        buf_refs, (in_sems, out_sems) = refs[:-2], refs[-2:]
        out = Outputs(out_names, out_refs, dict(zip(buf_names, buf_refs)), out_sems)
        kernel(Inputs(in_names, in_refs, in_bufs, in_sems), out)
        out.finish()

    def in_shape(n):
        shape = ins[n].shape
        return {"inner": (SECT, ROW_EDGE, 128), "edge": (SECT, shape[1] - ROW_EDGE, 128)}.get(n, shape)

    hbm = pl.BlockSpec(memory_space=pltpu.HBM)
    return pl.pallas_call(
        body,
        out_shape=[jax.ShapeDtypeStruct(*outs[n]) for n in out_names],
        in_specs=[hbm] * n_in,
        out_specs=[hbm] * n_out,
        scratch_shapes=[(pltpu.SMEM if n in in_smem else pltpu.VMEM)(in_shape(n), ins[n].dtype) for n in in_names]
        + [pltpu.VMEM(*bufs[n]) for n in buf_names]
        + [pltpu.SemaphoreType.DMA((n_in,)), pltpu.SemaphoreType.DMA((copies,))],
        compiler_params=pltpu.CompilerParams(vmem_limit_bytes=VMEM_LIMIT),
        cost_estimate=pl.CostEstimate(flops=flops, bytes_accessed=2 * 1024 * 1024, transcendentals=0),
        name=name,
    )(*arrays)


def rows_of(x):
    lead = x.shape[:-2]
    x = x.reshape(*lead, 2, 2, 128)
    return jnp.swapaxes(x, -3, -2).reshape(-1, 128)


def per_device(velocity, viscosity, bfield, particle_velocity, particle_cell, send_rows, send_counts):
    ax = lax.axis_size("ax")
    vel, nu, mag = rows_of(velocity), rows_of(viscosity), rows_of(bfield)
    pv, pc = particle_velocity, particle_cell
    tables = {"basis": jnp.asarray(BASIS), "weight": jnp.asarray(MODE_WEIGHT), "basis_t": jnp.asarray(BASIS_T)}
    swap_one = [(i, i ^ 1) for i in range(ax)]
    swap_two = [(i, ((i + 1) ^ 1) - 1) for i in range(1, ax - 1)]

    def exchange(msg, one, two):
        one = lax.ppermute(one, "ax", swap_one)
        two = lax.ppermute(two, "ax", swap_two)
        return lax.all_to_all(msg, "az", split_axis=0, concat_axis=0, tiled=True), one, two

    face = ((384, 128), f32)
    field = ((768, 128), f32)
    materials_bufs = {"nu": ((256, 128), f32), "mag": field}
    message_bufs = {"inner": ((ROW_EDGE, 128), f32), "one": face, "two": face}
    msg, one, two, stay = call(
        pack_kernel,
        "pack",
        {"pc": pc, "pv": pv, "rows": send_rows, "cnt": send_counts, "vel": vel, "nu": nu},
        {"msg": ((SECT, ROW_EDGE + EDGE1, 128), f32), "one": face, "two": face, "stay": ((1, NP), f32)},
        message_bufs
        | {"edge": ((SECT, EDGE1, 128), f32), "stay": ((1, NP), f32), "tmp": ((1024, 128), f32), "nu": ((256, 128), f32)},
        12,
        in_smem=("cnt",),
    )
    recv, one, two = exchange(msg, one, two)
    (sums,) = call(
        scatter_kernel,
        "deposit",
        {"pc": pc, "stay": stay, "pv": pv},
        {"sums": ((1024, 128), f32)},
        {"sums": ((1024, 128), f32), "acc": ((256, 896), f32)},
        1,
        flops=2 * NP * 256 * 896,
    )
    msg2, one2, two2, mid, rest, pick = call(
        first_kernel,
        "first_section",
        {"edge": recv, "cnt": send_counts, "inner": recv, "sums": sums, "nu": nu, "mag": mag, "vel": vel}
        | tables
        | {"one": one, "two": two},
        {
            "msg": ((SECT, ROW_EDGE + EDGE2, 128), f32),
            "one": face,
            "two": face,
            "mid": field,
            "rest": field,
            "pick": ((384, 512), bf16),
        },
        message_bufs
        | materials_bufs
        | {"edge": ((SECT, EDGE2, 128), f32), "mid": field, "rest": field, "pick": ((384, 512), bf16)},
        14,
        in_smem=("cnt",),
    )
    recv2, one2, two2 = exchange(msg2, one2, two2)
    kept, arrived = call(
        gather_kernel,
        "take",
        {"pc": pc, "stay": stay, "pick": pick, "pv": pv, "edge": recv, "cnt": send_counts},
        {"kept": ((3, NP), f32), "arrived": ((3, 1, SECT * CAP), f32)},
        {"kept": ((3, NP), f32), "arrived": ((3, 1, SECT * CAP), f32)},
        2,
        flops=2 * NP * 512 * 384,
        in_smem=("cnt",),
    )
    (new,) = call(
        last_kernel,
        "second_section",
        {"mid": mid, "inner": recv2, "nu": nu, "mag": mag} | tables | {"edge": recv2, "one": one2, "two": two2, "rest": rest},
        {"new": field},
        materials_bufs | {"new": field},
        1,
    )
    new = jnp.swapaxes(new.reshape(3, TH, 2, 2, 128), 2, 3).reshape(3, TH, 2, NR)
    return new, kept, jnp.swapaxes(arrived, 0, 1)


def solution(mesh):
    return jax.shard_map(
        per_device,
        mesh=mesh,
        in_specs=(
            P(None, "az", "ax", None),
            P("az", "ax", None),
            P(None, "az", "ax", None),
            P(None, ("az", "ax")),
            P(None, ("az", "ax")),
            P(("az", "ax"), None, None),
            P(None, "ax", None),
        ),
        out_specs=(P(None, "az", "ax", None), P(None, ("az", "ax")), P(("az", "ax"), None, None)),
        check_vma=False,
    )
```

```python
import math

import jax
import jax.numpy as jnp
import numpy as np
from jax import lax
from jax.experimental import pallas as pl
from jax.experimental.pallas import tpu as pltpu
from jax.sharding import PartitionSpec as P

NA = 512
NR = 256
KR = 32
SECT = 8
TH = NA // SECT
CAP = 128
NP = 8192
DTHETA = 2.0 * math.pi / NA
DT = 0.02
POLE_SIGNS = (-1.0, -1.0, 1.0)
HIGHEST = lax.Precision.HIGHEST
f32 = jnp.float32
bf16 = jnp.bfloat16
i32 = jnp.int32
VMEM_LIMIT = 65408 * 1024

ROW_B = 64
ROW_EDGE = 128
EDGE_PART = 16
EDGE1 = 24
EDGE2 = 16
CHUNK = 2048


def filter_tables():
    a = np.arange(NA // 2)
    even, odd, even_mode, odd_mode = [], [], [], []
    for m in range(NA // 2 + 1):
        scale = math.sqrt((1.0 if m in (0, NA // 2) else 2.0) / NA)
        phase = 2.0 * math.pi * (m * a % NA) / NA
        rows = [scale * np.cos(phase)]
        if m not in (0, NA // 2):
            rows.append(scale * np.sin(phase))
        for row in rows:
            (odd if m % 2 else even).append(row)
            (odd_mode if m % 2 else even_mode).append(m)
    basis = np.stack([np.stack(even), np.stack(odd)]).astype(np.float32)
    modes = np.stack([np.array(even_mode), np.array(odd_mode)]).astype(np.float64)
    cutoff = 4.0 * (np.arange(KR) + 0.5)
    weight = 1.0 / (1.0 + (modes[:, :, None] / cutoff) ** 4)
    weight = np.tile(weight, (1, 1, 256 // KR)).astype(np.float32)
    return basis, np.ascontiguousarray(basis.transpose(0, 2, 1)), weight


BASIS, BASIS_T, MODE_WEIGHT = filter_tables()


def lane_iota(shape):
    return lax.broadcasted_iota(i32, shape, len(shape) - 1)


def row_iota(shape):
    return lax.broadcasted_iota(i32, shape, len(shape) - 2)


def strided(c, z, h):
    return pl.ds(c * 256 + h * 2 + z, TH, stride=4)


def block(c, z, h):
    return pl.ds(((c * 2 + z) * 2 + h) * TH, TH)


def lanes(x, by):
    by %= 128
    return x if by == 0 else pltpu.roll(x, by, 1)


def split2(x):
    hi = x.astype(bf16)
    return hi, (x - hi.astype(f32)).astype(bf16)


def split3(x):
    hi = x.astype(bf16)
    rest = x - hi.astype(f32)
    mid = rest.astype(bf16)
    return hi, mid, (rest - mid.astype(f32)).astype(bf16)


def pack_inner(field, nu):
    lane = lane_iota((TH, 128))

    def four(p, q, r, s):
        low = jnp.where(lane < 32, p, lanes(q, 32))
        high = jnp.where(lane < 96, lanes(r, 64), lanes(s, 96))
        return jnp.where(lane < 64, low, high)

    first = four(field[0][0][0], field[0][1][0], field[1][0][0], field[1][1][0])
    second = four(field[2][0][0], field[2][1][0], nu[0], nu[1])
    return first, second


def write_message(inner_ref, edge_ref, field, nu, me):
    first, second = pack_inner(field, nu)
    inner_ref[0:TH, :] = first
    inner_ref[TH : 2 * TH, :] = second
    up = (me + 1) % SECT
    for c in range(3):
        for z in range(2):
            for h in range(2):
                x = field[c][z][h]
                row = (c * 2 + z) * 2 + h
                for t in range(SECT):
                    edge_ref[t, row : row + 1, :] = jnp.where(t == up, x[TH - 1 : TH], x[0:1])


def send_message(out, edges):
    inner = out.vmem("inner")
    for t in range(SECT):
        out.copy(inner, out.hbm("msg").at[t, 0:ROW_EDGE, :])
    out.copy(edges, out.hbm("msg").at[:, ROW_EDGE:, :])


def write_axial(one_ref, two_ref, field, slab):
    odd = slab % 2 == 1
    for c in range(3):
        for h in range(2):
            rows = pl.ds((c * 2 + h) * TH, TH)
            low, high = field[c][0][h], field[c][1][h]
            one_ref[rows, :] = jnp.where(odd, low, high)
            two_ref[rows, :] = jnp.where(odd, high, low)


class Inputs:
    def __init__(self, names, refs, bufs, sems):
        self.refs = dict(zip(names, bufs))
        self.copies = {}
        for i, (name, ref, buf) in enumerate(zip(names, refs, bufs)):
            if name == "inner":
                ref = ref.at[:, 0:ROW_EDGE, :]
            if name == "edge":
                ref = ref.at[:, ROW_EDGE:, :]
            self.copies[name] = [pltpu.make_async_copy(ref, buf, sems.at[i])]
            self.copies[name][0].start()

    def __call__(self, name):
        for copy in self.copies.pop(name, ()):
            copy.wait()
        return self.refs[name]


class Outputs:
    def __init__(self, names, refs, bufs, sems):
        self.refs, self.bufs, self.sems, self.started = dict(zip(names, refs)), bufs, sems, []

    def hbm(self, name):
        return self.refs[name]

    def vmem(self, name):
        return self.bufs[name]

    def copy(self, src, dst):
        copy = pltpu.make_async_copy(src, dst, self.sems.at[len(self.started)])
        copy.start()
        self.started.append(copy)

    def send(self, name):
        self.copy(self.bufs[name], self.refs[name])

    def finish(self):
        for copy in self.started:
            copy.wait()


def pack_kernel(inp, out):
    me = lax.axis_index("az")
    slab = lax.axis_index("ax")
    pv_ref, pc_ref = inp("pv"), inp("pc")
    tmp_ref, nu_s, edge_ref, stay_ref = out.vmem("tmp"), out.vmem("nu"), out.vmem("edge"), out.vmem("stay")
    for i in range(64):
        tmp_ref[i * 8 : i * 8 + 3, :] = pv_ref[:, i * 128 : (i + 1) * 128]
        tmp_ref[512 + i * 8 : 512 + i * 8 + 3, :] = pc_ref[:, i * 128 : (i + 1) * 128].astype(f32)
    parts = []
    for k in range(2):
        for c in range(3):
            parts.append(split3(tmp_ref[pl.ds(k * 512 + c, 64, stride=8), :]))
    stack = jnp.concatenate([jnp.concatenate([p[s] for p in parts], axis=1) for s in range(3)], axis=0)
    rows_ref, cnt_ref = inp("rows"), inp("cnt")
    high_iota = row_iota((64, 128))
    low_iota = row_iota((128, 128))
    highs, lows, used_lows = [], [], []
    lane = lane_iota((1, 128))
    for t in range(SECT):
        row = rows_ref[0, t : t + 1, :]
        used = (lane < cnt_ref[me, 0, t]).astype(f32)
        highs.append((high_iota == row // 128).astype(f32).astype(bf16))
        low = (low_iota == row % 128).astype(f32)
        lows.append(low)
        used_lows.append((low * used).astype(bf16))
    high = jnp.concatenate(highs, axis=1)
    leaving = lax.dot_general(
        high, jnp.concatenate(used_lows, axis=1), (((1,), (1,)), ((), ())), preferred_element_type=f32
    )
    stay = 1.0 - leaving
    for i in range(64):
        stay_ref[0:1, i * 128 : (i + 1) * 128] = stay[i : i + 1, :]
    out.send("stay")
    picked = lax.dot_general(
        stack, jnp.concatenate([high, high, high], axis=0), (((0,), (0,)), ((), ())), preferred_element_type=f32
    )
    for t in range(SECT):
        for q in range(6):
            value = picked[q * 128 : (q + 1) * 128, t * 128 : (t + 1) * 128] * lows[t]
            edge_ref[t, EDGE_PART + q : EDGE_PART + q + 1, :] = jnp.sum(value, axis=0, keepdims=True)
    vel_ref, nu_ref = inp("vel"), inp("nu")
    field = [[[vel_ref[strided(c, z, h), :] for h in range(2)] for z in range(2)] for c in range(3)]
    nu_s[...] = nu_ref[...].astype(f32)
    nu = [nu_s[pl.ds(z, TH, stride=4), :] for z in range(2)]
    write_message(out.vmem("inner"), edge_ref, field, nu, me)
    send_message(out, edge_ref)
    write_axial(out.vmem("one"), out.vmem("two"), field, slab)
    out.send("one")
    out.send("two")


def local_row(theta, r, z, me, slab):
    return ((z - 2 * slab) * 2 + r // 128) * TH + theta - me * TH


def one_hot_pair(row, col, n):
    rows = (row_iota((256, n)) == row).astype(f32).astype(bf16)
    cols = row_iota((128, n)) == col
    return rows, cols


def deposit(row, col, velocity, n):
    rows, cols = one_hot_pair(row, col, n)
    pieces = []
    for c in range(3):
        for part in split2(velocity[c]):
            pieces.append(jnp.where(cols, part.astype(f32), 0.0).astype(bf16))
    pieces.append(cols.astype(f32).astype(bf16))
    return lax.dot_general(
        rows, jnp.concatenate(pieces, axis=0), (((1,), (1,)), ((), ())), preferred_element_type=f32
    )


def add_deposit(acc):
    out = [acc[:, c * 256 : c * 256 + 128] + acc[:, c * 256 + 128 : c * 256 + 256] for c in range(3)]
    out.append(acc[:, 768:896])
    return out


def scatter_kernel(inp, out):
    me = lax.axis_index("az")
    slab = lax.axis_index("ax")
    pc_ref, stay_ref, pv_ref = inp("pc"), inp("stay"), inp("pv")
    sum_ref, acc_ref = out.vmem("sums"), out.vmem("acc")
    for k in range(NP // CHUNK):
        part = pl.ds(k * CHUNK, CHUNK)
        row = local_row(pc_ref[0:1, part], pc_ref[1:2, part], pc_ref[2:3, part], me, slab)
        row = jnp.where(stay_ref[0:1, part] > 0.5, row, -1)
        col = pc_ref[1:2, part] % 128
        more = deposit(row, col, [pv_ref[c : c + 1, part] for c in range(3)], CHUNK)
        if k == 0:
            acc_ref[...] = more
        else:
            acc_ref[...] += more
    for c, x in enumerate(add_deposit(acc_ref[...])):
        sum_ref[c * 256 : (c + 1) * 256, :] = x
    out.send("sums")


def arrivals(edge_ref, cnt_ref, me, slab):
    lane = lane_iota((1, CAP))
    live = jnp.concatenate([(lane < cnt_ref[s, 0, me]).astype(i32) for s in range(SECT)], axis=1)

    def channel(q):
        return jnp.concatenate([edge_ref[s, EDGE_PART + q : EDGE_PART + q + 1, :] for s in range(SECT)], axis=1)

    velocity = [channel(c) for c in range(3)]
    theta, r, z = [channel(3 + c).astype(i32) for c in range(3)]
    row = jnp.where(live > 0, local_row(theta, r, z, me, slab), -1)
    return live, row, r % 128, velocity


def filtered_inner(inp, me):
    recv_ref = inp("inner")
    first = recv_ref[:, 0:TH, :].reshape(NA, 128)
    second = recv_ref[:, ROW_B : ROW_B + TH, :].reshape(NA, 128)
    lane = lane_iota((1, 128))
    radius = (lane % KR).astype(f32) + 0.5
    left = lane < 64
    first_swap = pltpu.roll(first, 64, 1)
    second_swap = pltpu.roll(second, 64, 1)
    nu = jnp.where(left, second_swap, second)
    swirl = jnp.where(left, first_swap, first)

    def differences(x):
        after = pltpu.roll(x, NA - 1, 0)
        before = pltpu.roll(x, 1, 0)
        lap = (after - 2.0 * x + before) * (1.0 / (radius * radius * (DTHETA * DTHETA)))
        return lap, (after - before) * (1.0 / (2.0 * DTHETA * radius))

    lap, grad = differences(first)
    cross = jnp.where(left, -2.0, 2.0) / radius
    part_first = nu * lap - swirl * grad + cross * nu * pltpu.roll(grad, 64, 1)
    lap, grad = differences(second)
    part_second = jnp.where(left, nu * lap - swirl * grad, 0.0)
    part = jnp.concatenate([part_first, part_second], axis=1)
    low, high = part[: NA // 2], part[NA // 2 :]
    basis_ref, weight_ref, basis_t_ref = inp("basis"), inp("weight"), inp("basis_t")
    own = pl.ds(pl.multiple_of((me % 4) * TH, TH), TH)
    out = 0.0
    for parity, x in enumerate((low + high, low - high)):
        spectrum = jnp.dot(basis_ref[parity], x, precision=HIGHEST, preferred_element_type=f32)
        spectrum = spectrum * weight_ref[parity]
        back = jnp.dot(basis_t_ref[parity, own, :], spectrum, precision=HIGHEST, preferred_element_type=f32)
        if parity:
            back = jnp.where(me < 4, back, -back)
        out = out + back
    return out[:, :128], out[:, 128:]


def fluid_rate(field, nu, magnetic, inp, me, slab):
    filtered = filtered_inner(inp, me)
    recv_ref, edge_ref, one_ref, two_ref = inp("inner"), inp("edge"), inp("one"), inp("two")
    odd = slab % 2 == 1
    before_sector = (me + SECT - 1) % SECT
    after_sector = (me + 1) % SECT
    opposite = (me + SECT // 2) % SECT
    lane = lane_iota((TH, 128))
    row = row_iota((TH, 128))
    poles = [recv_ref[opposite, 0:TH, :], recv_ref[opposite, ROW_B : ROW_B + TH, :]]
    rates = [[[None, None], [None, None]] for _ in range(3)]
    for z in range(2):
        ghosts = []
        for c in range(3):
            ghosts.append(POLE_SIGNS[c] * lanes(poles[c // 2], -((c % 2) * 64 + z * 32)))
        rolled = [[(pltpu.roll(field[c][z][h], 1, 1), pltpu.roll(field[c][z][h], 127, 1)) for h in range(2)] for c in range(3)]
        for h in range(2):
            radius = lane_iota((1, 128)).astype(f32) + (h * 128 + 0.5)
            inverse = 1.0 / radius
            eddy = nu[z][h]
            u = [field[c][z][h] for c in range(3)]
            lap_ax, lap_rad, grad_rad, grad_ax, lap_th, grad_th = [], [], [], [], [], []
            for c in range(3):
                x = u[c]
                if h == 0:
                    prev_r = jnp.where(lane == 0, ghosts[c], rolled[c][0][0])
                    next_r = jnp.where(lane == 127, rolled[c][1][1], rolled[c][0][1])
                else:
                    prev_r = jnp.where(lane == 0, rolled[c][0][0], rolled[c][1][0])
                    next_r = jnp.where(lane == 127, 0.0, rolled[c][1][1])
                face = pl.ds((c * 2 + h) * TH, TH)
                if z == 0:
                    prev_z = jnp.where(odd, one_ref[face, :], two_ref[face, :])
                    next_z = field[c][1][h]
                else:
                    prev_z = field[c][0][h]
                    next_z = jnp.where(odd, two_ref[face, :], one_ref[face, :])
                halo = (c * 2 + z) * 2 + h
                prev_t = jnp.where(row == 0, edge_ref[before_sector, halo : halo + 1, :], pltpu.roll(x, 1, 0))
                next_t = jnp.where(row == TH - 1, edge_ref[after_sector, halo : halo + 1, :], pltpu.roll(x, TH - 1, 0))
                lap_rad.append(((radius + 0.5) * (next_r - x) - (radius - 0.5) * (x - prev_r)) * inverse)
                lap_ax.append(next_z - 2.0 * x + prev_z)
                grad_rad.append(0.5 * (next_r - prev_r))
                grad_ax.append(0.5 * (next_z - prev_z))
                lap_th.append((next_t - 2.0 * x + prev_t) * (1.0 / (radius * radius * (DTHETA * DTHETA))))
                grad_th.append((next_t - prev_t) * (1.0 / (2.0 * DTHETA * radius)))
            b = [magnetic[c][z][h] for c in range(3)]
            slip = [-u[0], radius * (2.0 / NR) - u[1], -u[2]]
            current = [slip[1] * b[2] - slip[2] * b[1], slip[2] * b[0] - slip[0] * b[2], slip[0] * b[1] - slip[1] * b[0]]
            force = [
                current[1] * b[2] - current[2] * b[1],
                current[2] * b[0] - current[0] * b[2],
                current[0] * b[1] - current[1] * b[0],
            ]
            inverse2 = inverse * inverse
            metric = [
                u[1] * u[1] * inverse - eddy * u[0] * inverse2,
                -eddy * u[1] * inverse2 - u[0] * u[1] * inverse,
                0.0,
            ]
            coupling = [-2.0 * eddy * grad_th[1] * inverse, 2.0 * eddy * grad_th[0] * inverse, 0.0]
            for c in range(3):
                azimuth = eddy * lap_th[c] - u[1] * grad_th[c] + coupling[c]
                if h == 0:
                    inner = lanes(filtered[c // 2], -((c % 2) * 64 + z * 32))
                    azimuth = jnp.where(lane < KR, inner, azimuth)
                rates[c][z][h] = (
                    eddy * (lap_rad[c] + lap_ax[c])
                    - (u[0] * grad_rad[c] + u[2] * grad_ax[c])
                    + metric[c]
                    + 0.5 * force[c]
                    + azimuth
                )
    return rates


def materials(inp, out):
    nu_s, mag_s = out.vmem("nu"), out.vmem("mag")
    nu_s[...] = inp("nu")[...].astype(f32)
    mag_s[...] = inp("mag")[...].astype(f32)
    nu = [[nu_s[strided(0, z, h), :] for h in range(2)] for z in range(2)]
    magnetic = [[[mag_s[strided(c, z, h), :] for h in range(2)] for z in range(2)] for c in range(3)]
    return nu, magnetic


def first_kernel(inp, out):
    me = lax.axis_index("az")
    slab = lax.axis_index("ax")
    live, row, col, velocity = arrivals(inp("edge"), inp("cnt"), me, slab)
    arrived = add_deposit(deposit(row, col, velocity, SECT * CAP))
    sum_ref = inp("sums")
    total = [sum_ref[c * 256 : (c + 1) * 256, :] + arrived[c] for c in range(4)]
    nu, magnetic = materials(inp, out)
    vel_ref = inp("vel")
    field = [[[vel_ref[strided(c, z, h), :] for h in range(2)] for z in range(2)] for c in range(3)]
    rates = fluid_rate(field, nu, magnetic, inp, me, slab)
    mid_ref, rest_ref, pick_ref = out.vmem("mid"), out.vmem("rest"), out.vmem("pick")
    mid = [[[None, None], [None, None]] for _ in range(3)]
    picks = []
    for c in range(3):
        halves = []
        for z in range(2):
            for h in range(2):
                at = slice((z * 2 + h) * TH, (z * 2 + h + 1) * TH)
                x, s, n = field[c][z][h], total[c][at], total[3][at]
                u1 = x + DT * (rates[c][z][h] + 2.0 * (s - n * x))
                mid[c][z][h] = u1
                mid_ref[block(c, z, h), :] = u1
                rest_ref[block(c, z, h), :] = 0.5 * (x + u1) + DT * (0.8 * s + 0.2 * n * x - n * u1)
                halves.append(0.08 * x + 0.1 * u1)
        picks.append(jnp.concatenate(halves, axis=0))
    write_message(out.vmem("inner"), out.vmem("edge"), mid, [nu[z][0] for z in range(2)], me)
    send_message(out, out.vmem("edge"))
    write_axial(out.vmem("one"), out.vmem("two"), mid, slab)
    out.send("one")
    out.send("two")
    out.send("mid")
    out.send("rest")
    for c in range(3):
        hi, lo = split2(picks[c].T)
        pick_ref[c * 128 : (c + 1) * 128, 0:256] = hi
        pick_ref[c * 128 : (c + 1) * 128, 256:512] = lo
    out.send("pick")


def take(pick, row, col, n):
    rows, cols = one_hot_pair(row, col, n)
    got = jnp.dot(pick, jnp.concatenate([rows, rows], axis=0), preferred_element_type=f32)
    return [jnp.sum(jnp.where(cols, got[c * 128 : (c + 1) * 128], 0.0), axis=0, keepdims=True) for c in range(3)]


def gather_kernel(inp, out):
    me = lax.axis_index("az")
    slab = lax.axis_index("ax")
    pc_ref, stay_ref, pv_ref = inp("pc"), inp("stay"), inp("pv")
    kept_ref, arr_ref = out.vmem("kept"), out.vmem("arrived")
    pick = inp("pick")[...]
    for k in range(NP // CHUNK):
        part = pl.ds(k * CHUNK, CHUNK)
        row = local_row(pc_ref[0:1, part], pc_ref[1:2, part], pc_ref[2:3, part], me, slab)
        stay = stay_ref[0:1, part] > 0.5
        row = jnp.where(stay, row, -1)
        got = take(pick, row, pc_ref[1:2, part] % 128, CHUNK)
        for c in range(3):
            kept_ref[c : c + 1, part] = jnp.where(stay, 0.82 * pv_ref[c : c + 1, part] + got[c], 0.0)
    out.send("kept")
    live, row, col, velocity = arrivals(inp("edge"), inp("cnt"), me, slab)
    got = take(pick, row, col, SECT * CAP)
    for c in range(3):
        arr_ref[c, 0:1, :] = jnp.where(live > 0, 0.82 * velocity[c] + got[c], 0.0)
    out.send("arrived")


def last_kernel(inp, out):
    me = lax.axis_index("az")
    slab = lax.axis_index("ax")
    mid_ref = inp("mid")
    field = [[[mid_ref[block(c, z, h), :] for h in range(2)] for z in range(2)] for c in range(3)]
    nu, magnetic = materials(inp, out)
    rates = fluid_rate(field, nu, magnetic, inp, me, slab)
    rest_ref, out_ref = inp("rest"), out.vmem("new")
    for c in range(3):
        for z in range(2):
            for h in range(2):
                out_ref[strided(c, z, h), :] = rest_ref[block(c, z, h), :] + (0.5 * DT) * rates[c][z][h]
    out.send("new")


def call(kernel, name, ins, outs, bufs, copies, flops=0, in_smem=()):
    in_names, out_names, buf_names = list(ins), list(outs), list(bufs)
    arrays = [ins[n] for n in in_names]
    n_in, n_out = len(in_names), len(out_names)

    def body(*refs):
        in_refs, refs = refs[:n_in], refs[n_in:]
        out_refs, refs = refs[:n_out], refs[n_out:]
        in_bufs, refs = refs[:n_in], refs[n_in:]
        buf_refs, (in_sems, out_sems) = refs[:-2], refs[-2:]
        out = Outputs(out_names, out_refs, dict(zip(buf_names, buf_refs)), out_sems)
        kernel(Inputs(in_names, in_refs, in_bufs, in_sems), out)
        out.finish()

    def in_shape(n):
        shape = ins[n].shape
        return {"inner": (SECT, ROW_EDGE, 128), "edge": (SECT, shape[1] - ROW_EDGE, 128)}.get(n, shape)

    hbm = pl.BlockSpec(memory_space=pltpu.HBM)
    return pl.pallas_call(
        body,
        out_shape=[jax.ShapeDtypeStruct(*outs[n]) for n in out_names],
        in_specs=[hbm] * n_in,
        out_specs=[hbm] * n_out,
        scratch_shapes=[(pltpu.SMEM if n in in_smem else pltpu.VMEM)(in_shape(n), ins[n].dtype) for n in in_names]
        + [pltpu.VMEM(*bufs[n]) for n in buf_names]
        + [pltpu.SemaphoreType.DMA((n_in,)), pltpu.SemaphoreType.DMA((copies,))],
        compiler_params=pltpu.CompilerParams(vmem_limit_bytes=VMEM_LIMIT),
        cost_estimate=pl.CostEstimate(flops=flops, bytes_accessed=2 * 1024 * 1024, transcendentals=0),
        name=name,
    )(*arrays)


def rows_of(x):
    lead = x.shape[:-2]
    x = x.reshape(*lead, 2, 2, 128)
    return jnp.swapaxes(x, -3, -2).reshape(-1, 128)


def per_device(velocity, viscosity, bfield, particle_velocity, particle_cell, send_rows, send_counts):
    ax = lax.axis_size("ax")
    vel, nu, mag = rows_of(velocity), rows_of(viscosity), rows_of(bfield)
    pv, pc = particle_velocity, particle_cell
    tables = {"basis": jnp.asarray(BASIS), "weight": jnp.asarray(MODE_WEIGHT), "basis_t": jnp.asarray(BASIS_T)}
    swap_one = [(i, i ^ 1) for i in range(ax)]
    swap_two = [(i, ((i + 1) ^ 1) - 1) for i in range(1, ax - 1)]

    def exchange(msg, one, two):
        one = lax.ppermute(one, "ax", swap_one)
        two = lax.ppermute(two, "ax", swap_two)
        return lax.all_to_all(msg, "az", split_axis=0, concat_axis=0, tiled=True), one, two

    face = ((384, 128), f32)
    field = ((768, 128), f32)
    materials_bufs = {"nu": ((256, 128), f32), "mag": field}
    message_bufs = {"inner": ((ROW_EDGE, 128), f32), "one": face, "two": face}
    msg, one, two, stay = call(
        pack_kernel,
        "pack",
        {"pc": pc, "pv": pv, "rows": send_rows, "cnt": send_counts, "vel": vel, "nu": nu},
        {"msg": ((SECT, ROW_EDGE + EDGE1, 128), f32), "one": face, "two": face, "stay": ((1, NP), f32)},
        message_bufs
        | {"edge": ((SECT, EDGE1, 128), f32), "stay": ((1, NP), f32), "tmp": ((1024, 128), f32), "nu": ((256, 128), f32)},
        12,
        in_smem=("cnt",),
    )
    recv, one, two = exchange(msg, one, two)
    (sums,) = call(
        scatter_kernel,
        "deposit",
        {"pc": pc, "stay": stay, "pv": pv},
        {"sums": ((1024, 128), f32)},
        {"sums": ((1024, 128), f32), "acc": ((256, 896), f32)},
        1,
        flops=2 * NP * 256 * 896,
    )
    msg2, one2, two2, mid, rest, pick = call(
        first_kernel,
        "first_section",
        {"edge": recv, "cnt": send_counts, "inner": recv, "sums": sums, "nu": nu, "mag": mag, "vel": vel}
        | tables
        | {"one": one, "two": two},
        {
            "msg": ((SECT, ROW_EDGE + EDGE2, 128), f32),
            "one": face,
            "two": face,
            "mid": field,
            "rest": field,
            "pick": ((384, 512), bf16),
        },
        message_bufs
        | materials_bufs
        | {"edge": ((SECT, EDGE2, 128), f32), "mid": field, "rest": field, "pick": ((384, 512), bf16)},
        14,
        in_smem=("cnt",),
    )
    recv2, one2, two2 = exchange(msg2, one2, two2)
    kept, arrived = call(
        gather_kernel,
        "take",
        {"pc": pc, "stay": stay, "pick": pick, "pv": pv, "edge": recv, "cnt": send_counts},
        {"kept": ((3, NP), f32), "arrived": ((3, 1, SECT * CAP), f32)},
        {"kept": ((3, NP), f32), "arrived": ((3, 1, SECT * CAP), f32)},
        2,
        flops=2 * NP * 512 * 384,
        in_smem=("cnt",),
    )
    (new,) = call(
        last_kernel,
        "second_section",
        {"mid": mid, "inner": recv2, "nu": nu, "mag": mag} | tables | {"edge": recv2, "one": one2, "two": two2, "rest": rest},
        {"new": field},
        materials_bufs | {"new": field},
        1,
    )
    new = jnp.swapaxes(new.reshape(3, TH, 2, 2, 128), 2, 3).reshape(3, TH, 2, NR)
    return new, kept, jnp.swapaxes(arrived, 0, 1)


def solution(mesh):
    return jax.shard_map(
        per_device,
        mesh=mesh,
        in_specs=(
            P(None, "az", "ax", None),
            P("az", "ax", None),
            P(None, "az", "ax", None),
            P(None, ("az", "ax")),
            P(None, ("az", "ax")),
            P(("az", "ax"), None, None),
            P(None, "ax", None),
        ),
        out_specs=(P(None, "az", "ax", None), P(None, ("az", "ax")), P(("az", "ax"), None, None)),
        check_vma=False,
    )
```

```python
import math

import jax
import jax.numpy as jnp
import numpy as np
from jax import lax
from jax.experimental import pallas as pl
from jax.experimental.pallas import tpu as pltpu
from jax.sharding import PartitionSpec as P

NA = 512
NR = 256
KR = 32
SECT = 8
TH = NA // SECT
CAP = 128
NP = 8192
DTHETA = 2.0 * math.pi / NA
DT = 0.02
POLE_SIGNS = (-1.0, -1.0, 1.0)
HIGHEST = lax.Precision.HIGHEST
f32 = jnp.float32
bf16 = jnp.bfloat16
i32 = jnp.int32
VMEM_LIMIT = 65408 * 1024

ROW_B = 64
ROW_EDGE1 = 128
ROW_EDGE2 = 96
EDGE_PART = 16
EDGE1 = 24
EDGE2 = 16
CHUNK = 1024


def filter_tables():
    a = np.arange(NA // 2)
    even, odd, even_mode, odd_mode = [], [], [], []
    for m in range(NA // 2 + 1):
        scale = math.sqrt((1.0 if m in (0, NA // 2) else 2.0) / NA)
        phase = 2.0 * math.pi * (m * a % NA) / NA
        rows = [scale * np.cos(phase)]
        if m not in (0, NA // 2):
            rows.append(scale * np.sin(phase))
        for row in rows:
            (odd if m % 2 else even).append(row)
            (odd_mode if m % 2 else even_mode).append(m)
    basis = np.stack([np.stack(even), np.stack(odd)]).astype(np.float32)
    modes = np.stack([np.array(even_mode), np.array(odd_mode)]).astype(np.float64)
    cutoff = 4.0 * (np.arange(KR) + 0.5)
    weight = 1.0 / (1.0 + (modes[:, :, None] / cutoff) ** 4)
    weight = np.tile(weight, (1, 1, 128 // KR)).astype(np.float32)
    return basis, np.ascontiguousarray(basis.transpose(0, 2, 1)), weight


BASIS, BASIS_T, MODE_WEIGHT = filter_tables()


def lane_iota(shape):
    return lax.broadcasted_iota(i32, shape, len(shape) - 1)


def row_iota(shape):
    return lax.broadcasted_iota(i32, shape, len(shape) - 2)


def strided(c, z, h):
    return pl.ds(c * 256 + h * 2 + z, TH, stride=4)


def block(c, z, h):
    return pl.ds(((c * 2 + z) * 2 + h) * TH, TH)


def lanes(x, by):
    by %= 128
    return x if by == 0 else pltpu.roll(x, by, 1)


def split2(x):
    hi = x.astype(bf16)
    return hi, (x - hi.astype(f32)).astype(bf16)


def split3(x):
    hi = x.astype(bf16)
    rest = x - hi.astype(f32)
    mid = rest.astype(bf16)
    return hi, mid, (rest - mid.astype(f32)).astype(bf16)


def pack_inner(field, nu):
    lane = lane_iota((TH, 128))

    def four(p, q, r, s):
        low = jnp.where(lane < 32, p, lanes(q, 32))
        high = jnp.where(lane < 96, lanes(r, 64), lanes(s, 96))
        return jnp.where(lane < 64, low, high)

    first = four(field[0][0][0], field[0][1][0], field[1][0][0], field[1][1][0])
    second = four(field[2][0][0], field[2][1][0], nu[0], nu[1])
    return first, second


def write_edges(edge_ref, field, me):
    up = (me + 1) % SECT
    for c in range(3):
        for z in range(2):
            for h in range(2):
                x = field[c][z][h]
                row = (c * 2 + z) * 2 + h
                for t in range(SECT):
                    edge_ref[t, row : row + 1, :] = jnp.where(t == up, x[TH - 1 : TH], x[0:1])


def send_inner(out, rows):
    for t in range(SECT):
        out.copy(out.vmem("inner"), out.hbm("msg").at[t, 0:rows, :])


def write_axial(one_ref, two_ref, field, slab):
    odd = slab % 2 == 1
    for c in range(3):
        for h in range(2):
            rows = pl.ds((c * 2 + h) * TH, TH)
            low, high = field[c][0][h], field[c][1][h]
            one_ref[rows, :] = jnp.where(odd, low, high)
            two_ref[rows, :] = jnp.where(odd, high, low)


def message_rows(name, rows):
    edge = ROW_EDGE1 if rows == ROW_EDGE1 + EDGE1 else ROW_EDGE2
    return {"inner": slice(0, edge), "edge": slice(edge, rows), "inner_nu": slice(ROW_B, edge)}[name]


class Inputs:
    def __init__(self, names, refs, bufs, sems):
        self.refs = dict(zip(names, bufs))
        self.copies = {}
        for i, (name, ref, buf) in enumerate(zip(names, refs, bufs)):
            if name in ("inner", "edge", "inner_nu"):
                ref = ref.at[:, message_rows(name, ref.shape[1]), :]
            if name == "basis_t":
                own = lax.axis_index("az") % 4
                ref = ref.at[:, pl.ds(pl.multiple_of(own * TH, TH), TH), :]
            self.copies[name] = [pltpu.make_async_copy(ref, buf, sems.at[i])]
            self.copies[name][0].start()

    def __call__(self, name):
        for copy in self.copies.pop(name, ()):
            copy.wait()
        return self.refs[name]


class Outputs:
    def __init__(self, names, refs, bufs, sems):
        self.refs, self.bufs, self.sems, self.started = dict(zip(names, refs)), bufs, sems, []

    def hbm(self, name):
        return self.refs[name]

    def vmem(self, name):
        return self.bufs[name]

    def copy(self, src, dst):
        copy = pltpu.make_async_copy(src, dst, self.sems.at[len(self.started)])
        copy.start()
        self.started.append(copy)

    def send(self, name):
        self.copy(self.bufs[name], self.refs[name])

    def finish(self):
        for copy in self.started:
            copy.wait()


def pack_kernel(inp, out):
    me = lax.axis_index("az")
    tmp_ref, nu_s, edge_ref, stay_ref = out.vmem("tmp"), out.vmem("nu"), out.vmem("edge"), out.vmem("stay")
    vel_ref, nu_ref = inp("vel"), inp("nu")
    field = [[[vel_ref[strided(c, z, h), :] for h in range(2)] for z in range(2)] for c in range(3)]
    nu_s[...] = nu_ref[...].astype(f32)
    nu = [nu_s[pl.ds(z, TH, stride=4), :] for z in range(2)]
    inner_ref = out.vmem("inner")
    inner_ref[0:TH, :], inner_ref[TH:, :] = pack_inner(field, nu)
    send_inner(out, ROW_EDGE1)
    write_axial(out.vmem("one"), out.vmem("two"), field, lax.axis_index("ax"))
    out.send("one")
    out.send("two")
    write_edges(edge_ref, field, me)
    pv_ref, pc_ref = inp("pv"), inp("pc")
    for i in range(64):
        tmp_ref[i * 8 : i * 8 + 3, :] = pv_ref[:, i * 128 : (i + 1) * 128]
        tmp_ref[512 + i * 8 : 512 + i * 8 + 3, :] = pc_ref[:, i * 128 : (i + 1) * 128].astype(f32)
    parts = []
    for k in range(2):
        for c in range(3):
            parts.append(split3(tmp_ref[pl.ds(k * 512 + c, 64, stride=8), :]))
    stack = jnp.concatenate([jnp.concatenate([p[s] for p in parts], axis=1) for s in range(3)], axis=0)
    rows_ref, cnt_ref = inp("rows"), inp("cnt")
    high_iota = row_iota((64, 128))
    low_iota = row_iota((128, 128))
    highs, lows, used_lows = [], [], []
    lane = lane_iota((1, 128))
    for t in range(SECT):
        row = rows_ref[0, t : t + 1, :]
        used = (lane < cnt_ref[me, 0, t]).astype(f32)
        highs.append((high_iota == row // 128).astype(f32).astype(bf16))
        low = (low_iota == row % 128).astype(f32)
        lows.append(low)
        used_lows.append((low * used).astype(bf16))
    high = jnp.concatenate(highs, axis=1)
    leaving = lax.dot_general(
        high, jnp.concatenate(used_lows, axis=1), (((1,), (1,)), ((), ())), preferred_element_type=f32
    )
    stay = 1.0 - leaving
    for i in range(64):
        stay_ref[0:1, i * 128 : (i + 1) * 128] = stay[i : i + 1, :]
    out.send("stay")
    picked = lax.dot_general(
        stack, jnp.concatenate([high, high, high], axis=0), (((0,), (0,)), ((), ())), preferred_element_type=f32
    )
    for t in range(SECT):
        for q in range(6):
            value = picked[q * 128 : (q + 1) * 128, t * 128 : (t + 1) * 128] * lows[t]
            edge_ref[t, EDGE_PART + q : EDGE_PART + q + 1, :] = jnp.sum(value, axis=0, keepdims=True)
    out.copy(edge_ref, out.hbm("msg").at[:, ROW_EDGE1:, :])


def local_row(theta, r, z, me, slab):
    return ((z - 2 * slab) * 2 + r // 128) * TH + theta - me * TH


def spread(x, rows, n):
    tile = jnp.broadcast_to(x, (16, n)).astype(bf16)
    return jnp.concatenate([tile] * (rows // 16), axis=0)


def matches(index, rows, n):
    return row_iota((rows, n)).astype(f32).astype(bf16) == spread(index.astype(f32), rows, n)


def one_hot(index, rows, n):
    return jnp.where(matches(index, rows, n), jnp.ones((), bf16), jnp.zeros((), bf16))


def deposit(row, col, velocity, n):
    cols = matches(col, 128, n)
    pieces = []
    for c in range(3):
        for part in split2(velocity[c]):
            pieces.append(jnp.where(cols, spread(part.astype(f32), 128, n), jnp.zeros((), bf16)))
    pieces.append(one_hot(col, 128, n))
    return lax.dot_general(
        one_hot(row, 256, n), jnp.concatenate(pieces, axis=0), (((1,), (1,)), ((), ())), preferred_element_type=f32
    )


def add_parts(acc):
    out = [acc[:, c * 256 : c * 256 + 128] + acc[:, c * 256 + 128 : c * 256 + 256] for c in range(3)]
    out.append(acc[:, 768:896])
    return out


def write_blocks(ref, x):
    for c in range(3):
        for z in range(2):
            for h in range(2):
                ref[block(c, z, h), :] = x[c][z][h]


def scatter_kernel(inp, out):
    me = lax.axis_index("az")
    slab = lax.axis_index("ax")
    pc_ref, stay_ref, pv_ref = inp("pc"), inp("stay"), inp("pv")
    sum_ref, acc_ref = out.vmem("sums"), out.vmem("acc")
    for k in range(NP // CHUNK):
        part = pl.ds(k * CHUNK, CHUNK)
        row = local_row(pc_ref[0:1, part], pc_ref[1:2, part], pc_ref[2:3, part], me, slab)
        row = jnp.where(stay_ref[0:1, part] > 0.5, row, -1)
        col = pc_ref[1:2, part] % 128
        more = deposit(row, col, [pv_ref[c : c + 1, part] for c in range(3)], CHUNK)
        if k == 0:
            acc_ref[...] = more
        else:
            acc_ref[...] += more
    for c, x in enumerate(add_parts(acc_ref)):
        sum_ref[c * 256 : (c + 1) * 256, :] = x
    out.send("sums")
    rates = local_rate(input_blocks(inp), viscosity_blocks(inp, out), magnetic_blocks(inp, out))
    write_blocks(out.vmem("local"), rates)
    out.send("local")


def arrivals(edge_ref, cnt_ref, me, slab):
    lane = lane_iota((1, CAP))
    live = jnp.concatenate([(lane < cnt_ref[s, 0, me]).astype(i32) for s in range(SECT)], axis=1)

    def channel(q):
        return jnp.concatenate([edge_ref[s, EDGE_PART + q : EDGE_PART + q + 1, :] for s in range(SECT)], axis=1)

    velocity = [channel(c) for c in range(3)]
    theta, r, z = [channel(3 + c).astype(i32) for c in range(3)]
    row = jnp.where(live > 0, local_row(theta, r, z, me, slab), -1)
    return live, row, r % 128, velocity


def inner_fields(inp):
    recv_ref = inp("inner")
    first = recv_ref[:, 0:TH, :].reshape(NA, 128)
    if recv_ref.shape[1] == ROW_EDGE1:
        return first, recv_ref[:, ROW_B : ROW_B + TH, :].reshape(NA, 128)
    halves = []
    for t in range(SECT):
        x = recv_ref[t, ROW_B : ROW_B + TH // 2, :]
        halves += [x, pltpu.roll(x, 64, 1)]
    second = jnp.concatenate(halves, axis=0)
    return first, jnp.where(lane_iota((NA, 128)) < 64, second, inp("inner_nu")[...].reshape(NA, 128))


def filtered_inner(inp, me):
    first, second = inner_fields(inp)
    lane = lane_iota((1, 128))
    radius = (lane % KR).astype(f32) + 0.5
    left = lane < 64
    first_swap = pltpu.roll(first, 64, 1)
    second_swap = pltpu.roll(second, 64, 1)
    nu = jnp.where(left, second_swap, second)
    swirl = jnp.where(left, first_swap, first)

    def differences(x):
        after = pltpu.roll(x, NA - 1, 0)
        before = pltpu.roll(x, 1, 0)
        lap = (after - 2.0 * x + before) * (1.0 / (radius * radius * (DTHETA * DTHETA)))
        return lap, (after - before) * (1.0 / (2.0 * DTHETA * radius))

    lap, grad = differences(first)
    cross = jnp.where(left, -2.0, 2.0) / radius
    part_first = nu * lap - swirl * grad + cross * nu * pltpu.roll(grad, 64, 1)
    lap, grad = differences(second)
    part_second = jnp.where(left, nu * lap - swirl * grad, 0.0)
    part = jnp.concatenate([part_first, part_second], axis=1)
    low, high = part[: NA // 2], part[NA // 2 :]
    basis_ref, weight_ref, basis_t_ref = inp("basis"), inp("weight"), inp("basis_t")
    out = 0.0
    for parity, x in enumerate((low + high, low - high)):
        spectrum = jnp.dot(basis_ref[parity], x, precision=HIGHEST, preferred_element_type=f32)
        weight = weight_ref[parity]
        spectrum = spectrum * jnp.concatenate([weight, weight], axis=1)
        back = jnp.dot(basis_t_ref[parity], spectrum, precision=HIGHEST, preferred_element_type=f32)
        if parity:
            back = jnp.where(me < 4, back, -back)
        out = out + back
    return out[:, :128], out[:, 128:]


def local_rate(field, nu, magnetic):
    lane = lane_iota((TH, 128))
    row = row_iota((TH, 128))
    rates = [[[None, None], [None, None]] for _ in range(3)]
    for z in range(2):
        rolled = [[(pltpu.roll(field[c][z][h], 1, 1), pltpu.roll(field[c][z][h], 127, 1)) for h in range(2)] for c in range(3)]
        for h in range(2):
            radius = lane_iota((1, 128)).astype(f32) + (h * 128 + 0.5)
            inverse = 1.0 / radius
            eddy = nu[z][h]
            u = [field[c][z][h] for c in range(3)]
            lap_ax, lap_rad, grad_rad, grad_ax, lap_th, grad_th = [], [], [], [], [], []
            for c in range(3):
                x = u[c]
                if h == 0:
                    prev_r = jnp.where(lane == 0, 0.0, rolled[c][0][0])
                    next_r = jnp.where(lane == 127, rolled[c][1][1], rolled[c][0][1])
                else:
                    prev_r = jnp.where(lane == 0, rolled[c][0][0], rolled[c][1][0])
                    next_r = jnp.where(lane == 127, 0.0, rolled[c][1][1])
                other = field[c][1 - z][h]
                prev_t = jnp.where(row == 0, 0.0, pltpu.roll(x, 1, 0))
                next_t = jnp.where(row == TH - 1, 0.0, pltpu.roll(x, TH - 1, 0))
                lap_rad.append(((radius + 0.5) * (next_r - x) - (radius - 0.5) * (x - prev_r)) * inverse)
                lap_ax.append(other - 2.0 * x)
                grad_rad.append(0.5 * (next_r - prev_r))
                grad_ax.append((0.5 if z == 0 else -0.5) * other)
                lap_th.append((next_t - 2.0 * x + prev_t) * (1.0 / (radius * radius * (DTHETA * DTHETA))))
                grad_th.append((next_t - prev_t) * (1.0 / (2.0 * DTHETA * radius)))
            b = [magnetic[c][z][h] for c in range(3)]
            slip = [-u[0], radius * (2.0 / NR) - u[1], -u[2]]
            current = [slip[1] * b[2] - slip[2] * b[1], slip[2] * b[0] - slip[0] * b[2], slip[0] * b[1] - slip[1] * b[0]]
            force = [
                current[1] * b[2] - current[2] * b[1],
                current[2] * b[0] - current[0] * b[2],
                current[0] * b[1] - current[1] * b[0],
            ]
            inverse2 = inverse * inverse
            metric = [
                u[1] * u[1] * inverse - eddy * u[0] * inverse2,
                -eddy * u[1] * inverse2 - u[0] * u[1] * inverse,
                0.0,
            ]
            coupling = [-2.0 * eddy * grad_th[1] * inverse, 2.0 * eddy * grad_th[0] * inverse, 0.0]
            for c in range(3):
                azimuth = eddy * lap_th[c] - u[1] * grad_th[c] + coupling[c]
                if h == 0:
                    azimuth = jnp.where(lane < KR, 0.0, azimuth)
                rates[c][z][h] = (
                    eddy * (lap_rad[c] + lap_ax[c])
                    - (u[0] * grad_rad[c] + u[2] * grad_ax[c])
                    + metric[c]
                    + 0.5 * force[c]
                    + azimuth
                )
    return rates


def outer_rate(field, nu, inp, me, slab):
    filtered = filtered_inner(inp, me)
    recv_ref, edge_ref, one_ref, two_ref = inp("inner"), inp("edge"), inp("one"), inp("two")
    before_sector = (me + SECT - 1) % SECT
    after_sector = (me + 1) % SECT
    opposite = (me + SECT // 2) % SECT
    odd = slab % 2 == 1
    lane = lane_iota((TH, 128))
    row = row_iota((8, 128))
    poles = [recv_ref[opposite, 0:TH, :]]
    if recv_ref.shape[1] == ROW_EDGE1:
        poles.append(recv_ref[opposite, ROW_B : ROW_B + TH, :])
    else:
        pole = recv_ref[opposite, ROW_B : ROW_B + TH // 2, :]
        poles.append(jnp.concatenate([pole, pltpu.roll(pole, 64, 1)], axis=0))
    rates = [[[None, None], [None, None]] for _ in range(3)]
    for z in range(2):
        for h in range(2):
            radius = lane_iota((1, 128)).astype(f32) + (h * 128 + 0.5)
            lap_factor = 1.0 / (radius * radius * (DTHETA * DTHETA))
            grad_factor = 1.0 / (2.0 * DTHETA * radius)
            cross = 2.0 * grad_factor / radius
            eddy, u = nu[z][h], [field[c][z][h] for c in range(3)]
            by_face = eddy + (0.5 if z == 0 else -0.5) * u[2]
            end = slab == (0 if z == 0 else lax.axis_size("ax") - 1)
            halos = []
            for sector, at, sign in ((before_sector, slice(0, 8), -1.0), (after_sector, slice(TH - 8, TH), 1.0)):
                f = [edge_ref[sector, (c * 2 + z) * 2 + h : (c * 2 + z) * 2 + h + 1, :] for c in range(3)]
                nu8, swirl8 = eddy[at], u[1][at]
                by_halo = nu8 * lap_factor - sign * swirl8 * grad_factor
                extra = [-sign * cross * nu8 * f[1], sign * cross * nu8 * f[0], 0.0]
                keep = row == (0 if sign < 0 else 7)
                if h == 0:
                    keep = keep & (lane_iota((8, 128)) >= KR)
                halos.append([jnp.where(keep, by_halo * f[c] + extra[c], 0.0) for c in range(3)])
            for c in range(3):
                face = pl.ds((c * 2 + h) * TH, TH)
                one, two = one_ref[face, :], two_ref[face, :]
                face = jnp.where(odd, one, two) if z == 0 else jnp.where(odd, two, one)
                rate = jnp.where(end, 0.0, face) * by_face
                if h == 0:
                    offset = (c % 2) * 64 + z * 32
                    ghost = POLE_SIGNS[c] * lanes(poles[c // 2], -offset)
                    rate = rate + jnp.where(lane < KR, lanes(filtered[c // 2], -offset), 0.0)
                    rate = rate + jnp.where(lane == 0, 0.5 * u[0] * ghost, 0.0)
                rates[c][z][h] = jnp.concatenate(
                    [rate[:8] + halos[0][c], rate[8 : TH - 8], rate[TH - 8 :] + halos[1][c]], axis=0
                )
    return rates


def viscosity_blocks(inp, out):
    nu_s = out.vmem("nu")
    nu_s[...] = inp("nu")[...].astype(f32)
    return [[nu_s[strided(0, z, h), :] for h in range(2)] for z in range(2)]


def magnetic_blocks(inp, out):
    mag_s = out.vmem("mag")
    mag_s[...] = inp("mag")[...].astype(f32)
    return [[[mag_s[strided(c, z, h), :] for h in range(2)] for z in range(2)] for c in range(3)]


def input_blocks(inp):
    vel_ref = inp("vel")
    return [[[vel_ref[strided(c, z, h), :] for h in range(2)] for z in range(2)] for c in range(3)]


def blocks(ref):
    return [[[ref[block(c, z, h), :] for h in range(2)] for z in range(2)] for c in range(3)]


def first_kernel(inp, out):
    me = lax.axis_index("az")
    slab = lax.axis_index("ax")
    live, row, col, velocity = arrivals(inp("edge"), inp("cnt"), me, slab)
    arrived = add_parts(deposit(row, col, velocity, SECT * CAP))
    sum_ref = inp("sums")
    total = [sum_ref[c * 256 : (c + 1) * 256, :] + arrived[c] for c in range(4)]
    nu, field = viscosity_blocks(inp, out), input_blocks(inp)
    rates = outer_rate(field, nu, inp, me, slab)
    local_ref = inp("local")
    mid_ref, rest_ref = out.vmem("mid"), out.vmem("rest")
    mid = [[[None, None], [None, None]] for _ in range(3)]
    for c in range(3):
        for z in range(2):
            for h in range(2):
                at = slice((z * 2 + h) * TH, (z * 2 + h + 1) * TH)
                x, s, n = field[c][z][h], total[c][at], total[3][at]
                u1 = x + DT * (local_ref[block(c, z, h), :] + rates[c][z][h] + 2.0 * (s - n * x))
                mid[c][z][h] = u1
                mid_ref[block(c, z, h), :] = u1
                rest_ref[block(c, z, h), :] = 0.5 * (x + u1) + DT * (0.8 * s + 0.2 * n * x - n * u1)
    inner_ref = out.vmem("inner")
    first, second = pack_inner(mid, [nu[z][0] for z in range(2)])
    inner_ref[0:TH, :] = first
    inner_ref[TH:, :] = jnp.where(
        lane_iota((TH // 2, 128)) < 64, second[: TH // 2], pltpu.roll(second[TH // 2 :], 64, 1)
    )
    send_inner(out, ROW_EDGE2)
    write_edges(out.vmem("edge"), mid, me)
    out.copy(out.vmem("edge"), out.hbm("msg").at[:, ROW_EDGE2:, :])
    write_axial(out.vmem("one"), out.vmem("two"), mid, slab)
    out.send("one")
    out.send("two")
    out.send("mid")
    out.send("rest")


def take(pick, row, col, n):
    got = jnp.dot(pick, one_hot(row, 256, n), preferred_element_type=f32)
    got = got[:384] + got[384:]
    cols = row_iota((128, n)) == col
    return [jnp.sum(jnp.where(cols, got[c * 128 : (c + 1) * 128], 0.0), axis=0, keepdims=True) for c in range(3)]


def gather_kernel(inp, out):
    me = lax.axis_index("az")
    slab = lax.axis_index("ax")
    pc_ref, stay_ref, pv_ref = inp("pc"), inp("stay"), inp("pv")
    kept_ref, arr_ref = out.vmem("kept"), out.vmem("arrived")
    vel_ref, mid_ref = inp("vel"), inp("mid")
    parts = []
    for c in range(3):
        rows = []
        for z in range(2):
            for h in range(2):
                rows.append(0.08 * vel_ref[strided(c, z, h), :] + 0.1 * mid_ref[block(c, z, h), :])
        parts.append(split2(jnp.concatenate(rows, axis=0).T))
    pick = jnp.concatenate([p[0] for p in parts] + [p[1] for p in parts], axis=0)
    for k in range(NP // CHUNK):
        part = pl.ds(k * CHUNK, CHUNK)
        row = local_row(pc_ref[0:1, part], pc_ref[1:2, part], pc_ref[2:3, part], me, slab)
        stay = stay_ref[0:1, part] > 0.5
        row = jnp.where(stay, row, -1)
        got = take(pick, row, pc_ref[1:2, part] % 128, CHUNK)
        for c in range(3):
            kept_ref[c : c + 1, part] = jnp.where(stay, 0.82 * pv_ref[c : c + 1, part] + got[c], 0.0)
    out.send("kept")
    rates = local_rate(blocks(mid_ref), viscosity_blocks(inp, out), magnetic_blocks(inp, out))
    rest_ref, part_ref = inp("rest"), out.vmem("part")
    for c in range(3):
        for z in range(2):
            for h in range(2):
                part_ref[block(c, z, h), :] = rest_ref[block(c, z, h), :] + (0.5 * DT) * rates[c][z][h]
    out.send("part")
    live, row, col, velocity = arrivals(inp("edge"), inp("cnt"), me, slab)
    got = take(pick, row, col, SECT * CAP)
    for c in range(3):
        arr_ref[c, 0:1, :] = jnp.where(live > 0, 0.82 * velocity[c] + got[c], 0.0)
    out.send("arrived")


def second_kernel(inp, out):
    me = lax.axis_index("az")
    slab = lax.axis_index("ax")
    rates = outer_rate(blocks(inp("mid")), viscosity_blocks(inp, out), inp, me, slab)
    part_ref, new_ref = inp("part"), out.vmem("new")
    for c in range(3):
        for z in range(2):
            for h in range(2):
                new_ref[strided(c, z, h), :] = part_ref[block(c, z, h), :] + (0.5 * DT) * rates[c][z][h]
    out.send("new")


def call(kernel, name, ins, outs, bufs, copies, flops=0, in_smem=()):
    in_names, out_names, buf_names = list(ins), list(outs), list(bufs)
    arrays = [ins[n] for n in in_names]
    n_in, n_out = len(in_names), len(out_names)

    def body(*refs):
        in_refs, refs = refs[:n_in], refs[n_in:]
        out_refs, refs = refs[:n_out], refs[n_out:]
        in_bufs, refs = refs[:n_in], refs[n_in:]
        buf_refs, (in_sems, out_sems) = refs[:-2], refs[-2:]
        out = Outputs(out_names, out_refs, dict(zip(buf_names, buf_refs)), out_sems)
        kernel(Inputs(in_names, in_refs, in_bufs, in_sems), out)
        out.finish()

    def in_shape(n):
        shape = ins[n].shape
        if n == "basis_t":
            return (2, TH, shape[2])
        if n not in ("inner", "edge", "inner_nu"):
            return shape
        part = message_rows(n, shape[1])
        return (SECT, part.stop - part.start, 128)

    hbm = pl.BlockSpec(memory_space=pltpu.HBM)
    return pl.pallas_call(
        body,
        out_shape=[jax.ShapeDtypeStruct(*outs[n]) for n in out_names],
        in_specs=[hbm] * n_in,
        out_specs=[hbm] * n_out,
        scratch_shapes=[(pltpu.SMEM if n in in_smem else pltpu.VMEM)(in_shape(n), ins[n].dtype) for n in in_names]
        + [pltpu.VMEM(*bufs[n]) for n in buf_names]
        + [pltpu.SemaphoreType.DMA((n_in,)), pltpu.SemaphoreType.DMA((copies,))],
        compiler_params=pltpu.CompilerParams(vmem_limit_bytes=VMEM_LIMIT),
        cost_estimate=pl.CostEstimate(flops=flops, bytes_accessed=2 * 1024 * 1024, transcendentals=0),
        name=name,
    )(*arrays)


def rows_of(x):
    lead = x.shape[:-2]
    x = x.reshape(*lead, 2, 2, 128)
    return jnp.swapaxes(x, -3, -2).reshape(-1, 128)


def per_device(velocity, viscosity, bfield, particle_velocity, particle_cell, send_rows, send_counts):
    ax = lax.axis_size("ax")
    vel, nu, mag = rows_of(velocity), rows_of(viscosity), rows_of(bfield)
    pv, pc = particle_velocity, particle_cell
    tables = {"basis": jnp.asarray(BASIS), "weight": jnp.asarray(MODE_WEIGHT), "basis_t": jnp.asarray(BASIS_T)}
    swap_one = [(i, i ^ 1) for i in range(ax)]
    swap_two = []
    for a in range(SECT):
        swap_two += [(a * ax + i, a * ax + ((i + 1) ^ 1) - 1) for i in range(1, ax - 1)]
        swap_two += [(a * ax + i, (a ^ 1) * ax + i) for i in (0, ax - 1)]

    def swap(one, two):
        return lax.ppermute(one, "ax", swap_one), lax.ppermute(two, ("az", "ax"), swap_two)

    def to_all(msg):
        return lax.all_to_all(msg, "az", split_axis=0, concat_axis=0, tiled=True)

    face = ((384, 128), f32)
    field = ((768, 128), f32)
    materials = {"nu": ((256, 128), f32), "mag": field}
    msg, one, two, stay = call(
        pack_kernel,
        "pack",
        {"vel": vel, "nu": nu, "pc": pc, "pv": pv, "rows": send_rows, "cnt": send_counts},
        {"msg": ((SECT, ROW_EDGE1 + EDGE1, 128), f32), "one": face, "two": face, "stay": ((1, NP), f32)},
        {
            "inner": ((ROW_EDGE1, 128), f32),
            "one": face,
            "two": face,
            "edge": ((SECT, EDGE1, 128), f32),
            "stay": ((1, NP), f32),
            "tmp": ((1024, 128), f32),
            "nu": ((256, 128), f32),
        },
        12,
        in_smem=("cnt",),
    )
    one, two = swap(one, two)
    recv = to_all(msg)
    sums, local = call(
        scatter_kernel,
        "deposit",
        {"pc": pc, "stay": stay, "pv": pv, "vel": vel, "nu": nu, "mag": mag},
        {"sums": ((1024, 128), f32), "local": field},
        {"sums": ((1024, 128), f32), "acc": ((256, 896), f32), "local": field} | materials,
        2,
        flops=2 * NP * 256 * 896,
    )
    msg2, one2, two2, mid, rest = call(
        first_kernel,
        "first_section",
        {"edge": recv, "inner": recv, "cnt": send_counts, "basis": tables["basis"], "sums": sums, "nu": nu, "vel": vel}
        | tables
        | {"one": one, "two": two, "local": local},
        {"msg": ((SECT, ROW_EDGE2 + EDGE2, 128), f32), "one": face, "two": face, "mid": field, "rest": field},
        {
            "inner": ((ROW_EDGE2, 128), f32),
            "edge": ((SECT, EDGE2, 128), f32),
            "one": face,
            "two": face,
            "mid": field,
            "rest": field,
            "nu": ((256, 128), f32),
        },
        13,
        in_smem=("cnt",),
    )
    one2, two2 = swap(one2, two2)
    recv2 = to_all(msg2)
    kept, arrived, part = call(
        gather_kernel,
        "take",
        {"vel": vel, "mid": mid, "pc": pc, "stay": stay, "pv": pv, "nu": nu, "mag": mag, "rest": rest}
        | {"edge": recv, "cnt": send_counts},
        {"kept": ((3, NP), f32), "arrived": ((3, 1, SECT * CAP), f32), "part": field},
        {"kept": ((3, NP), f32), "arrived": ((3, 1, SECT * CAP), f32), "part": field} | materials,
        3,
        flops=2 * NP * 512 * 384,
        in_smem=("cnt",),
    )
    (new,) = call(
        second_kernel,
        "second_section",
        {"inner": recv2, "inner_nu": recv} | tables | {"edge": recv2, "mid": mid, "nu": nu, "one": one2, "two": two2, "part": part},
        {"new": field},
        {"nu": ((256, 128), f32), "new": field},
        1,
    )
    new = jnp.swapaxes(new.reshape(3, TH, 2, 2, 128), 2, 3).reshape(3, TH, 2, NR)
    return new, kept, jnp.swapaxes(arrived, 0, 1)


def solution(mesh):
    return jax.shard_map(
        per_device,
        mesh=mesh,
        in_specs=(
            P(None, "az", "ax", None),
            P("az", "ax", None),
            P(None, "az", "ax", None),
            P(None, ("az", "ax")),
            P(None, ("az", "ax")),
            P(("az", "ax"), None, None),
            P(None, "ax", None),
        ),
        out_specs=(P(None, "az", "ax", None), P(None, ("az", "ax")), P(("az", "ax"), None, None)),
        check_vma=False,
    )
```

```python
import math

import jax
import jax.numpy as jnp
import numpy as np
from jax import lax
from jax.experimental import pallas as pl
from jax.experimental.pallas import tpu as pltpu
from jax.sharding import PartitionSpec as P

NA = 512
NR = 256
KR = 32
SECT = 8
TH = NA // SECT
CAP = 128
NP = 8192
DTHETA = 2.0 * math.pi / NA
DT = 0.02
POLE_SIGNS = (-1.0, -1.0, 1.0)
HIGHEST = lax.Precision.HIGHEST
f32 = jnp.float32
bf16 = jnp.bfloat16
i32 = jnp.int32
VMEM_LIMIT = 65408 * 1024

ROW_B = 64
ROW_EDGE1 = 128
ROW_EDGE2 = 96
EDGE_PART = 16
EDGE1 = 24
EDGE2 = 16
CHUNK = 1024


def filter_tables():
    a = np.arange(NA // 2)
    even, odd, even_mode, odd_mode = [], [], [], []
    for m in range(NA // 2 + 1):
        scale = math.sqrt((1.0 if m in (0, NA // 2) else 2.0) / NA)
        phase = 2.0 * math.pi * (m * a % NA) / NA
        rows = [scale * np.cos(phase)]
        if m not in (0, NA // 2):
            rows.append(scale * np.sin(phase))
        for row in rows:
            (odd if m % 2 else even).append(row)
            (odd_mode if m % 2 else even_mode).append(m)
    basis = np.stack([np.stack(even), np.stack(odd)]).astype(np.float32)
    modes = np.stack([np.array(even_mode), np.array(odd_mode)]).astype(np.float64)
    cutoff = 4.0 * (np.arange(KR) + 0.5)
    weight = 1.0 / (1.0 + (modes[:, :, None] / cutoff) ** 4)
    weight = np.tile(weight, (1, 1, 128 // KR)).astype(np.float32)
    return basis, np.ascontiguousarray(basis.transpose(0, 2, 1)), weight


BASIS, BASIS_T, MODE_WEIGHT = filter_tables()


def lane_iota(shape):
    return lax.broadcasted_iota(i32, shape, len(shape) - 1)


def row_iota(shape):
    return lax.broadcasted_iota(i32, shape, len(shape) - 2)


def strided(c, z, h):
    return pl.ds(c * 256 + h * 2 + z, TH, stride=4)


def block(c, z, h):
    return pl.ds(((c * 2 + z) * 2 + h) * TH, TH)


def lanes(x, by):
    by %= 128
    return x if by == 0 else pltpu.roll(x, by, 1)


def split2(x):
    hi = x.astype(bf16)
    return hi, (x - hi.astype(f32)).astype(bf16)


def pack_inner(field, nu):
    lane = lane_iota((TH, 128))

    def four(p, q, r, s):
        low = jnp.where(lane < 32, p, lanes(q, 32))
        high = jnp.where(lane < 96, lanes(r, 64), lanes(s, 96))
        return jnp.where(lane < 64, low, high)

    first = four(field[0][0][0], field[0][1][0], field[1][0][0], field[1][1][0])
    second = four(field[2][0][0], field[2][1][0], nu[0], nu[1])
    return first, second


def write_edges(edge_ref, field, me):
    up = (me + 1) % SECT
    for c in range(3):
        for z in range(2):
            for h in range(2):
                x = field[c][z][h]
                row = (c * 2 + z) * 2 + h
                for t in range(SECT):
                    edge_ref[t, row : row + 1, :] = jnp.where(t == up, x[TH - 1 : TH], x[0:1])


def send_inner(out, rows):
    for t in range(SECT):
        out.copy(out.vmem("inner"), out.hbm("msg").at[t, 0:rows, :])


def write_axial(one_ref, two_ref, field, slab):
    odd = slab % 2 == 1
    for c in range(3):
        for h in range(2):
            rows = pl.ds((c * 2 + h) * TH, TH)
            low, high = field[c][0][h], field[c][1][h]
            one_ref[rows, :] = jnp.where(odd, low, high)
            two_ref[rows, :] = jnp.where(odd, high, low)


def message_rows(name, rows):
    edge = ROW_EDGE1 if rows == ROW_EDGE1 + EDGE1 else ROW_EDGE2
    return {"inner": slice(0, edge), "edge": slice(edge, rows), "inner_nu": slice(ROW_B, edge)}[name]


class Inputs:
    def __init__(self, names, refs, bufs, sems):
        self.refs = dict(zip(names, bufs))
        self.copies = {}
        for i, (name, ref, buf) in enumerate(zip(names, refs, bufs)):
            if name in ("inner", "edge", "inner_nu"):
                ref = ref.at[:, message_rows(name, ref.shape[1]), :]
            if name == "basis_t":
                own = lax.axis_index("az") % 4
                ref = ref.at[:, pl.ds(pl.multiple_of(own * TH, TH), TH), :]
            self.copies[name] = [pltpu.make_async_copy(ref, buf, sems.at[i])]
            self.copies[name][0].start()

    def __call__(self, name):
        for copy in self.copies.pop(name, ()):
            copy.wait()
        return self.refs[name]


class Outputs:
    def __init__(self, names, refs, bufs, sems):
        self.refs, self.bufs, self.sems, self.started = dict(zip(names, refs)), bufs, sems, []

    def hbm(self, name):
        return self.refs[name]

    def vmem(self, name):
        return self.bufs[name]

    def copy(self, src, dst):
        copy = pltpu.make_async_copy(src, dst, self.sems.at[len(self.started)])
        copy.start()
        self.started.append(copy)

    def send(self, name):
        self.copy(self.bufs[name], self.refs[name])

    def finish(self):
        for copy in self.started:
            copy.wait()


def pack_kernel(inp, out):
    me = lax.axis_index("az")
    tmp_ref, nu_s, edge_ref, stay_ref = out.vmem("tmp"), out.vmem("nu"), out.vmem("edge"), out.vmem("stay")
    vel_ref, nu_ref = inp("vel"), inp("nu")
    field = [[[vel_ref[strided(c, z, h), :] for h in range(2)] for z in range(2)] for c in range(3)]
    nu_s[...] = nu_ref[...].astype(f32)
    nu = [nu_s[pl.ds(z, TH, stride=4), :] for z in range(2)]
    inner_ref = out.vmem("inner")
    inner_ref[0:TH, :], inner_ref[TH:, :] = pack_inner(field, nu)
    send_inner(out, ROW_EDGE1)
    write_axial(out.vmem("one"), out.vmem("two"), field, lax.axis_index("ax"))
    out.send("one")
    out.send("two")
    write_edges(edge_ref, field, me)
    pv_ref, pc_ref = inp("pv"), inp("pc")
    for i in range(64):
        tmp_ref[i * 8 : i * 8 + 3, :] = pv_ref[:, i * 128 : (i + 1) * 128]
        tmp_ref[512 + i * 8 : 512 + i * 8 + 3, :] = pc_ref[:, i * 128 : (i + 1) * 128].astype(f32)
    parts = []
    for k in range(2):
        for c in range(3):
            parts.append(jnp.concatenate(split2(tmp_ref[pl.ds(k * 512 + c, 64, stride=8), :]), axis=1))
    rows_ref, cnt_ref = inp("rows"), inp("cnt")
    lane = lane_iota((1, 128))
    listed = [rows_ref[0, t : t + 1, :] for t in range(SECT)]
    low = jnp.concatenate([one_hot(row % 128, 128, 128) for row in listed], axis=1)
    high = [row_iota((64, 128)) == row // 128 for row in listed]
    used_high = []
    for t in range(SECT):
        used = (high[t] & (lane < cnt_ref[me, 0, t])).astype(f32)
        used_high.append(used.astype(bf16))
    picked = jnp.dot(
        jnp.concatenate(parts, axis=0), jnp.concatenate([low, low], axis=0), preferred_element_type=f32
    )
    for t in range(SECT):
        for q in range(6):
            value = picked[q * 64 : (q + 1) * 64, t * 128 : (t + 1) * 128]
            edge_ref[t, EDGE_PART + q : EDGE_PART + q + 1, :] = jnp.sum(
                jnp.where(high[t], value, 0.0), axis=0, keepdims=True
            )
    out.copy(edge_ref, out.hbm("msg").at[:, ROW_EDGE1:, :])
    leaving = lax.dot_general(
        jnp.concatenate(used_high, axis=1), low, (((1,), (1,)), ((), ())), preferred_element_type=f32
    )
    stay = 1.0 - leaving
    for i in range(64):
        stay_ref[0:1, i * 128 : (i + 1) * 128] = stay[i : i + 1, :]
    out.send("stay")


def local_row(theta, r, z, me, slab):
    return ((z - 2 * slab) * 2 + r // 128) * TH + theta - me * TH


def spread(x, rows, n):
    tile = jnp.broadcast_to(x, (16, n)).astype(bf16)
    return jnp.concatenate([tile] * (rows // 16), axis=0)


def matches(index, rows, n):
    return row_iota((rows, n)).astype(f32).astype(bf16) == spread(index.astype(f32), rows, n)


def one_hot(index, rows, n):
    return jnp.where(matches(index, rows, n), jnp.ones((), bf16), jnp.zeros((), bf16))


def deposit(row, col, velocity, n):
    cols = matches(col, 128, n)
    pieces = []
    for c in range(3):
        for part in split2(velocity[c]):
            pieces.append(jnp.where(cols, spread(part.astype(f32), 128, n), jnp.zeros((), bf16)))
    pieces.append(one_hot(col, 128, n))
    return lax.dot_general(
        one_hot(row, 256, n), jnp.concatenate(pieces, axis=0), (((1,), (1,)), ((), ())), preferred_element_type=f32
    )


def add_parts(acc):
    out = [acc[:, c * 256 : c * 256 + 128] + acc[:, c * 256 + 128 : c * 256 + 256] for c in range(3)]
    out.append(acc[:, 768:896])
    return out


def write_blocks(ref, x):
    for c in range(3):
        for z in range(2):
            for h in range(2):
                ref[block(c, z, h), :] = x[c][z][h]


def scatter_kernel(inp, out):
    me = lax.axis_index("az")
    slab = lax.axis_index("ax")
    pc_ref, stay_ref, pv_ref = inp("pc"), inp("stay"), inp("pv")
    sum_ref, acc_ref = out.vmem("sums"), out.vmem("acc")
    for k in range(NP // CHUNK):
        part = pl.ds(k * CHUNK, CHUNK)
        row = local_row(pc_ref[0:1, part], pc_ref[1:2, part], pc_ref[2:3, part], me, slab)
        row = jnp.where(stay_ref[0:1, part] > 0.5, row, -1)
        col = pc_ref[1:2, part] % 128
        more = deposit(row, col, [pv_ref[c : c + 1, part] for c in range(3)], CHUNK)
        if k == 0:
            acc_ref[...] = more
        else:
            acc_ref[...] += more
    for c, x in enumerate(add_parts(acc_ref)):
        sum_ref[c * 256 : (c + 1) * 256, :] = x
    out.send("sums")
    rates = local_rate(input_blocks(inp), viscosity_blocks(inp, out), magnetic_blocks(inp, out))
    write_blocks(out.vmem("local"), rates)
    out.send("local")


def arrivals(edge_ref, cnt_ref, me, slab):
    lane = lane_iota((1, CAP))
    live = jnp.concatenate([(lane < cnt_ref[s, 0, me]).astype(i32) for s in range(SECT)], axis=1)

    def channel(q):
        return jnp.concatenate([edge_ref[s, EDGE_PART + q : EDGE_PART + q + 1, :] for s in range(SECT)], axis=1)

    velocity = [channel(c) for c in range(3)]
    theta, r, z = [channel(3 + c).astype(i32) for c in range(3)]
    row = jnp.where(live > 0, local_row(theta, r, z, me, slab), -1)
    return live, row, r % 128, velocity


def inner_fields(inp):
    recv_ref = inp("inner")
    first = recv_ref[:, 0:TH, :].reshape(NA, 128)
    if recv_ref.shape[1] == ROW_EDGE1:
        return first, recv_ref[:, ROW_B : ROW_B + TH, :].reshape(NA, 128)
    halves = []
    for t in range(SECT):
        x = recv_ref[t, ROW_B : ROW_B + TH // 2, :]
        halves += [x, pltpu.roll(x, 64, 1)]
    second = jnp.concatenate(halves, axis=0)
    return first, jnp.where(lane_iota((NA, 128)) < 64, second, inp("inner_nu")[...].reshape(NA, 128))


def filtered_inner(inp, me):
    first, second = inner_fields(inp)
    lane = lane_iota((1, 128))
    radius = (lane % KR).astype(f32) + 0.5
    left = lane < 64
    first_swap = pltpu.roll(first, 64, 1)
    second_swap = pltpu.roll(second, 64, 1)
    nu = jnp.where(left, second_swap, second)
    swirl = jnp.where(left, first_swap, first)

    def differences(x):
        after = pltpu.roll(x, NA - 1, 0)
        before = pltpu.roll(x, 1, 0)
        lap = (after - 2.0 * x + before) * (1.0 / (radius * radius * (DTHETA * DTHETA)))
        return lap, (after - before) * (1.0 / (2.0 * DTHETA * radius))

    lap, grad = differences(first)
    cross = jnp.where(left, -2.0, 2.0) / radius
    part_first = nu * lap - swirl * grad + cross * nu * pltpu.roll(grad, 64, 1)
    lap, grad = differences(second)
    part_second = jnp.where(left, nu * lap - swirl * grad, 0.0)
    part = jnp.concatenate([part_first, part_second], axis=1)
    low, high = part[: NA // 2], part[NA // 2 :]
    basis_ref, weight_ref, basis_t_ref = inp("basis"), inp("weight"), inp("basis_t")
    out = 0.0
    for parity, x in enumerate((low + high, low - high)):
        spectrum = jnp.dot(basis_ref[parity], x, precision=HIGHEST, preferred_element_type=f32)
        weight = weight_ref[parity]
        spectrum = spectrum * jnp.concatenate([weight, weight], axis=1)
        back = jnp.dot(basis_t_ref[parity], spectrum, precision=HIGHEST, preferred_element_type=f32)
        if parity:
            back = jnp.where(me < 4, back, -back)
        out = out + back
    return out[:, :128], out[:, 128:]


def local_rate(field, nu, magnetic):
    lane = lane_iota((TH, 128))
    row = row_iota((TH, 128))
    rates = [[[None, None], [None, None]] for _ in range(3)]
    for z in range(2):
        rolled = [[(pltpu.roll(field[c][z][h], 1, 1), pltpu.roll(field[c][z][h], 127, 1)) for h in range(2)] for c in range(3)]
        for h in range(2):
            radius = lane_iota((1, 128)).astype(f32) + (h * 128 + 0.5)
            inverse = 1.0 / radius
            eddy = nu[z][h]
            u = [field[c][z][h] for c in range(3)]
            lap_ax, lap_rad, grad_rad, grad_ax, lap_th, grad_th = [], [], [], [], [], []
            for c in range(3):
                x = u[c]
                if h == 0:
                    prev_r = jnp.where(lane == 0, 0.0, rolled[c][0][0])
                    next_r = jnp.where(lane == 127, rolled[c][1][1], rolled[c][0][1])
                else:
                    prev_r = jnp.where(lane == 0, rolled[c][0][0], rolled[c][1][0])
                    next_r = jnp.where(lane == 127, 0.0, rolled[c][1][1])
                other = field[c][1 - z][h]
                prev_t = jnp.where(row == 0, 0.0, pltpu.roll(x, 1, 0))
                next_t = jnp.where(row == TH - 1, 0.0, pltpu.roll(x, TH - 1, 0))
                lap_rad.append(((radius + 0.5) * (next_r - x) - (radius - 0.5) * (x - prev_r)) * inverse)
                lap_ax.append(other - 2.0 * x)
                grad_rad.append(0.5 * (next_r - prev_r))
                grad_ax.append((0.5 if z == 0 else -0.5) * other)
                lap_th.append((next_t - 2.0 * x + prev_t) * (1.0 / (radius * radius * (DTHETA * DTHETA))))
                grad_th.append((next_t - prev_t) * (1.0 / (2.0 * DTHETA * radius)))
            b = [magnetic[c][z][h] for c in range(3)]
            slip = [-u[0], radius * (2.0 / NR) - u[1], -u[2]]
            current = [slip[1] * b[2] - slip[2] * b[1], slip[2] * b[0] - slip[0] * b[2], slip[0] * b[1] - slip[1] * b[0]]
            force = [
                current[1] * b[2] - current[2] * b[1],
                current[2] * b[0] - current[0] * b[2],
                current[0] * b[1] - current[1] * b[0],
            ]
            inverse2 = inverse * inverse
            metric = [
                u[1] * u[1] * inverse - eddy * u[0] * inverse2,
                -eddy * u[1] * inverse2 - u[0] * u[1] * inverse,
                0.0,
            ]
            coupling = [-2.0 * eddy * grad_th[1] * inverse, 2.0 * eddy * grad_th[0] * inverse, 0.0]
            for c in range(3):
                azimuth = eddy * lap_th[c] - u[1] * grad_th[c] + coupling[c]
                if h == 0:
                    azimuth = jnp.where(lane < KR, 0.0, azimuth)
                rates[c][z][h] = (
                    eddy * (lap_rad[c] + lap_ax[c])
                    - (u[0] * grad_rad[c] + u[2] * grad_ax[c])
                    + metric[c]
                    + 0.5 * force[c]
                    + azimuth
                )
    return rates


def outer_rate(field, nu, inp, me, slab):
    filtered = filtered_inner(inp, me)
    recv_ref, edge_ref, one_ref, two_ref = inp("inner"), inp("edge"), inp("one"), inp("two")
    before_sector = (me + SECT - 1) % SECT
    after_sector = (me + 1) % SECT
    opposite = (me + SECT // 2) % SECT
    odd = slab % 2 == 1
    lane = lane_iota((TH, 128))
    row = row_iota((8, 128))
    poles = [recv_ref[opposite, 0:TH, :]]
    if recv_ref.shape[1] == ROW_EDGE1:
        poles.append(recv_ref[opposite, ROW_B : ROW_B + TH, :])
    else:
        pole = recv_ref[opposite, ROW_B : ROW_B + TH // 2, :]
        poles.append(jnp.concatenate([pole, pltpu.roll(pole, 64, 1)], axis=0))
    rates = [[[None, None], [None, None]] for _ in range(3)]
    for z in range(2):
        for h in range(2):
            radius = lane_iota((1, 128)).astype(f32) + (h * 128 + 0.5)
            lap_factor = 1.0 / (radius * radius * (DTHETA * DTHETA))
            grad_factor = 1.0 / (2.0 * DTHETA * radius)
            cross = 2.0 * grad_factor / radius
            eddy, u = nu[z][h], [field[c][z][h] for c in range(3)]
            by_face = eddy + (0.5 if z == 0 else -0.5) * u[2]
            end = slab == (0 if z == 0 else lax.axis_size("ax") - 1)
            halos = []
            for sector, at, sign in ((before_sector, slice(0, 8), -1.0), (after_sector, slice(TH - 8, TH), 1.0)):
                f = [edge_ref[sector, (c * 2 + z) * 2 + h : (c * 2 + z) * 2 + h + 1, :] for c in range(3)]
                nu8, swirl8 = eddy[at], u[1][at]
                by_halo = nu8 * lap_factor - sign * swirl8 * grad_factor
                extra = [-sign * cross * nu8 * f[1], sign * cross * nu8 * f[0], 0.0]
                keep = row == (0 if sign < 0 else 7)
                if h == 0:
                    keep = keep & (lane_iota((8, 128)) >= KR)
                halos.append([jnp.where(keep, by_halo * f[c] + extra[c], 0.0) for c in range(3)])
            for c in range(3):
                face = pl.ds((c * 2 + h) * TH, TH)
                one, two = one_ref[face, :], two_ref[face, :]
                face = jnp.where(odd, one, two) if z == 0 else jnp.where(odd, two, one)
                rate = jnp.where(end, 0.0, face) * by_face
                if h == 0:
                    offset = (c % 2) * 64 + z * 32
                    ghost = POLE_SIGNS[c] * lanes(poles[c // 2], -offset)
                    rate = rate + jnp.where(lane < KR, lanes(filtered[c // 2], -offset), 0.0)
                    rate = rate + jnp.where(lane == 0, 0.5 * u[0] * ghost, 0.0)
                rates[c][z][h] = jnp.concatenate(
                    [rate[:8] + halos[0][c], rate[8 : TH - 8], rate[TH - 8 :] + halos[1][c]], axis=0
                )
    return rates


def viscosity_blocks(inp, out):
    nu_s = out.vmem("nu")
    nu_s[...] = inp("nu")[...].astype(f32)
    return [[nu_s[strided(0, z, h), :] for h in range(2)] for z in range(2)]


def magnetic_blocks(inp, out):
    mag_s = out.vmem("mag")
    mag_s[...] = inp("mag")[...].astype(f32)
    return [[[mag_s[strided(c, z, h), :] for h in range(2)] for z in range(2)] for c in range(3)]


def input_blocks(inp):
    vel_ref = inp("vel")
    return [[[vel_ref[strided(c, z, h), :] for h in range(2)] for z in range(2)] for c in range(3)]


def blocks(ref):
    return [[[ref[block(c, z, h), :] for h in range(2)] for z in range(2)] for c in range(3)]


def first_kernel(inp, out):
    me = lax.axis_index("az")
    slab = lax.axis_index("ax")
    live, row, col, velocity = arrivals(inp("edge"), inp("cnt"), me, slab)
    arrived = add_parts(deposit(row, col, velocity, SECT * CAP))
    sum_ref = inp("sums")
    total = [sum_ref[c * 256 : (c + 1) * 256, :] + arrived[c] for c in range(4)]
    nu, field = viscosity_blocks(inp, out), input_blocks(inp)
    rates = outer_rate(field, nu, inp, me, slab)
    local_ref = inp("local")
    mid_ref, rest_ref = out.vmem("mid"), out.vmem("rest")
    mid = [[[None, None], [None, None]] for _ in range(3)]
    for c in range(3):
        for z in range(2):
            for h in range(2):
                at = slice((z * 2 + h) * TH, (z * 2 + h + 1) * TH)
                x, s, n = field[c][z][h], total[c][at], total[3][at]
                u1 = x + DT * (local_ref[block(c, z, h), :] + rates[c][z][h] + 2.0 * (s - n * x))
                mid[c][z][h] = u1
                mid_ref[block(c, z, h), :] = u1
                rest_ref[block(c, z, h), :] = 0.5 * (x + u1) + DT * (0.8 * s + 0.2 * n * x - n * u1)
    inner_ref = out.vmem("inner")
    first, second = pack_inner(mid, [nu[z][0] for z in range(2)])
    inner_ref[0:TH, :] = first
    inner_ref[TH:, :] = jnp.where(
        lane_iota((TH // 2, 128)) < 64, second[: TH // 2], pltpu.roll(second[TH // 2 :], 64, 1)
    )
    send_inner(out, ROW_EDGE2)
    write_edges(out.vmem("edge"), mid, me)
    out.copy(out.vmem("edge"), out.hbm("msg").at[:, ROW_EDGE2:, :])
    write_axial(out.vmem("one"), out.vmem("two"), mid, slab)
    out.send("one")
    out.send("two")
    out.send("mid")
    out.send("rest")


def take(pick, row, col, n):
    got = jnp.dot(pick, one_hot(row, 256, n), preferred_element_type=f32)
    got = got[:384] + got[384:]
    cols = row_iota((128, n)) == col
    return [jnp.sum(jnp.where(cols, got[c * 128 : (c + 1) * 128], 0.0), axis=0, keepdims=True) for c in range(3)]


def gather_kernel(inp, out):
    me = lax.axis_index("az")
    slab = lax.axis_index("ax")
    pc_ref, stay_ref, pv_ref = inp("pc"), inp("stay"), inp("pv")
    kept_ref, arr_ref = out.vmem("kept"), out.vmem("arrived")
    vel_ref, mid_ref = inp("vel"), inp("mid")
    parts = []
    for c in range(3):
        rows = []
        for z in range(2):
            for h in range(2):
                rows.append(0.08 * vel_ref[strided(c, z, h), :] + 0.1 * mid_ref[block(c, z, h), :])
        parts.append(split2(jnp.concatenate(rows, axis=0).T))
    pick = jnp.concatenate([p[0] for p in parts] + [p[1] for p in parts], axis=0)
    for k in range(NP // CHUNK):
        part = pl.ds(k * CHUNK, CHUNK)
        row = local_row(pc_ref[0:1, part], pc_ref[1:2, part], pc_ref[2:3, part], me, slab)
        stay = stay_ref[0:1, part] > 0.5
        row = jnp.where(stay, row, -1)
        got = take(pick, row, pc_ref[1:2, part] % 128, CHUNK)
        for c in range(3):
            kept_ref[c : c + 1, part] = jnp.where(stay, 0.82 * pv_ref[c : c + 1, part] + got[c], 0.0)
    out.send("kept")
    rates = local_rate(blocks(mid_ref), viscosity_blocks(inp, out), magnetic_blocks(inp, out))
    rest_ref, part_ref = inp("rest"), out.vmem("part")
    for c in range(3):
        for z in range(2):
            for h in range(2):
                part_ref[block(c, z, h), :] = rest_ref[block(c, z, h), :] + (0.5 * DT) * rates[c][z][h]
    out.send("part")
    live, row, col, velocity = arrivals(inp("edge"), inp("cnt"), me, slab)
    got = take(pick, row, col, SECT * CAP)
    for c in range(3):
        arr_ref[c, 0:1, :] = jnp.where(live > 0, 0.82 * velocity[c] + got[c], 0.0)
    out.send("arrived")


def second_kernel(inp, out):
    me = lax.axis_index("az")
    slab = lax.axis_index("ax")
    rates = outer_rate(blocks(inp("mid")), viscosity_blocks(inp, out), inp, me, slab)
    part_ref, new_ref = inp("part"), out.vmem("new")
    for c in range(3):
        for z in range(2):
            for h in range(2):
                new_ref[strided(c, z, h), :] = part_ref[block(c, z, h), :] + (0.5 * DT) * rates[c][z][h]
        rows = pl.ds(c * 256, 256)
        out.copy(new_ref.at[rows, :], out.hbm("new").at[rows, :])


def call(kernel, name, ins, outs, bufs, copies, flops=0, in_smem=()):
    in_names, out_names, buf_names = list(ins), list(outs), list(bufs)
    arrays = [ins[n] for n in in_names]
    n_in, n_out = len(in_names), len(out_names)

    def body(*refs):
        in_refs, refs = refs[:n_in], refs[n_in:]
        out_refs, refs = refs[:n_out], refs[n_out:]
        in_bufs, refs = refs[:n_in], refs[n_in:]
        buf_refs, (in_sems, out_sems) = refs[:-2], refs[-2:]
        out = Outputs(out_names, out_refs, dict(zip(buf_names, buf_refs)), out_sems)
        kernel(Inputs(in_names, in_refs, in_bufs, in_sems), out)
        out.finish()

    def in_shape(n):
        shape = ins[n].shape
        if n == "basis_t":
            return (2, TH, shape[2])
        if n not in ("inner", "edge", "inner_nu"):
            return shape
        part = message_rows(n, shape[1])
        return (SECT, part.stop - part.start, 128)

    hbm = pl.BlockSpec(memory_space=pltpu.HBM)
    return pl.pallas_call(
        body,
        out_shape=[jax.ShapeDtypeStruct(*outs[n]) for n in out_names],
        in_specs=[hbm] * n_in,
        out_specs=[hbm] * n_out,
        scratch_shapes=[(pltpu.SMEM if n in in_smem else pltpu.VMEM)(in_shape(n), ins[n].dtype) for n in in_names]
        + [pltpu.VMEM(*bufs[n]) for n in buf_names]
        + [pltpu.SemaphoreType.DMA((n_in,)), pltpu.SemaphoreType.DMA((copies,))],
        compiler_params=pltpu.CompilerParams(vmem_limit_bytes=VMEM_LIMIT),
        cost_estimate=pl.CostEstimate(flops=flops, bytes_accessed=2 * 1024 * 1024, transcendentals=0),
        name=name,
    )(*arrays)


def rows_of(x):
    lead = x.shape[:-2]
    x = x.reshape(*lead, 2, 2, 128)
    return jnp.swapaxes(x, -3, -2).reshape(-1, 128)


def per_device(velocity, viscosity, bfield, particle_velocity, particle_cell, send_rows, send_counts):
    ax = lax.axis_size("ax")
    vel, nu, mag = rows_of(velocity), rows_of(viscosity), rows_of(bfield)
    pv, pc = particle_velocity, particle_cell
    tables = {"basis": jnp.asarray(BASIS), "weight": jnp.asarray(MODE_WEIGHT), "basis_t": jnp.asarray(BASIS_T)}
    swap_one = [(i, i ^ 1) for i in range(ax)]
    swap_two = []
    for a in range(SECT):
        swap_two += [(a * ax + i, a * ax + ((i + 1) ^ 1) - 1) for i in range(1, ax - 1)]
        swap_two += [(a * ax + i, (a ^ 2) * ax + i) for i in (0, ax - 1)]

    def swap(one, two):
        return lax.ppermute(one, "ax", swap_one), lax.ppermute(two, ("az", "ax"), swap_two)

    def to_all(msg):
        return lax.all_to_all(msg, "az", split_axis=0, concat_axis=0, tiled=True)

    face = ((384, 128), f32)
    field = ((768, 128), f32)
    materials = {"nu": ((256, 128), f32), "mag": field}
    msg, one, two, stay = call(
        pack_kernel,
        "pack",
        {"vel": vel, "nu": nu, "pc": pc, "pv": pv, "rows": send_rows, "cnt": send_counts},
        {"msg": ((SECT, ROW_EDGE1 + EDGE1, 128), f32), "one": face, "two": face, "stay": ((1, NP), f32)},
        {
            "inner": ((ROW_EDGE1, 128), f32),
            "one": face,
            "two": face,
            "edge": ((SECT, EDGE1, 128), f32),
            "stay": ((1, NP), f32),
            "tmp": ((1024, 128), f32),
            "nu": ((256, 128), f32),
        },
        12,
        in_smem=("cnt",),
    )
    one, two = swap(one, two)
    recv = to_all(msg)
    sums, local = call(
        scatter_kernel,
        "deposit",
        {"pc": pc, "stay": stay, "pv": pv, "vel": vel, "nu": nu, "mag": mag},
        {"sums": ((1024, 128), f32), "local": field},
        {"sums": ((1024, 128), f32), "acc": ((256, 896), f32), "local": field} | materials,
        2,
        flops=2 * NP * 256 * 896,
    )
    msg2, one2, two2, mid, rest = call(
        first_kernel,
        "first_section",
        {"edge": recv, "inner": recv, "cnt": send_counts, "basis": tables["basis"], "sums": sums, "nu": nu, "vel": vel}
        | tables
        | {"one": one, "two": two, "local": local},
        {"msg": ((SECT, ROW_EDGE2 + EDGE2, 128), f32), "one": face, "two": face, "mid": field, "rest": field},
        {
            "inner": ((ROW_EDGE2, 128), f32),
            "edge": ((SECT, EDGE2, 128), f32),
            "one": face,
            "two": face,
            "mid": field,
            "rest": field,
            "nu": ((256, 128), f32),
        },
        13,
        in_smem=("cnt",),
    )
    one2, two2 = swap(one2, two2)
    recv2 = to_all(msg2)
    kept, arrived, part = call(
        gather_kernel,
        "take",
        {"vel": vel, "mid": mid, "pc": pc, "stay": stay, "pv": pv, "nu": nu, "mag": mag, "rest": rest}
        | {"edge": recv, "cnt": send_counts},
        {"kept": ((3, NP), f32), "arrived": ((3, 1, SECT * CAP), f32), "part": field},
        {"kept": ((3, NP), f32), "arrived": ((3, 1, SECT * CAP), f32), "part": field} | materials,
        3,
        flops=2 * NP * 512 * 384,
        in_smem=("cnt",),
    )
    (new,) = call(
        second_kernel,
        "second_section",
        {"inner": recv2, "inner_nu": recv} | tables | {"edge": recv2, "mid": mid, "nu": nu, "one": one2, "two": two2, "part": part},
        {"new": field},
        {"nu": ((256, 128), f32), "new": field},
        3,
    )
    new = jnp.swapaxes(new.reshape(3, TH, 2, 2, 128), 2, 3).reshape(3, TH, 2, NR)
    return new, kept, jnp.swapaxes(arrived, 0, 1)


def solution(mesh):
    return jax.shard_map(
        per_device,
        mesh=mesh,
        in_specs=(
            P(None, "az", "ax", None),
            P("az", "ax", None),
            P(None, "az", "ax", None),
            P(None, ("az", "ax")),
            P(None, ("az", "ax")),
            P(("az", "ax"), None, None),
            P(None, "ax", None),
        ),
        out_specs=(P(None, "az", "ax", None), P(None, ("az", "ax")), P(("az", "ax"), None, None)),
        check_vma=False,
    )
```

```python
import math

import jax
import jax.numpy as jnp
import numpy as np
from jax import lax
from jax.experimental import pallas as pl
from jax.experimental.pallas import tpu as pltpu
from jax.sharding import PartitionSpec as P

NA = 512
NR = 256
KR = 32
SECT = 8
TH = NA // SECT
CAP = 128
NP = 8192
DTHETA = 2.0 * math.pi / NA
DT = 0.02
POLE_SIGNS = (-1.0, -1.0, 1.0)
HIGHEST = lax.Precision.HIGHEST
f32 = jnp.float32
bf16 = jnp.bfloat16
i32 = jnp.int32
VMEM_LIMIT = 65408 * 1024

ROW_B = 64
ROW_EDGE = 96
EDGE_BOUND = 12
EDGE_PART = 16
EDGE1 = 24
EDGE2 = 16
CHUNK = 1024


def filter_tables():
    a = np.arange(NA // 2)
    even, odd, even_mode, odd_mode = [], [], [], []
    for m in range(NA // 2 + 1):
        scale = math.sqrt((1.0 if m in (0, NA // 2) else 2.0) / NA)
        phase = 2.0 * math.pi * (m * a % NA) / NA
        rows = [scale * np.cos(phase)]
        if m not in (0, NA // 2):
            rows.append(scale * np.sin(phase))
        for row in rows:
            (odd if m % 2 else even).append(row)
            (odd_mode if m % 2 else even_mode).append(m)
    basis = np.stack([np.stack(even), np.stack(odd)]).astype(np.float32)
    modes = np.stack([np.array(even_mode), np.array(odd_mode)]).astype(np.float64)
    cutoff = 4.0 * (np.arange(KR) + 0.5)
    weight = 1.0 / (1.0 + (modes[:, :, None] / cutoff) ** 4)
    weight = np.tile(weight, (1, 1, 128 // KR)).astype(np.float32)
    return basis, np.ascontiguousarray(basis.transpose(0, 2, 1)), weight


BASIS, BASIS_T, MODE_WEIGHT = filter_tables()


def lane_iota(shape):
    return lax.broadcasted_iota(i32, shape, len(shape) - 1)


def row_iota(shape):
    return lax.broadcasted_iota(i32, shape, len(shape) - 2)


def strided(c, z, h):
    return pl.ds(c * 256 + h * 2 + z, TH, stride=4)


def block(c, z, h):
    return pl.ds(((c * 2 + z) * 2 + h) * TH, TH)


def lanes(x, by):
    by %= 128
    return x if by == 0 else pltpu.roll(x, by, 1)


def split2(x):
    hi = x.astype(bf16)
    return hi, (x - hi.astype(f32)).astype(bf16)


def pack_inner(field, nu):
    lane = lane_iota((TH, 128))

    def four(p, q, r, s):
        low = jnp.where(lane < 32, p, lanes(q, 32))
        high = jnp.where(lane < 96, lanes(r, 64), lanes(s, 96))
        return jnp.where(lane < 64, low, high)

    first = four(field[0][0][0], field[0][1][0], field[1][0][0], field[1][1][0])
    second = four(field[2][0][0], field[2][1][0], nu[0], nu[1])
    return first, second


def azimuth_factors():
    lane = lane_iota((1, 128))
    radius = (lane % KR).astype(f32) + 0.5
    lap = 1.0 / (radius * radius * (DTHETA * DTHETA))
    grad = 1.0 / (2.0 * DTHETA * radius)
    return lane < 64, lap, grad, jnp.where(lane < 64, -2.0, 2.0) / radius


def both_halves(x, left):
    side = lane_iota((1, 128)) < 64
    return jnp.where(side == left, x, pltpu.roll(x, 64, 1))


def azimuth_inner(first, second):
    left, lap_factor, grad_factor, cross = azimuth_factors()
    row = row_iota((TH, 128))
    nu, swirl = both_halves(second, False), both_halves(first, False)

    def differences(x):
        after = jnp.where(row == TH - 1, 0.0, pltpu.roll(x, TH - 1, 0))
        before = jnp.where(row == 0, 0.0, pltpu.roll(x, 1, 0))
        return (after - 2.0 * x + before) * lap_factor, (after - before) * grad_factor

    lap, grad = differences(first)
    part_first = nu * lap - swirl * grad + cross * nu * pltpu.roll(grad, 64, 1)
    lap, grad = differences(second)
    return part_first, jnp.where(left, nu * lap - swirl * grad, 0.0)


def write_message(inner_ref, edge_ref, field, nu, me):
    first, second = pack_inner(field, nu)
    part_first, part_second = azimuth_inner(first, second)
    inner_ref[0:TH, :] = part_first
    inner_ref[TH:, :] = part_second[: TH // 2] + pltpu.roll(part_second[TH // 2 :], 64, 1)
    turned = jnp.concatenate([first, second], axis=0).T
    up, opposite = (me + 1) % SECT, (me + SECT // 2) % SECT
    bounds = [first[0:1], second[0:1], first[TH - 1 : TH], second[TH - 1 : TH]]
    for t in range(SECT):
        for k in range(4):
            edge_ref[t, EDGE_BOUND + k : EDGE_BOUND + k + 1, :] = bounds[k]
    for c in range(3):
        for z in range(2):
            for h in range(2):
                x = field[c][z][h]
                row = (c * 2 + z) * 2 + h
                for t in range(SECT):
                    edge = jnp.where(t == up, x[TH - 1 : TH], x[0:1])
                    if row < 4:
                        edge = jnp.where(t == opposite, turned[row * 32 : row * 32 + 1], edge)
                    edge_ref[t, row : row + 1, :] = edge


def send_inner(out, rows):
    for t in range(SECT):
        out.copy(out.vmem("inner"), out.hbm("msg").at[t, 0:rows, :])


def write_axial(one_ref, two_ref, field, slab):
    odd = slab % 2 == 1
    for c in range(3):
        for h in range(2):
            rows = pl.ds((c * 2 + h) * TH, TH)
            low, high = field[c][0][h], field[c][1][h]
            one_ref[rows, :] = jnp.where(odd, low, high)
            two_ref[rows, :] = jnp.where(odd, high, low)


class Inputs:
    def __init__(self, names, refs, bufs, sems):
        self.refs = dict(zip(names, bufs))
        self.copies = {}
        for i, (name, ref, buf) in enumerate(zip(names, refs, bufs)):
            if name == "inner":
                ref = ref.at[:, 0:ROW_EDGE, :]
            if name == "edge":
                ref = ref.at[:, ROW_EDGE:, :]
            if name == "basis_t":
                own = lax.axis_index("az") % 4
                ref = ref.at[:, pl.ds(pl.multiple_of(own * TH, TH), TH), :]
            self.copies[name] = [pltpu.make_async_copy(ref, buf, sems.at[i])]
            self.copies[name][0].start()

    def __call__(self, name):
        for copy in self.copies.pop(name, ()):
            copy.wait()
        return self.refs[name]


class Outputs:
    def __init__(self, names, refs, bufs, sems):
        self.refs, self.bufs, self.sems, self.started = dict(zip(names, refs)), bufs, sems, []

    def hbm(self, name):
        return self.refs[name]

    def vmem(self, name):
        return self.bufs[name]

    def copy(self, src, dst):
        copy = pltpu.make_async_copy(src, dst, self.sems.at[len(self.started)])
        copy.start()
        self.started.append(copy)

    def send(self, name):
        self.copy(self.bufs[name], self.refs[name])

    def finish(self):
        for copy in self.started:
            copy.wait()


def pack_kernel(inp, out):
    me = lax.axis_index("az")
    tmp_ref, nu_s, edge_ref, stay_ref = out.vmem("tmp"), out.vmem("nu"), out.vmem("edge"), out.vmem("stay")
    vel_ref, nu_ref = inp("vel"), inp("nu")
    field = [[[vel_ref[strided(c, z, h), :] for h in range(2)] for z in range(2)] for c in range(3)]
    nu_s[...] = nu_ref[...].astype(f32)
    nu = [nu_s[pl.ds(z, TH, stride=4), :] for z in range(2)]
    write_message(out.vmem("inner"), edge_ref, field, nu, me)
    send_inner(out, ROW_EDGE)
    write_axial(out.vmem("one"), out.vmem("two"), field, lax.axis_index("ax"))
    out.send("one")
    out.send("two")
    pv_ref, pc_ref = inp("pv"), inp("pc")
    for i in range(64):
        tmp_ref[i * 8 : i * 8 + 3, :] = pv_ref[:, i * 128 : (i + 1) * 128]
        tmp_ref[512 + i * 8 : 512 + i * 8 + 3, :] = pc_ref[:, i * 128 : (i + 1) * 128].astype(f32)
    parts = []
    for k in range(2):
        for c in range(3):
            parts.append(jnp.concatenate(split2(tmp_ref[pl.ds(k * 512 + c, 64, stride=8), :]), axis=1))
    rows_ref, cnt_ref = inp("rows"), inp("cnt")
    lane = lane_iota((1, 128))
    listed = [rows_ref[0, t : t + 1, :] for t in range(SECT)]
    low = jnp.concatenate([one_hot(row % 128, 128, 128) for row in listed], axis=1)
    high = [row_iota((64, 128)) == row // 128 for row in listed]
    used_high = []
    for t in range(SECT):
        used = (high[t] & (lane < cnt_ref[me, 0, t])).astype(f32)
        used_high.append(used.astype(bf16))
    picked = jnp.dot(
        jnp.concatenate(parts, axis=0), jnp.concatenate([low, low], axis=0), preferred_element_type=f32
    )
    for t in range(SECT):
        for q in range(6):
            value = picked[q * 64 : (q + 1) * 64, t * 128 : (t + 1) * 128]
            edge_ref[t, EDGE_PART + q : EDGE_PART + q + 1, :] = jnp.sum(
                jnp.where(high[t], value, 0.0), axis=0, keepdims=True
            )
    out.copy(edge_ref, out.hbm("msg").at[:, ROW_EDGE:, :])
    leaving = lax.dot_general(
        jnp.concatenate(used_high, axis=1), low, (((1,), (1,)), ((), ())), preferred_element_type=f32
    )
    stay = 1.0 - leaving
    for i in range(64):
        stay_ref[0:1, i * 128 : (i + 1) * 128] = stay[i : i + 1, :]
    out.send("stay")


def local_row(theta, r, z, me, slab):
    return ((z - 2 * slab) * 2 + r // 128) * TH + theta - me * TH


def spread(x, rows, n):
    tile = jnp.broadcast_to(x, (16, n)).astype(bf16)
    return jnp.concatenate([tile] * (rows // 16), axis=0)


def matches(index, rows, n):
    return row_iota((rows, n)).astype(f32).astype(bf16) == spread(index.astype(f32), rows, n)


def one_hot(index, rows, n):
    return jnp.where(matches(index, rows, n), jnp.ones((), bf16), jnp.zeros((), bf16))


def deposit(row, col, velocity, n):
    cols = matches(col, 128, n)
    pieces = []
    for c in range(3):
        for part in split2(velocity[c]):
            pieces.append(jnp.where(cols, spread(part.astype(f32), 128, n), jnp.zeros((), bf16)))
    pieces.append(one_hot(col, 128, n))
    return lax.dot_general(
        one_hot(row, 256, n), jnp.concatenate(pieces, axis=0), (((1,), (1,)), ((), ())), preferred_element_type=f32
    )


def add_parts(acc):
    out = [acc[:, c * 256 : c * 256 + 128] + acc[:, c * 256 + 128 : c * 256 + 256] for c in range(3)]
    out.append(acc[:, 768:896])
    return out


def write_blocks(ref, x):
    for c in range(3):
        for z in range(2):
            for h in range(2):
                ref[block(c, z, h), :] = x[c][z][h]


def scatter_kernel(inp, out):
    me = lax.axis_index("az")
    slab = lax.axis_index("ax")
    pc_ref, stay_ref, pv_ref = inp("pc"), inp("stay"), inp("pv")
    sum_ref, acc_ref = out.vmem("sums"), out.vmem("acc")
    for k in range(NP // CHUNK):
        part = pl.ds(k * CHUNK, CHUNK)
        row = local_row(pc_ref[0:1, part], pc_ref[1:2, part], pc_ref[2:3, part], me, slab)
        row = jnp.where(stay_ref[0:1, part] > 0.5, row, -1)
        col = pc_ref[1:2, part] % 128
        more = deposit(row, col, [pv_ref[c : c + 1, part] for c in range(3)], CHUNK)
        if k == 0:
            acc_ref[...] = more
        else:
            acc_ref[...] += more
    for c, x in enumerate(add_parts(acc_ref)):
        sum_ref[c * 256 : (c + 1) * 256, :] = x
    out.send("sums")
    rates = local_rate(input_blocks(inp), viscosity_blocks(inp, out), magnetic_blocks(inp, out))
    write_blocks(out.vmem("local"), rates)
    out.send("local")


def arrivals(edge_ref, cnt_ref, me, slab):
    lane = lane_iota((1, CAP))
    live = jnp.concatenate([(lane < cnt_ref[s, 0, me]).astype(i32) for s in range(SECT)], axis=1)

    def channel(q):
        return jnp.concatenate([edge_ref[s, EDGE_PART + q : EDGE_PART + q + 1, :] for s in range(SECT)], axis=1)

    velocity = [channel(c) for c in range(3)]
    theta, r, z = [channel(3 + c).astype(i32) for c in range(3)]
    row = jnp.where(live > 0, local_row(theta, r, z, me, slab), -1)
    return live, row, r % 128, velocity


def whole_azimuth_part(inp):
    recv_ref, edge_ref = inp("inner"), inp("edge")
    left, lap_factor, grad_factor, cross = azimuth_factors()
    bounds = []
    for k in range(4):
        at = EDGE_BOUND + k
        bounds.append(jnp.concatenate([edge_ref[t, at : at + 1, :] for t in range(SECT)], axis=0))

    def share(near, far, sign):
        nu, swirl = both_halves(near[1], False), both_halves(near[0], False)
        factor = nu * lap_factor - sign * swirl * grad_factor
        turn = cross * nu * pltpu.roll(sign * far[0] * grad_factor, 64, 1)
        return factor * far[0] + turn, jnp.where(left, factor * far[1], 0.0)

    begin, end = bounds[:2], bounds[2:]
    at_begin = share(begin, [pltpu.roll(x, 1, 0) for x in end], -1.0)
    at_end = share(end, [pltpu.roll(x, SECT - 1, 0) for x in begin], 1.0)
    row = row_iota((8, 128))
    out = ([], [])
    for t in range(SECT):
        folded = recv_ref[t, ROW_B : ROW_B + TH // 2, :]
        second = jnp.concatenate([folded, pltpu.roll(folded, 64, 1)], axis=0)
        for k, x in enumerate((recv_ref[t, 0:TH, :], jnp.where(left, second, 0.0))):
            out[k].append(x[:8] + jnp.where(row == 0, at_begin[k][t : t + 1], 0.0))
            out[k].append(x[8 : TH - 8])
            out[k].append(x[TH - 8 :] + jnp.where(row == 7, at_end[k][t : t + 1], 0.0))
    return jnp.concatenate(out[0], axis=0), jnp.concatenate(out[1], axis=0)


def filtered_inner(inp, me):
    part = jnp.concatenate(whole_azimuth_part(inp), axis=1)
    low, high = part[: NA // 2], part[NA // 2 :]
    basis_ref, weight_ref, basis_t_ref = inp("basis"), inp("weight"), inp("basis_t")
    out = 0.0
    for parity, x in enumerate((low + high, low - high)):
        spectrum = jnp.dot(basis_ref[parity], x, precision=HIGHEST, preferred_element_type=f32)
        weight = weight_ref[parity]
        spectrum = spectrum * jnp.concatenate([weight, weight], axis=1)
        back = jnp.dot(basis_t_ref[parity], spectrum, precision=HIGHEST, preferred_element_type=f32)
        if parity:
            back = jnp.where(me < 4, back, -back)
        out = out + back
    return out[:, :128], out[:, 128:]


def local_rate(field, nu, magnetic):
    lane = lane_iota((TH, 128))
    row = row_iota((TH, 128))
    rates = [[[None, None], [None, None]] for _ in range(3)]
    for z in range(2):
        rolled = [[(pltpu.roll(field[c][z][h], 1, 1), pltpu.roll(field[c][z][h], 127, 1)) for h in range(2)] for c in range(3)]
        for h in range(2):
            radius = lane_iota((1, 128)).astype(f32) + (h * 128 + 0.5)
            inverse = 1.0 / radius
            eddy = nu[z][h]
            u = [field[c][z][h] for c in range(3)]
            lap_ax, lap_rad, grad_rad, grad_ax, lap_th, grad_th = [], [], [], [], [], []
            for c in range(3):
                x = u[c]
                if h == 0:
                    prev_r = jnp.where(lane == 0, 0.0, rolled[c][0][0])
                    next_r = jnp.where(lane == 127, rolled[c][1][1], rolled[c][0][1])
                else:
                    prev_r = jnp.where(lane == 0, rolled[c][0][0], rolled[c][1][0])
                    next_r = jnp.where(lane == 127, 0.0, rolled[c][1][1])
                other = field[c][1 - z][h]
                prev_t = jnp.where(row == 0, 0.0, pltpu.roll(x, 1, 0))
                next_t = jnp.where(row == TH - 1, 0.0, pltpu.roll(x, TH - 1, 0))
                lap_rad.append(((radius + 0.5) * (next_r - x) - (radius - 0.5) * (x - prev_r)) * inverse)
                lap_ax.append(other - 2.0 * x)
                grad_rad.append(0.5 * (next_r - prev_r))
                grad_ax.append((0.5 if z == 0 else -0.5) * other)
                lap_th.append((next_t - 2.0 * x + prev_t) * (1.0 / (radius * radius * (DTHETA * DTHETA))))
                grad_th.append((next_t - prev_t) * (1.0 / (2.0 * DTHETA * radius)))
            b = [magnetic[c][z][h] for c in range(3)]
            slip = [-u[0], radius * (2.0 / NR) - u[1], -u[2]]
            current = [slip[1] * b[2] - slip[2] * b[1], slip[2] * b[0] - slip[0] * b[2], slip[0] * b[1] - slip[1] * b[0]]
            force = [
                current[1] * b[2] - current[2] * b[1],
                current[2] * b[0] - current[0] * b[2],
                current[0] * b[1] - current[1] * b[0],
            ]
            inverse2 = inverse * inverse
            metric = [
                u[1] * u[1] * inverse - eddy * u[0] * inverse2,
                -eddy * u[1] * inverse2 - u[0] * u[1] * inverse,
                0.0,
            ]
            coupling = [-2.0 * eddy * grad_th[1] * inverse, 2.0 * eddy * grad_th[0] * inverse, 0.0]
            for c in range(3):
                azimuth = eddy * lap_th[c] - u[1] * grad_th[c] + coupling[c]
                if h == 0:
                    azimuth = jnp.where(lane < KR, 0.0, azimuth)
                rates[c][z][h] = (
                    eddy * (lap_rad[c] + lap_ax[c])
                    - (u[0] * grad_rad[c] + u[2] * grad_ax[c])
                    + metric[c]
                    + 0.5 * force[c]
                    + azimuth
                )
    return rates


def outer_rate(field, nu, inp, me, slab):
    filtered = filtered_inner(inp, me)
    edge_ref, one_ref, two_ref = inp("edge"), inp("one"), inp("two")
    before_sector = (me + SECT - 1) % SECT
    after_sector = (me + 1) % SECT
    opposite = (me + SECT // 2) % SECT
    odd = slab % 2 == 1
    lane = lane_iota((TH, 128))
    row = row_iota((8, 128))
    turned = jnp.concatenate([edge_ref[opposite, 0:8, :], jnp.zeros((120, 128), f32)], axis=0).T
    rates = [[[None, None], [None, None]] for _ in range(3)]
    for z in range(2):
        for h in range(2):
            radius = lane_iota((1, 128)).astype(f32) + (h * 128 + 0.5)
            lap_factor = 1.0 / (radius * radius * (DTHETA * DTHETA))
            grad_factor = 1.0 / (2.0 * DTHETA * radius)
            cross = 2.0 * grad_factor / radius
            eddy, u = nu[z][h], [field[c][z][h] for c in range(3)]
            by_face = eddy + (0.5 if z == 0 else -0.5) * u[2]
            end = slab == (0 if z == 0 else lax.axis_size("ax") - 1)
            halos = []
            for sector, at, sign in ((before_sector, slice(0, 8), -1.0), (after_sector, slice(TH - 8, TH), 1.0)):
                f = [edge_ref[sector, (c * 2 + z) * 2 + h : (c * 2 + z) * 2 + h + 1, :] for c in range(3)]
                nu8, swirl8 = eddy[at], u[1][at]
                by_halo = nu8 * lap_factor - sign * swirl8 * grad_factor
                extra = [-sign * cross * nu8 * f[1], sign * cross * nu8 * f[0], 0.0]
                keep = row == (0 if sign < 0 else 7)
                if h == 0:
                    keep = keep & (lane_iota((8, 128)) >= KR)
                halos.append([jnp.where(keep, by_halo * f[c] + extra[c], 0.0) for c in range(3)])
            for c in range(3):
                face = pl.ds((c * 2 + h) * TH, TH)
                one, two = one_ref[face, :], two_ref[face, :]
                face = jnp.where(odd, one, two) if z == 0 else jnp.where(odd, two, one)
                rate = jnp.where(end, 0.0, face) * by_face
                if h == 0:
                    offset = (c % 2) * 64 + z * 32
                    pole = turned[TH:] if c == 2 else turned[:TH]
                    ghost = POLE_SIGNS[c] * lanes(pole, -((c % 2) * 2 + z))
                    rate = rate + jnp.where(lane < KR, lanes(filtered[c // 2], -offset), 0.0)
                    rate = rate + jnp.where(lane == 0, 0.5 * u[0] * ghost, 0.0)
                rates[c][z][h] = jnp.concatenate(
                    [rate[:8] + halos[0][c], rate[8 : TH - 8], rate[TH - 8 :] + halos[1][c]], axis=0
                )
    return rates


def viscosity_blocks(inp, out):
    nu_s = out.vmem("nu")
    nu_s[...] = inp("nu")[...].astype(f32)
    return [[nu_s[strided(0, z, h), :] for h in range(2)] for z in range(2)]


def magnetic_blocks(inp, out):
    mag_s = out.vmem("mag")
    mag_s[...] = inp("mag")[...].astype(f32)
    return [[[mag_s[strided(c, z, h), :] for h in range(2)] for z in range(2)] for c in range(3)]


def input_blocks(inp):
    vel_ref = inp("vel")
    return [[[vel_ref[strided(c, z, h), :] for h in range(2)] for z in range(2)] for c in range(3)]


def blocks(ref):
    return [[[ref[block(c, z, h), :] for h in range(2)] for z in range(2)] for c in range(3)]


def first_kernel(inp, out):
    me = lax.axis_index("az")
    slab = lax.axis_index("ax")
    live, row, col, velocity = arrivals(inp("edge"), inp("cnt"), me, slab)
    arrived = add_parts(deposit(row, col, velocity, SECT * CAP))
    sum_ref = inp("sums")
    total = [sum_ref[c * 256 : (c + 1) * 256, :] + arrived[c] for c in range(4)]
    nu, field = viscosity_blocks(inp, out), input_blocks(inp)
    rates = outer_rate(field, nu, inp, me, slab)
    local_ref = inp("local")
    mid_ref, rest_ref = out.vmem("mid"), out.vmem("rest")
    mid = [[[None, None], [None, None]] for _ in range(3)]
    for c in range(3):
        for z in range(2):
            for h in range(2):
                at = slice((z * 2 + h) * TH, (z * 2 + h + 1) * TH)
                x, s, n = field[c][z][h], total[c][at], total[3][at]
                u1 = x + DT * (local_ref[block(c, z, h), :] + rates[c][z][h] + 2.0 * (s - n * x))
                mid[c][z][h] = u1
                mid_ref[block(c, z, h), :] = u1
                rest_ref[block(c, z, h), :] = 0.5 * (x + u1) + DT * (0.8 * s + 0.2 * n * x - n * u1)
    write_message(out.vmem("inner"), out.vmem("edge"), mid, [nu[z][0] for z in range(2)], me)
    send_inner(out, ROW_EDGE)
    out.copy(out.vmem("edge"), out.hbm("msg").at[:, ROW_EDGE:, :])
    write_axial(out.vmem("one"), out.vmem("two"), mid, slab)
    out.send("one")
    out.send("two")
    out.send("mid")
    out.send("rest")


def take(pick, row, col, n):
    got = jnp.dot(pick, one_hot(row, 256, n), preferred_element_type=f32)
    got = got[:384] + got[384:]
    cols = row_iota((128, n)) == col
    return [jnp.sum(jnp.where(cols, got[c * 128 : (c + 1) * 128], 0.0), axis=0, keepdims=True) for c in range(3)]


def gather_kernel(inp, out):
    me = lax.axis_index("az")
    slab = lax.axis_index("ax")
    pc_ref, stay_ref, pv_ref = inp("pc"), inp("stay"), inp("pv")
    kept_ref, arr_ref = out.vmem("kept"), out.vmem("arrived")
    vel_ref, mid_ref = inp("vel"), inp("mid")
    parts = []
    for c in range(3):
        rows = []
        for z in range(2):
            for h in range(2):
                rows.append(0.08 * vel_ref[strided(c, z, h), :] + 0.1 * mid_ref[block(c, z, h), :])
        parts.append(split2(jnp.concatenate(rows, axis=0).T))
    pick = jnp.concatenate([p[0] for p in parts] + [p[1] for p in parts], axis=0)
    for k in range(NP // CHUNK):
        part = pl.ds(k * CHUNK, CHUNK)
        row = local_row(pc_ref[0:1, part], pc_ref[1:2, part], pc_ref[2:3, part], me, slab)
        stay = stay_ref[0:1, part] > 0.5
        row = jnp.where(stay, row, -1)
        got = take(pick, row, pc_ref[1:2, part] % 128, CHUNK)
        for c in range(3):
            kept_ref[c : c + 1, part] = jnp.where(stay, 0.82 * pv_ref[c : c + 1, part] + got[c], 0.0)
    out.send("kept")
    rates = local_rate(blocks(mid_ref), viscosity_blocks(inp, out), magnetic_blocks(inp, out))
    rest_ref, part_ref = inp("rest"), out.vmem("part")
    for c in range(3):
        for z in range(2):
            for h in range(2):
                part_ref[block(c, z, h), :] = rest_ref[block(c, z, h), :] + (0.5 * DT) * rates[c][z][h]
    out.send("part")
    live, row, col, velocity = arrivals(inp("edge"), inp("cnt"), me, slab)
    got = take(pick, row, col, SECT * CAP)
    for c in range(3):
        arr_ref[c, 0:1, :] = jnp.where(live > 0, 0.82 * velocity[c] + got[c], 0.0)
    out.send("arrived")


def second_kernel(inp, out):
    me = lax.axis_index("az")
    slab = lax.axis_index("ax")
    rates = outer_rate(blocks(inp("mid")), viscosity_blocks(inp, out), inp, me, slab)
    part_ref, new_ref = inp("part"), out.vmem("new")
    for c in range(3):
        for z in range(2):
            for h in range(2):
                new_ref[strided(c, z, h), :] = part_ref[block(c, z, h), :] + (0.5 * DT) * rates[c][z][h]
        rows = pl.ds(c * 256, 256)
        out.copy(new_ref.at[rows, :], out.hbm("new").at[rows, :])


def call(kernel, name, ins, outs, bufs, copies, flops=0, in_smem=()):
    in_names, out_names, buf_names = list(ins), list(outs), list(bufs)
    arrays = [ins[n] for n in in_names]
    n_in, n_out = len(in_names), len(out_names)

    def body(*refs):
        in_refs, refs = refs[:n_in], refs[n_in:]
        out_refs, refs = refs[:n_out], refs[n_out:]
        in_bufs, refs = refs[:n_in], refs[n_in:]
        buf_refs, (in_sems, out_sems) = refs[:-2], refs[-2:]
        out = Outputs(out_names, out_refs, dict(zip(buf_names, buf_refs)), out_sems)
        kernel(Inputs(in_names, in_refs, in_bufs, in_sems), out)
        out.finish()

    def in_shape(n):
        shape = ins[n].shape
        if n == "basis_t":
            return (2, TH, shape[2])
        return {"inner": (SECT, ROW_EDGE, 128), "edge": (SECT, shape[1] - ROW_EDGE, 128)}.get(n, shape)

    hbm = pl.BlockSpec(memory_space=pltpu.HBM)
    return pl.pallas_call(
        body,
        out_shape=[jax.ShapeDtypeStruct(*outs[n]) for n in out_names],
        in_specs=[hbm] * n_in,
        out_specs=[hbm] * n_out,
        scratch_shapes=[(pltpu.SMEM if n in in_smem else pltpu.VMEM)(in_shape(n), ins[n].dtype) for n in in_names]
        + [pltpu.VMEM(*bufs[n]) for n in buf_names]
        + [pltpu.SemaphoreType.DMA((n_in,)), pltpu.SemaphoreType.DMA((copies,))],
        compiler_params=pltpu.CompilerParams(vmem_limit_bytes=VMEM_LIMIT),
        cost_estimate=pl.CostEstimate(flops=flops, bytes_accessed=2 * 1024 * 1024, transcendentals=0),
        name=name,
    )(*arrays)


def rows_of(x):
    lead = x.shape[:-2]
    x = x.reshape(*lead, 2, 2, 128)
    return jnp.swapaxes(x, -3, -2).reshape(-1, 128)


def per_device(velocity, viscosity, bfield, particle_velocity, particle_cell, send_rows, send_counts):
    ax = lax.axis_size("ax")
    vel, nu, mag = rows_of(velocity), rows_of(viscosity), rows_of(bfield)
    pv, pc = particle_velocity, particle_cell
    tables = {"basis": jnp.asarray(BASIS), "weight": jnp.asarray(MODE_WEIGHT), "basis_t": jnp.asarray(BASIS_T)}
    swap_one = [(i, i ^ 1) for i in range(ax)]
    swap_two = []
    for a in range(SECT):
        swap_two += [(a * ax + i, a * ax + ((i + 1) ^ 1) - 1) for i in range(1, ax - 1)]
        swap_two += [(a * ax + i, (a ^ 2) * ax + i) for i in (0, ax - 1)]

    def swap(one, two):
        return lax.ppermute(one, "ax", swap_one), lax.ppermute(two, ("az", "ax"), swap_two)

    def to_all(msg):
        return lax.all_to_all(msg, "az", split_axis=0, concat_axis=0, tiled=True)

    face = ((384, 128), f32)
    field = ((768, 128), f32)
    materials = {"nu": ((256, 128), f32), "mag": field}
    msg, one, two, stay = call(
        pack_kernel,
        "pack",
        {"vel": vel, "nu": nu, "pc": pc, "pv": pv, "rows": send_rows, "cnt": send_counts},
        {"msg": ((SECT, ROW_EDGE + EDGE1, 128), f32), "one": face, "two": face, "stay": ((1, NP), f32)},
        {
            "inner": ((ROW_EDGE, 128), f32),
            "one": face,
            "two": face,
            "edge": ((SECT, EDGE1, 128), f32),
            "stay": ((1, NP), f32),
            "tmp": ((1024, 128), f32),
            "nu": ((256, 128), f32),
        },
        12,
        in_smem=("cnt",),
    )
    one, two = swap(one, two)
    recv = to_all(msg)
    sums, local = call(
        scatter_kernel,
        "deposit",
        {"pc": pc, "stay": stay, "pv": pv, "vel": vel, "nu": nu, "mag": mag},
        {"sums": ((1024, 128), f32), "local": field},
        {"sums": ((1024, 128), f32), "acc": ((256, 896), f32), "local": field} | materials,
        2,
        flops=2 * NP * 256 * 896,
    )
    msg2, one2, two2, mid, rest = call(
        first_kernel,
        "first_section",
        {"edge": recv, "inner": recv, "cnt": send_counts, "basis": tables["basis"], "sums": sums, "nu": nu, "vel": vel}
        | tables
        | {"one": one, "two": two, "local": local},
        {"msg": ((SECT, ROW_EDGE + EDGE2, 128), f32), "one": face, "two": face, "mid": field, "rest": field},
        {
            "inner": ((ROW_EDGE, 128), f32),
            "edge": ((SECT, EDGE2, 128), f32),
            "one": face,
            "two": face,
            "mid": field,
            "rest": field,
            "nu": ((256, 128), f32),
        },
        13,
        in_smem=("cnt",),
    )
    one2, two2 = swap(one2, two2)
    recv2 = to_all(msg2)
    kept, arrived, part = call(
        gather_kernel,
        "take",
        {"vel": vel, "mid": mid, "pc": pc, "stay": stay, "pv": pv, "nu": nu, "mag": mag, "rest": rest}
        | {"edge": recv, "cnt": send_counts},
        {"kept": ((3, NP), f32), "arrived": ((3, 1, SECT * CAP), f32), "part": field},
        {"kept": ((3, NP), f32), "arrived": ((3, 1, SECT * CAP), f32), "part": field} | materials,
        3,
        flops=2 * NP * 512 * 384,
        in_smem=("cnt",),
    )
    (new,) = call(
        second_kernel,
        "second_section",
        {"inner": recv2} | tables | {"edge": recv2, "mid": mid, "nu": nu, "one": one2, "two": two2, "part": part},
        {"new": field},
        {"nu": ((256, 128), f32), "new": field},
        3,
    )
    new = jnp.swapaxes(new.reshape(3, TH, 2, 2, 128), 2, 3).reshape(3, TH, 2, NR)
    return new, kept, jnp.swapaxes(arrived, 0, 1)


def solution(mesh):
    return jax.shard_map(
        per_device,
        mesh=mesh,
        in_specs=(
            P(None, "az", "ax", None),
            P("az", "ax", None),
            P(None, "az", "ax", None),
            P(None, ("az", "ax")),
            P(None, ("az", "ax")),
            P(("az", "ax"), None, None),
            P(None, "ax", None),
        ),
        out_specs=(P(None, "az", "ax", None), P(None, ("az", "ax")), P(("az", "ax"), None, None)),
        check_vma=False,
    )
```

```python
import math

import jax
import jax.numpy as jnp
import numpy as np
from jax import lax
from jax.experimental import pallas as pl
from jax.experimental.pallas import tpu as pltpu
from jax.sharding import PartitionSpec as P

NA = 512
NR = 256
KR = 32
SECT = 8
TH = NA // SECT
CAP = 128
NP = 8192
DTHETA = 2.0 * math.pi / NA
DT = 0.02
POLE_SIGNS = (-1.0, -1.0, 1.0)
HIGHEST = lax.Precision.HIGHEST
f32 = jnp.float32
bf16 = jnp.bfloat16
i32 = jnp.int32
VMEM_LIMIT = 65408 * 1024

ROW_B = 64
ROW_EDGE = 96
EDGE_BOUND = 12
EDGE_PART = 16
EDGE1 = 24
EDGE2 = 16
CHUNK = 1024


def filter_tables():
    a = np.arange(NA // 2)
    even, odd, even_mode, odd_mode = [], [], [], []
    for m in range(NA // 2 + 1):
        scale = math.sqrt((1.0 if m in (0, NA // 2) else 2.0) / NA)
        phase = 2.0 * math.pi * (m * a % NA) / NA
        rows = [scale * np.cos(phase)]
        if m not in (0, NA // 2):
            rows.append(scale * np.sin(phase))
        for row in rows:
            (odd if m % 2 else even).append(row)
            (odd_mode if m % 2 else even_mode).append(m)
    basis = np.stack([np.stack(even), np.stack(odd)]).astype(np.float32)
    modes = np.stack([np.array(even_mode), np.array(odd_mode)]).astype(np.float64)
    cutoff = 4.0 * (np.arange(KR) + 0.5)
    weight = 1.0 / (1.0 + (modes[:, :, None] / cutoff) ** 4)
    weight = np.tile(weight, (1, 1, 128 // KR)).astype(np.float32)
    return basis, np.ascontiguousarray(basis.transpose(0, 2, 1)), weight


BASIS, BASIS_T, MODE_WEIGHT = filter_tables()


def lane_iota(shape):
    return lax.broadcasted_iota(i32, shape, len(shape) - 1)


def row_iota(shape):
    return lax.broadcasted_iota(i32, shape, len(shape) - 2)


def strided(c, z, h):
    return pl.ds(c * 256 + h * 2 + z, TH, stride=4)


def block(c, z, h):
    return pl.ds(((c * 2 + z) * 2 + h) * TH, TH)


def lanes(x, by):
    by %= 128
    return x if by == 0 else pltpu.roll(x, by, 1)


def split2(x):
    hi = x.astype(bf16)
    return hi, (x - hi.astype(f32)).astype(bf16)


def pack_inner(field, nu):
    lane = lane_iota((TH, 128))

    def four(p, q, r, s):
        low = jnp.where(lane < 32, p, lanes(q, 32))
        high = jnp.where(lane < 96, lanes(r, 64), lanes(s, 96))
        return jnp.where(lane < 64, low, high)

    first = four(field[0][0][0], field[0][1][0], field[1][0][0], field[1][1][0])
    second = four(field[2][0][0], field[2][1][0], nu[0], nu[1])
    return first, second


def azimuth_factors():
    lane = lane_iota((1, 128))
    radius = (lane % KR).astype(f32) + 0.5
    lap = 1.0 / (radius * radius * (DTHETA * DTHETA))
    grad = 1.0 / (2.0 * DTHETA * radius)
    return lane < 64, lap, grad, jnp.where(lane < 64, -2.0, 2.0) / radius


def both_halves(x, left):
    side = lane_iota((1, 128)) < 64
    return jnp.where(side == left, x, pltpu.roll(x, 64, 1))


def azimuth_inner(first, second):
    left, lap_factor, grad_factor, cross = azimuth_factors()
    row = row_iota((TH, 128))
    nu, swirl = both_halves(second, False), both_halves(first, False)

    def differences(x):
        after = jnp.where(row == TH - 1, 0.0, pltpu.roll(x, TH - 1, 0))
        before = jnp.where(row == 0, 0.0, pltpu.roll(x, 1, 0))
        return (after - 2.0 * x + before) * lap_factor, (after - before) * grad_factor

    lap, grad = differences(first)
    part_first = nu * lap - swirl * grad + cross * nu * pltpu.roll(grad, 64, 1)
    lap, grad = differences(second)
    return part_first, jnp.where(left, nu * lap - swirl * grad, 0.0)


def write_message(inner_ref, edge_ref, field, nu, me):
    first, second = pack_inner(field, nu)
    part_first, part_second = azimuth_inner(first, second)
    inner_ref[0:TH, :] = part_first
    inner_ref[TH:, :] = part_second[: TH // 2] + pltpu.roll(part_second[TH // 2 :], 64, 1)
    turned = jnp.concatenate([first, second], axis=0).T
    up, opposite = (me + 1) % SECT, (me + SECT // 2) % SECT
    bounds = [first[0:1], second[0:1], first[TH - 1 : TH], second[TH - 1 : TH]]
    for t in range(SECT):
        for k in range(4):
            edge_ref[t, EDGE_BOUND + k : EDGE_BOUND + k + 1, :] = bounds[k]
    for c in range(3):
        for z in range(2):
            for h in range(2):
                x = field[c][z][h]
                row = (c * 2 + z) * 2 + h
                for t in range(SECT):
                    edge = jnp.where(t == up, x[TH - 1 : TH], x[0:1])
                    if row < 4:
                        edge = jnp.where(t == opposite, turned[row * 32 : row * 32 + 1], edge)
                    edge_ref[t, row : row + 1, :] = edge


def send_inner(out, rows):
    for t in range(SECT):
        out.copy(out.vmem("inner"), out.hbm("msg").at[t, 0:rows, :])


def write_axial(one_ref, two_ref, field, slab):
    odd = slab % 2 == 1
    for c in range(3):
        for h in range(2):
            rows = pl.ds((c * 2 + h) * TH, TH)
            low, high = field[c][0][h], field[c][1][h]
            one_ref[rows, :] = jnp.where(odd, low, high)
            two_ref[rows, :] = jnp.where(odd, high, low)


class Inputs:
    def __init__(self, names, refs, bufs, sems):
        self.refs = dict(zip(names, bufs))
        self.copies = {}
        for i, (name, ref, buf) in enumerate(zip(names, refs, bufs)):
            if name == "inner":
                ref = ref.at[:, 0:ROW_EDGE, :]
            if name == "edge":
                ref = ref.at[:, ROW_EDGE:, :]
            if name == "basis_t":
                own = lax.axis_index("az") % 4
                ref = ref.at[:, pl.ds(pl.multiple_of(own * TH, TH), TH), :]
            self.copies[name] = [pltpu.make_async_copy(ref, buf, sems.at[i])]
            self.copies[name][0].start()

    def __call__(self, name):
        for copy in self.copies.pop(name, ()):
            copy.wait()
        return self.refs[name]


class Outputs:
    def __init__(self, names, refs, bufs, sems):
        self.refs, self.bufs, self.sems, self.started = dict(zip(names, refs)), bufs, sems, []

    def hbm(self, name):
        return self.refs[name]

    def vmem(self, name):
        return self.bufs[name]

    def copy(self, src, dst):
        copy = pltpu.make_async_copy(src, dst, self.sems.at[len(self.started)])
        copy.start()
        self.started.append(copy)

    def send(self, name):
        self.copy(self.bufs[name], self.refs[name])

    def finish(self):
        for copy in self.started:
            copy.wait()


def pack_kernel(inp, out):
    me = lax.axis_index("az")
    tmp_ref, nu_s, edge_ref, stay_ref = out.vmem("tmp"), out.vmem("nu"), out.vmem("edge"), out.vmem("stay")
    vel_ref, nu_ref = inp("vel"), inp("nu")
    field = [[[vel_ref[strided(c, z, h), :] for h in range(2)] for z in range(2)] for c in range(3)]
    nu_s[...] = nu_ref[...].astype(f32)
    nu = [nu_s[pl.ds(z, TH, stride=4), :] for z in range(2)]
    write_message(out.vmem("inner"), edge_ref, field, nu, me)
    send_inner(out, ROW_EDGE)
    write_axial(out.vmem("one"), out.vmem("two"), field, lax.axis_index("ax"))
    out.send("one")
    out.send("two")
    pv_ref, pc_ref = inp("pv"), inp("pc")
    for i in range(64):
        tmp_ref[i * 8 : i * 8 + 3, :] = pv_ref[:, i * 128 : (i + 1) * 128]
        tmp_ref[512 + i * 8 : 512 + i * 8 + 3, :] = pc_ref[:, i * 128 : (i + 1) * 128].astype(f32)
    parts = []
    for k in range(2):
        for c in range(3):
            parts.append(jnp.concatenate(split2(tmp_ref[pl.ds(k * 512 + c, 64, stride=8), :]), axis=1))
    rows_ref, cnt_ref = inp("rows"), inp("cnt")
    lane = lane_iota((1, 128))
    listed = [rows_ref[0, t : t + 1, :] for t in range(SECT)]
    low = jnp.concatenate([one_hot(row % 128, 128, 128) for row in listed], axis=1)
    high = [row_iota((64, 128)) == row // 128 for row in listed]
    used_high = []
    for t in range(SECT):
        used = (high[t] & (lane < cnt_ref[me, 0, t])).astype(f32)
        used_high.append(used.astype(bf16))
    picked = jnp.dot(
        jnp.concatenate(parts, axis=0), jnp.concatenate([low, low], axis=0), preferred_element_type=f32
    )
    for t in range(SECT):
        for q in range(6):
            value = picked[q * 64 : (q + 1) * 64, t * 128 : (t + 1) * 128]
            edge_ref[t, EDGE_PART + q : EDGE_PART + q + 1, :] = jnp.sum(
                jnp.where(high[t], value, 0.0), axis=0, keepdims=True
            )
    out.copy(edge_ref, out.hbm("msg").at[:, ROW_EDGE:, :])
    leaving = lax.dot_general(
        jnp.concatenate(used_high, axis=1), low, (((1,), (1,)), ((), ())), preferred_element_type=f32
    )
    stay = 1.0 - leaving
    for i in range(64):
        stay_ref[0:1, i * 128 : (i + 1) * 128] = stay[i : i + 1, :]
    out.send("stay")


def local_row(theta, r, z, me, slab):
    return ((z - 2 * slab) * 2 + r // 128) * TH + theta - me * TH


def spread(x, rows, n):
    tile = jnp.broadcast_to(x, (16, n)).astype(bf16)
    return jnp.concatenate([tile] * (rows // 16), axis=0)


def matches(index, rows, n):
    return row_iota((rows, n)).astype(f32).astype(bf16) == spread(index.astype(f32), rows, n)


def one_hot(index, rows, n):
    return jnp.where(matches(index, rows, n), jnp.ones((), bf16), jnp.zeros((), bf16))


def deposit(row, col, velocity, n):
    cols = matches(col, 128, n)
    pieces = []
    for c in range(3):
        for part in split2(velocity[c]):
            pieces.append(jnp.where(cols, spread(part.astype(f32), 128, n), jnp.zeros((), bf16)))
    pieces.append(one_hot(col, 128, n))
    return lax.dot_general(
        one_hot(row, 256, n), jnp.concatenate(pieces, axis=0), (((1,), (1,)), ((), ())), preferred_element_type=f32
    )


def add_parts(acc):
    out = [acc[:, c * 256 : c * 256 + 128] + acc[:, c * 256 + 128 : c * 256 + 256] for c in range(3)]
    out.append(acc[:, 768:896])
    return out


def write_blocks(ref, x):
    for c in range(3):
        for z in range(2):
            for h in range(2):
                ref[block(c, z, h), :] = x[c][z][h]


def scatter_kernel(inp, out):
    me = lax.axis_index("az")
    slab = lax.axis_index("ax")
    pc_ref, stay_ref, pv_ref = inp("pc"), inp("stay"), inp("pv")
    sum_ref, acc_ref = out.vmem("sums"), out.vmem("acc")
    for k in range(NP // CHUNK):
        part = pl.ds(k * CHUNK, CHUNK)
        row = local_row(pc_ref[0:1, part], pc_ref[1:2, part], pc_ref[2:3, part], me, slab)
        row = jnp.where(stay_ref[0:1, part] > 0.5, row, -1)
        col = pc_ref[1:2, part] % 128
        more = deposit(row, col, [pv_ref[c : c + 1, part] for c in range(3)], CHUNK)
        if k == 0:
            acc_ref[...] = more
        else:
            acc_ref[...] += more
    for c, x in enumerate(add_parts(acc_ref)):
        sum_ref[c * 256 : (c + 1) * 256, :] = x
    out.send("sums")
    rates = local_rate(input_blocks(inp), viscosity_blocks(inp, out), magnetic_blocks(inp, out))
    write_blocks(out.vmem("local"), rates)
    out.send("local")


def arrivals(edge_ref, cnt_ref, me, slab):
    lane = lane_iota((1, CAP))
    live = jnp.concatenate([(lane < cnt_ref[s, 0, me]).astype(i32) for s in range(SECT)], axis=1)

    def channel(q):
        return jnp.concatenate([edge_ref[s, EDGE_PART + q : EDGE_PART + q + 1, :] for s in range(SECT)], axis=1)

    velocity = [channel(c) for c in range(3)]
    theta, r, z = [channel(3 + c).astype(i32) for c in range(3)]
    row = jnp.where(live > 0, local_row(theta, r, z, me, slab), -1)
    return live, row, r % 128, velocity


def whole_azimuth_part(inp):
    recv_ref, edge_ref = inp("inner"), inp("edge")
    left, lap_factor, grad_factor, cross = azimuth_factors()
    bounds = []
    for k in range(4):
        at = EDGE_BOUND + k
        bounds.append(jnp.concatenate([edge_ref[t, at : at + 1, :] for t in range(SECT)], axis=0))

    def share(near, far, sign):
        nu, swirl = both_halves(near[1], False), both_halves(near[0], False)
        factor = nu * lap_factor - sign * swirl * grad_factor
        turn = cross * nu * pltpu.roll(sign * far[0] * grad_factor, 64, 1)
        return factor * far[0] + turn, jnp.where(left, factor * far[1], 0.0)

    begin, end = bounds[:2], bounds[2:]
    at_begin = share(begin, [pltpu.roll(x, 1, 0) for x in end], -1.0)
    at_end = share(end, [pltpu.roll(x, SECT - 1, 0) for x in begin], 1.0)
    row = row_iota((8, 128))
    out = ([], [])
    for t in range(SECT):
        folded = recv_ref[t, ROW_B : ROW_B + TH // 2, :]
        second = jnp.concatenate([folded, pltpu.roll(folded, 64, 1)], axis=0)
        for k, x in enumerate((recv_ref[t, 0:TH, :], jnp.where(left, second, 0.0))):
            out[k].append(x[:8] + jnp.where(row == 0, at_begin[k][t : t + 1], 0.0))
            out[k].append(x[8 : TH - 8])
            out[k].append(x[TH - 8 :] + jnp.where(row == 7, at_end[k][t : t + 1], 0.0))
    return jnp.concatenate(out[0], axis=0), jnp.concatenate(out[1], axis=0)


def filtered_inner(inp, me):
    part = jnp.concatenate(whole_azimuth_part(inp), axis=1)
    low, high = part[: NA // 2], part[NA // 2 :]
    basis_ref, weight_ref, basis_t_ref = inp("basis"), inp("weight"), inp("basis_t")
    out = 0.0
    for parity, x in enumerate((low + high, low - high)):
        spectrum = jnp.dot(basis_ref[parity], x, precision=HIGHEST, preferred_element_type=f32)
        weight = weight_ref[parity]
        spectrum = spectrum * jnp.concatenate([weight, weight], axis=1)
        back = jnp.dot(basis_t_ref[parity], spectrum, precision=HIGHEST, preferred_element_type=f32)
        if parity:
            back = jnp.where(me < 4, back, -back)
        out = out + back
    return out[:, :128], out[:, 128:]


def local_rate(field, nu, magnetic):
    lane = lane_iota((TH, 128))
    row = row_iota((TH, 128))
    rates = [[[None, None], [None, None]] for _ in range(3)]
    for z in range(2):
        rolled = [[(pltpu.roll(field[c][z][h], 1, 1), pltpu.roll(field[c][z][h], 127, 1)) for h in range(2)] for c in range(3)]
        for h in range(2):
            radius = lane_iota((1, 128)).astype(f32) + (h * 128 + 0.5)
            inverse = 1.0 / radius
            eddy = nu[z][h]
            u = [field[c][z][h] for c in range(3)]
            lap_ax, lap_rad, grad_rad, grad_ax, lap_th, grad_th = [], [], [], [], [], []
            for c in range(3):
                x = u[c]
                if h == 0:
                    prev_r = jnp.where(lane == 0, 0.0, rolled[c][0][0])
                    next_r = jnp.where(lane == 127, rolled[c][1][1], rolled[c][0][1])
                else:
                    prev_r = jnp.where(lane == 0, rolled[c][0][0], rolled[c][1][0])
                    next_r = jnp.where(lane == 127, 0.0, rolled[c][1][1])
                other = field[c][1 - z][h]
                prev_t = jnp.where(row == 0, 0.0, pltpu.roll(x, 1, 0))
                next_t = jnp.where(row == TH - 1, 0.0, pltpu.roll(x, TH - 1, 0))
                lap_rad.append(((radius + 0.5) * (next_r - x) - (radius - 0.5) * (x - prev_r)) * inverse)
                lap_ax.append(other - 2.0 * x)
                grad_rad.append(0.5 * (next_r - prev_r))
                grad_ax.append((0.5 if z == 0 else -0.5) * other)
                lap_th.append((next_t - 2.0 * x + prev_t) * (1.0 / (radius * radius * (DTHETA * DTHETA))))
                grad_th.append((next_t - prev_t) * (1.0 / (2.0 * DTHETA * radius)))
            b = [magnetic[c][z][h] for c in range(3)]
            slip = [-u[0], radius * (2.0 / NR) - u[1], -u[2]]
            current = [slip[1] * b[2] - slip[2] * b[1], slip[2] * b[0] - slip[0] * b[2], slip[0] * b[1] - slip[1] * b[0]]
            force = [
                current[1] * b[2] - current[2] * b[1],
                current[2] * b[0] - current[0] * b[2],
                current[0] * b[1] - current[1] * b[0],
            ]
            inverse2 = inverse * inverse
            metric = [
                u[1] * u[1] * inverse - eddy * u[0] * inverse2,
                -eddy * u[1] * inverse2 - u[0] * u[1] * inverse,
                0.0,
            ]
            coupling = [-2.0 * eddy * grad_th[1] * inverse, 2.0 * eddy * grad_th[0] * inverse, 0.0]
            for c in range(3):
                azimuth = eddy * lap_th[c] - u[1] * grad_th[c] + coupling[c]
                if h == 0:
                    azimuth = jnp.where(lane < KR, 0.0, azimuth)
                rates[c][z][h] = (
                    eddy * (lap_rad[c] + lap_ax[c])
                    - (u[0] * grad_rad[c] + u[2] * grad_ax[c])
                    + metric[c]
                    + 0.5 * force[c]
                    + azimuth
                )
    return rates


def outer_rate(filtered, field, nu, inp, me, slab):
    edge_ref, one_ref, two_ref = inp("edge"), inp("one"), inp("two")
    before_sector = (me + SECT - 1) % SECT
    after_sector = (me + 1) % SECT
    opposite = (me + SECT // 2) % SECT
    odd = slab % 2 == 1
    lane = lane_iota((TH, 128))
    row = row_iota((8, 128))
    turned = jnp.concatenate([edge_ref[opposite, 0:8, :], jnp.zeros((120, 128), f32)], axis=0).T
    rates = [[[None, None], [None, None]] for _ in range(3)]
    for z in range(2):
        for h in range(2):
            radius = lane_iota((1, 128)).astype(f32) + (h * 128 + 0.5)
            lap_factor = 1.0 / (radius * radius * (DTHETA * DTHETA))
            grad_factor = 1.0 / (2.0 * DTHETA * radius)
            cross = 2.0 * grad_factor / radius
            eddy, u = nu[z][h], [field[c][z][h] for c in range(3)]
            by_face = eddy + (0.5 if z == 0 else -0.5) * u[2]
            end = slab == (0 if z == 0 else lax.axis_size("ax") - 1)
            halos = []
            for sector, at, sign in ((before_sector, slice(0, 8), -1.0), (after_sector, slice(TH - 8, TH), 1.0)):
                f = [edge_ref[sector, (c * 2 + z) * 2 + h : (c * 2 + z) * 2 + h + 1, :] for c in range(3)]
                nu8, swirl8 = eddy[at], u[1][at]
                by_halo = nu8 * lap_factor - sign * swirl8 * grad_factor
                extra = [-sign * cross * nu8 * f[1], sign * cross * nu8 * f[0], 0.0]
                keep = row == (0 if sign < 0 else 7)
                if h == 0:
                    keep = keep & (lane_iota((8, 128)) >= KR)
                halos.append([jnp.where(keep, by_halo * f[c] + extra[c], 0.0) for c in range(3)])
            for c in range(3):
                face = pl.ds((c * 2 + h) * TH, TH)
                one, two = one_ref[face, :], two_ref[face, :]
                face = jnp.where(odd, one, two) if z == 0 else jnp.where(odd, two, one)
                rate = jnp.where(end, 0.0, face) * by_face
                if h == 0:
                    offset = (c % 2) * 64 + z * 32
                    pole = turned[TH:] if c == 2 else turned[:TH]
                    ghost = POLE_SIGNS[c] * lanes(pole, -((c % 2) * 2 + z))
                    rate = rate + jnp.where(lane < KR, lanes(filtered[c // 2], -offset), 0.0)
                    rate = rate + jnp.where(lane == 0, 0.5 * u[0] * ghost, 0.0)
                rates[c][z][h] = jnp.concatenate(
                    [rate[:8] + halos[0][c], rate[8 : TH - 8], rate[TH - 8 :] + halos[1][c]], axis=0
                )
    return rates


def viscosity_blocks(inp, out):
    nu_s = out.vmem("nu")
    nu_s[...] = inp("nu")[...].astype(f32)
    return [[nu_s[strided(0, z, h), :] for h in range(2)] for z in range(2)]


def magnetic_blocks(inp, out):
    mag_s = out.vmem("mag")
    mag_s[...] = inp("mag")[...].astype(f32)
    return [[[mag_s[strided(c, z, h), :] for h in range(2)] for z in range(2)] for c in range(3)]


def input_blocks(inp):
    vel_ref = inp("vel")
    return [[[vel_ref[strided(c, z, h), :] for h in range(2)] for z in range(2)] for c in range(3)]


def blocks(ref):
    return [[[ref[block(c, z, h), :] for h in range(2)] for z in range(2)] for c in range(3)]


def short_arrivals(edge_ref, cnt_ref, me, slab):
    lane = lane_iota((1, CAP))
    half = CAP // 2
    order = [(me + k) % SECT for k in (1, SECT - 1, 2, 3, 4, 5, 6)]

    def pick(get):
        full = [get(s, lane) for s in order[:2]]
        pairs = [
            jnp.where(lane < half, get(order[k], lane), pltpu.roll(get(order[k + 1], lane), half, 1)) for k in (2, 4)
        ]
        return jnp.concatenate(full + pairs + [jnp.where(lane < half, get(order[6], lane), 0.0)], axis=1)

    live = pick(lambda s, lane: (lane < cnt_ref[s, 0, me]).astype(f32))
    values = [pick(lambda s, lane, q=q: edge_ref[s, EDGE_PART + q : EDGE_PART + q + 1, :]) for q in range(6)]
    theta, r, z = [x.astype(i32) for x in values[3:]]
    row = jnp.where(live > 0.5, local_row(theta, r, z, me, slab), -1)
    return row, r % 128, values[:3]


def first_kernel(inp, out):
    me = lax.axis_index("az")
    slab = lax.axis_index("ax")
    row, col, velocity = short_arrivals(inp("edge"), inp("cnt"), me, slab)
    arrived = add_parts(deposit(row, col, velocity, 5 * CAP))
    filtered = filtered_inner(inp, me)
    sum_ref = inp("sums")
    total = [sum_ref[c * 256 : (c + 1) * 256, :] + arrived[c] for c in range(4)]
    nu, field = viscosity_blocks(inp, out), input_blocks(inp)
    rates = outer_rate(filtered, field, nu, inp, me, slab)
    local_ref = inp("local")
    mid_ref, rest_ref = out.vmem("mid"), out.vmem("rest")
    mid = [[[None, None], [None, None]] for _ in range(3)]
    for c in range(3):
        for z in range(2):
            for h in range(2):
                at = slice((z * 2 + h) * TH, (z * 2 + h + 1) * TH)
                x, s, n = field[c][z][h], total[c][at], total[3][at]
                u1 = x + DT * (local_ref[block(c, z, h), :] + rates[c][z][h] + 2.0 * (s - n * x))
                mid[c][z][h] = u1
                mid_ref[block(c, z, h), :] = u1
                rest_ref[block(c, z, h), :] = 0.5 * (x + u1) + DT * (0.8 * s + 0.2 * n * x - n * u1)
    out.send("mid")
    out.send("rest")
    write_message(out.vmem("inner"), out.vmem("edge"), mid, [nu[z][0] for z in range(2)], me)
    send_inner(out, ROW_EDGE)
    out.copy(out.vmem("edge"), out.hbm("msg").at[:, ROW_EDGE:, :])
    write_axial(out.vmem("one"), out.vmem("two"), mid, slab)
    out.send("one")
    out.send("two")


def take(pick, row, col, n):
    got = jnp.dot(pick, one_hot(row, 256, n), preferred_element_type=f32)
    got = got[:384] + got[384:]
    cols = row_iota((128, n)) == col
    return [jnp.sum(jnp.where(cols, got[c * 128 : (c + 1) * 128], 0.0), axis=0, keepdims=True) for c in range(3)]


def gather_kernel(inp, out):
    me = lax.axis_index("az")
    slab = lax.axis_index("ax")
    pc_ref, stay_ref, pv_ref = inp("pc"), inp("stay"), inp("pv")
    kept_ref, arr_ref = out.vmem("kept"), out.vmem("arrived")
    vel_ref, mid_ref = inp("vel"), inp("mid")
    parts = []
    for c in range(3):
        rows = []
        for z in range(2):
            for h in range(2):
                rows.append(0.08 * vel_ref[strided(c, z, h), :] + 0.1 * mid_ref[block(c, z, h), :])
        parts.append(split2(jnp.concatenate(rows, axis=0).T))
    pick = jnp.concatenate([p[0] for p in parts] + [p[1] for p in parts], axis=0)
    for k in range(NP // CHUNK):
        part = pl.ds(k * CHUNK, CHUNK)
        row = local_row(pc_ref[0:1, part], pc_ref[1:2, part], pc_ref[2:3, part], me, slab)
        stay = stay_ref[0:1, part] > 0.5
        row = jnp.where(stay, row, -1)
        got = take(pick, row, pc_ref[1:2, part] % 128, CHUNK)
        for c in range(3):
            kept_ref[c : c + 1, part] = jnp.where(stay, 0.82 * pv_ref[c : c + 1, part] + got[c], 0.0)
    out.send("kept")
    rates = local_rate(blocks(mid_ref), viscosity_blocks(inp, out), magnetic_blocks(inp, out))
    rest_ref, part_ref = inp("rest"), out.vmem("part")
    for c in range(3):
        for z in range(2):
            for h in range(2):
                part_ref[block(c, z, h), :] = rest_ref[block(c, z, h), :] + (0.5 * DT) * rates[c][z][h]
    out.send("part")
    live, row, col, velocity = arrivals(inp("edge"), inp("cnt"), me, slab)
    got = take(pick, row, col, SECT * CAP)
    for c in range(3):
        arr_ref[c, 0:1, :] = jnp.where(live > 0, 0.82 * velocity[c] + got[c], 0.0)
    out.send("arrived")


def second_kernel(inp, out):
    me = lax.axis_index("az")
    slab = lax.axis_index("ax")
    filtered = filtered_inner(inp, me)
    rates = outer_rate(filtered, blocks(inp("mid")), viscosity_blocks(inp, out), inp, me, slab)
    part_ref, new_ref = inp("part"), out.vmem("new")
    for c in range(3):
        for z in range(2):
            for h in range(2):
                new_ref[strided(c, z, h), :] = part_ref[block(c, z, h), :] + (0.5 * DT) * rates[c][z][h]
        rows = pl.ds(c * 256, 256)
        out.copy(new_ref.at[rows, :], out.hbm("new").at[rows, :])


def call(kernel, name, ins, outs, bufs, copies, flops=0, in_smem=()):
    in_names, out_names, buf_names = list(ins), list(outs), list(bufs)
    arrays = [ins[n] for n in in_names]
    n_in, n_out = len(in_names), len(out_names)

    def body(*refs):
        in_refs, refs = refs[:n_in], refs[n_in:]
        out_refs, refs = refs[:n_out], refs[n_out:]
        in_bufs, refs = refs[:n_in], refs[n_in:]
        buf_refs, (in_sems, out_sems) = refs[:-2], refs[-2:]
        out = Outputs(out_names, out_refs, dict(zip(buf_names, buf_refs)), out_sems)
        kernel(Inputs(in_names, in_refs, in_bufs, in_sems), out)
        out.finish()

    def in_shape(n):
        shape = ins[n].shape
        if n == "basis_t":
            return (2, TH, shape[2])
        return {"inner": (SECT, ROW_EDGE, 128), "edge": (SECT, shape[1] - ROW_EDGE, 128)}.get(n, shape)

    hbm = pl.BlockSpec(memory_space=pltpu.HBM)
    return pl.pallas_call(
        body,
        out_shape=[jax.ShapeDtypeStruct(*outs[n]) for n in out_names],
        in_specs=[hbm] * n_in,
        out_specs=[hbm] * n_out,
        scratch_shapes=[(pltpu.SMEM if n in in_smem else pltpu.VMEM)(in_shape(n), ins[n].dtype) for n in in_names]
        + [pltpu.VMEM(*bufs[n]) for n in buf_names]
        + [pltpu.SemaphoreType.DMA((n_in,)), pltpu.SemaphoreType.DMA((copies,))],
        compiler_params=pltpu.CompilerParams(vmem_limit_bytes=VMEM_LIMIT),
        cost_estimate=pl.CostEstimate(flops=flops, bytes_accessed=2 * 1024 * 1024, transcendentals=0),
        name=name,
    )(*arrays)


def rows_of(x):
    lead = x.shape[:-2]
    x = x.reshape(*lead, 2, 2, 128)
    return jnp.swapaxes(x, -3, -2).reshape(-1, 128)


def per_device(velocity, viscosity, bfield, particle_velocity, particle_cell, send_rows, send_counts):
    ax = lax.axis_size("ax")
    vel, nu, mag = rows_of(velocity), rows_of(viscosity), rows_of(bfield)
    pv, pc = particle_velocity, particle_cell
    tables = {"basis": jnp.asarray(BASIS), "weight": jnp.asarray(MODE_WEIGHT), "basis_t": jnp.asarray(BASIS_T)}
    swap_one = [(i, i ^ 1) for i in range(ax)]
    swap_two = []
    for a in range(SECT):
        swap_two += [(a * ax + i, a * ax + ((i + 1) ^ 1) - 1) for i in range(1, ax - 1)]
        swap_two += [(a * ax + i, (a ^ 2) * ax + i) for i in (0, ax - 1)]

    def swap(one, two):
        return lax.ppermute(one, "ax", swap_one), lax.ppermute(two, ("az", "ax"), swap_two)

    def to_all(msg):
        return lax.all_to_all(msg, "az", split_axis=0, concat_axis=0, tiled=True)

    face = ((384, 128), f32)
    field = ((768, 128), f32)
    materials = {"nu": ((256, 128), f32), "mag": field}
    msg, one, two, stay = call(
        pack_kernel,
        "pack",
        {"vel": vel, "nu": nu, "pc": pc, "pv": pv, "rows": send_rows, "cnt": send_counts},
        {"msg": ((SECT, ROW_EDGE + EDGE1, 128), f32), "one": face, "two": face, "stay": ((1, NP), f32)},
        {
            "inner": ((ROW_EDGE, 128), f32),
            "one": face,
            "two": face,
            "edge": ((SECT, EDGE1, 128), f32),
            "stay": ((1, NP), f32),
            "tmp": ((1024, 128), f32),
            "nu": ((256, 128), f32),
        },
        12,
        in_smem=("cnt",),
    )
    one, two = swap(one, two)
    recv = to_all(msg)
    sums, local = call(
        scatter_kernel,
        "deposit",
        {"pc": pc, "stay": stay, "pv": pv, "vel": vel, "nu": nu, "mag": mag},
        {"sums": ((1024, 128), f32), "local": field},
        {"sums": ((1024, 128), f32), "acc": ((256, 896), f32), "local": field} | materials,
        2,
        flops=2 * NP * 256 * 896,
    )
    msg2, one2, two2, mid, rest = call(
        first_kernel,
        "first_section",
        {"edge": recv, "inner": recv, "cnt": send_counts, "basis": tables["basis"], "sums": sums, "nu": nu, "vel": vel}
        | tables
        | {"one": one, "two": two, "local": local},
        {"msg": ((SECT, ROW_EDGE + EDGE2, 128), f32), "one": face, "two": face, "mid": field, "rest": field},
        {
            "inner": ((ROW_EDGE, 128), f32),
            "edge": ((SECT, EDGE2, 128), f32),
            "one": face,
            "two": face,
            "mid": field,
            "rest": field,
            "nu": ((256, 128), f32),
        },
        13,
        in_smem=("cnt",),
    )
    one2, two2 = swap(one2, two2)
    recv2 = to_all(msg2)
    kept, arrived, part = call(
        gather_kernel,
        "take",
        {"vel": vel, "mid": mid, "pc": pc, "stay": stay, "pv": pv, "nu": nu, "mag": mag, "rest": rest}
        | {"edge": recv, "cnt": send_counts},
        {"kept": ((3, NP), f32), "arrived": ((3, 1, SECT * CAP), f32), "part": field},
        {"kept": ((3, NP), f32), "arrived": ((3, 1, SECT * CAP), f32), "part": field} | materials,
        3,
        flops=2 * NP * 512 * 384,
        in_smem=("cnt",),
    )
    (new,) = call(
        second_kernel,
        "second_section",
        {"edge": recv2, "inner": recv2} | tables | { "mid": mid, "nu": nu, "one": one2, "two": two2, "part": part},
        {"new": field},
        {"nu": ((256, 128), f32), "new": field},
        3,
    )
    new = jnp.swapaxes(new.reshape(3, TH, 2, 2, 128), 2, 3).reshape(3, TH, 2, NR)
    return new, kept, jnp.swapaxes(arrived, 0, 1)


def solution(mesh):
    return jax.shard_map(
        per_device,
        mesh=mesh,
        in_specs=(
            P(None, "az", "ax", None),
            P("az", "ax", None),
            P(None, "az", "ax", None),
            P(None, ("az", "ax")),
            P(None, ("az", "ax")),
            P(("az", "ax"), None, None),
            P(None, "ax", None),
        ),
        out_specs=(P(None, "az", "ax", None), P(None, ("az", "ax")), P(("az", "ax"), None, None)),
        check_vma=False,
    )
```

```python
import math

import jax
import jax.numpy as jnp
import numpy as np
from jax import lax
from jax.experimental import pallas as pl
from jax.experimental.pallas import tpu as pltpu
from jax.sharding import PartitionSpec as P

NA = 512
NR = 256
KR = 32
SECT = 8
TH = NA // SECT
CAP = 128
NP = 8192
DTHETA = 2.0 * math.pi / NA
DT = 0.02
POLE_SIGNS = (-1.0, -1.0, 1.0)
HIGHEST = lax.Precision.HIGHEST
f32 = jnp.float32
bf16 = jnp.bfloat16
i32 = jnp.int32
VMEM_LIMIT = 65408 * 1024

ROW_B = 64
ROW_EDGE = 96
EDGE_BOUND = 12
EDGE_PART = 16
EDGE1 = 24
EDGE2 = 16
CHUNK = 1024


def filter_tables():
    a = np.arange(NA // 2)
    even, odd, even_mode, odd_mode = [], [], [], []
    for m in range(NA // 2 + 1):
        scale = math.sqrt((1.0 if m in (0, NA // 2) else 2.0) / NA)
        phase = 2.0 * math.pi * (m * a % NA) / NA
        rows = [scale * np.cos(phase)]
        if m not in (0, NA // 2):
            rows.append(scale * np.sin(phase))
        for row in rows:
            (odd if m % 2 else even).append(row)
            (odd_mode if m % 2 else even_mode).append(m)
    basis = np.stack([np.stack(even), np.stack(odd)]).astype(np.float32)
    modes = np.stack([np.array(even_mode), np.array(odd_mode)]).astype(np.float64)
    cutoff = 4.0 * (np.arange(KR) + 0.5)
    weight = 1.0 / (1.0 + (modes[:, :, None] / cutoff) ** 4)
    weight = np.tile(weight, (1, 1, 128 // KR)).astype(np.float32)
    return basis, np.ascontiguousarray(basis.transpose(0, 2, 1)), weight


BASIS, BASIS_T, MODE_WEIGHT = filter_tables()


def lane_iota(shape):
    return lax.broadcasted_iota(i32, shape, len(shape) - 1)


def row_iota(shape):
    return lax.broadcasted_iota(i32, shape, len(shape) - 2)


def strided(c, z, h):
    return pl.ds(c * 256 + h * 2 + z, TH, stride=4)


def block(c, z, h):
    return pl.ds(((c * 2 + z) * 2 + h) * TH, TH)


def lanes(x, by):
    by %= 128
    return x if by == 0 else pltpu.roll(x, by, 1)


def split2(x):
    hi = x.astype(bf16)
    return hi, (x - hi.astype(f32)).astype(bf16)


def pack_inner(field, nu):
    lane = lane_iota((TH, 128))

    def four(p, q, r, s):
        low = jnp.where(lane < 32, p, lanes(q, 32))
        high = jnp.where(lane < 96, lanes(r, 64), lanes(s, 96))
        return jnp.where(lane < 64, low, high)

    first = four(field[0][0][0], field[0][1][0], field[1][0][0], field[1][1][0])
    second = four(field[2][0][0], field[2][1][0], nu[0], nu[1])
    return first, second


def azimuth_factors():
    lane = lane_iota((1, 128))
    radius = (lane % KR).astype(f32) + 0.5
    lap = 1.0 / (radius * radius * (DTHETA * DTHETA))
    grad = 1.0 / (2.0 * DTHETA * radius)
    return lane < 64, lap, grad, jnp.where(lane < 64, -2.0, 2.0) / radius


def both_halves(x, left):
    side = lane_iota((1, 128)) < 64
    return jnp.where(side == left, x, pltpu.roll(x, 64, 1))


def azimuth_inner(first, second):
    left, lap_factor, grad_factor, cross = azimuth_factors()
    row = row_iota((TH, 128))
    nu, swirl = both_halves(second, False), both_halves(first, False)

    def differences(x):
        after = jnp.where(row == TH - 1, 0.0, pltpu.roll(x, TH - 1, 0))
        before = jnp.where(row == 0, 0.0, pltpu.roll(x, 1, 0))
        return (after - 2.0 * x + before) * lap_factor, (after - before) * grad_factor

    lap, grad = differences(first)
    part_first = nu * lap - swirl * grad + cross * nu * pltpu.roll(grad, 64, 1)
    lap, grad = differences(second)
    return part_first, jnp.where(left, nu * lap - swirl * grad, 0.0)


def write_message(inner_ref, edge_ref, field, nu, me):
    first, second = pack_inner(field, nu)
    part_first, part_second = azimuth_inner(first, second)
    inner_ref[0:TH, :] = part_first
    inner_ref[TH:, :] = part_second[: TH // 2] + pltpu.roll(part_second[TH // 2 :], 64, 1)
    turned = jnp.concatenate([first, second], axis=0).T
    up, opposite = (me + 1) % SECT, (me + SECT // 2) % SECT
    bounds = [first[0:1], second[0:1], first[TH - 1 : TH], second[TH - 1 : TH]]
    for t in range(SECT):
        for k in range(4):
            edge_ref[t, EDGE_BOUND + k : EDGE_BOUND + k + 1, :] = bounds[k]
    for c in range(3):
        for z in range(2):
            for h in range(2):
                x = field[c][z][h]
                row = (c * 2 + z) * 2 + h
                for t in range(SECT):
                    edge = jnp.where(t == up, x[TH - 1 : TH], x[0:1])
                    if row < 4:
                        edge = jnp.where(t == opposite, turned[row * 32 : row * 32 + 1], edge)
                    edge_ref[t, row : row + 1, :] = edge


def send_inner(out, rows):
    for t in range(SECT):
        out.copy(out.vmem("inner"), out.hbm("msg").at[t, 0:rows, :])


def write_axial(one_ref, two_ref, field, slab):
    odd = slab % 2 == 1
    for c in range(3):
        for h in range(2):
            rows = pl.ds((c * 2 + h) * TH, TH)
            low, high = field[c][0][h], field[c][1][h]
            one_ref[rows, :] = jnp.where(odd, low, high)
            two_ref[rows, :] = jnp.where(odd, high, low)


class Inputs:
    def __init__(self, names, refs, bufs, sems):
        self.refs = dict(zip(names, bufs))
        self.copies = {}
        for i, (name, ref, buf) in enumerate(zip(names, refs, bufs)):
            if name == "inner":
                ref = ref.at[:, 0:ROW_EDGE, :]
            if name == "edge":
                ref = ref.at[:, ROW_EDGE:, :]
            if name == "basis_t":
                own = lax.axis_index("az") % 4
                ref = ref.at[:, pl.ds(pl.multiple_of(own * TH, TH), TH), :]
            self.copies[name] = [pltpu.make_async_copy(ref, buf, sems.at[i])]
            self.copies[name][0].start()

    def __call__(self, name):
        for copy in self.copies.pop(name, ()):
            copy.wait()
        return self.refs[name]


class Outputs:
    def __init__(self, names, refs, bufs, sems):
        self.refs, self.bufs, self.sems, self.started = dict(zip(names, refs)), bufs, sems, []

    def hbm(self, name):
        return self.refs[name]

    def vmem(self, name):
        return self.bufs[name]

    def copy(self, src, dst):
        copy = pltpu.make_async_copy(src, dst, self.sems.at[len(self.started)])
        copy.start()
        self.started.append(copy)

    def send(self, name):
        self.copy(self.bufs[name], self.refs[name])

    def finish(self):
        for copy in self.started:
            copy.wait()


def pack_kernel(inp, out):
    me = lax.axis_index("az")
    tmp_ref, nu_s, edge_ref = out.vmem("tmp"), out.vmem("nu"), out.vmem("edge")
    vel_ref, nu_ref = inp("vel"), inp("nu")
    field = [[[vel_ref[strided(c, z, h), :] for h in range(2)] for z in range(2)] for c in range(3)]
    nu_s[...] = nu_ref[...].astype(f32)
    nu = [nu_s[pl.ds(z, TH, stride=4), :] for z in range(2)]
    write_message(out.vmem("inner"), edge_ref, field, nu, me)
    send_inner(out, ROW_EDGE)
    write_axial(out.vmem("one"), out.vmem("two"), field, lax.axis_index("ax"))
    out.send("one")
    out.send("two")
    pv_ref, pc_ref = inp("pv"), inp("pc")
    for i in range(64):
        tmp_ref[i * 8 : i * 8 + 3, :] = pv_ref[:, i * 128 : (i + 1) * 128]
        tmp_ref[512 + i * 8 : 512 + i * 8 + 3, :] = pc_ref[:, i * 128 : (i + 1) * 128].astype(f32)
    parts = []
    for k in range(2):
        for c in range(3):
            parts.append(jnp.concatenate(split2(tmp_ref[pl.ds(k * 512 + c, 64, stride=8), :]), axis=1))
    rows_ref = inp("rows")
    listed = [rows_ref[0, t : t + 1, :] for t in range(SECT)]
    low = jnp.concatenate([one_hot(row % 128, 128, 128) for row in listed], axis=1)
    high = [row_iota((64, 128)) == row // 128 for row in listed]
    picked = jnp.dot(
        jnp.concatenate(parts, axis=0), jnp.concatenate([low, low], axis=0), preferred_element_type=f32
    )
    for t in range(SECT):
        for q in range(6):
            value = picked[q * 64 : (q + 1) * 64, t * 128 : (t + 1) * 128]
            edge_ref[t, EDGE_PART + q : EDGE_PART + q + 1, :] = jnp.sum(
                jnp.where(high[t], value, 0.0), axis=0, keepdims=True
            )
    out.copy(edge_ref, out.hbm("msg").at[:, ROW_EDGE:, :])


def local_row(theta, r, z, me, slab):
    return ((z - 2 * slab) * 2 + r // 128) * TH + theta - me * TH


def spread(x, rows, n):
    tile = jnp.broadcast_to(x, (16, n)).astype(bf16)
    return jnp.concatenate([tile] * (rows // 16), axis=0)


def matches(index, rows, n):
    return row_iota((rows, n)).astype(f32).astype(bf16) == spread(index.astype(f32), rows, n)


def one_hot(index, rows, n):
    return jnp.where(matches(index, rows, n), jnp.ones((), bf16), jnp.zeros((), bf16))


def deposit(row, col, velocity, n):
    cols = matches(col, 128, n)
    pieces = []
    for c in range(3):
        for part in split2(velocity[c]):
            pieces.append(jnp.where(cols, spread(part.astype(f32), 128, n), jnp.zeros((), bf16)))
    pieces.append(one_hot(col, 128, n))
    return lax.dot_general(
        one_hot(row, 256, n), jnp.concatenate(pieces, axis=0), (((1,), (1,)), ((), ())), preferred_element_type=f32
    )


def add_parts(acc):
    out = [acc[:, c * 256 : c * 256 + 128] + acc[:, c * 256 + 128 : c * 256 + 256] for c in range(3)]
    out.append(acc[:, 768:896])
    return out


def write_blocks(ref, x):
    for c in range(3):
        for z in range(2):
            for h in range(2):
                ref[block(c, z, h), :] = x[c][z][h]


def write_stay(stay_ref, rows_ref, cnt_ref, me):
    lane = lane_iota((1, 128))
    lows, highs = [], []
    for t in range(SECT):
        row = rows_ref[0, t : t + 1, :]
        used = (row_iota((64, 128)) == row // 128) & (lane < cnt_ref[me, 0, t])
        highs.append(used.astype(f32).astype(bf16))
        lows.append(one_hot(row % 128, 128, 128))
    leaving = lax.dot_general(
        jnp.concatenate(highs, axis=1),
        jnp.concatenate(lows, axis=1),
        (((1,), (1,)), ((), ())),
        preferred_element_type=f32,
    )
    stay = 1.0 - leaving
    for i in range(64):
        stay_ref[0:1, i * 128 : (i + 1) * 128] = stay[i : i + 1, :]


def scatter_kernel(inp, out):
    me = lax.axis_index("az")
    slab = lax.axis_index("ax")
    stay_ref = out.vmem("stay")
    write_stay(stay_ref, inp("rows"), inp("cnt"), me)
    out.send("stay")
    pc_ref, pv_ref = inp("pc"), inp("pv")
    sum_ref, acc_ref = out.vmem("sums"), out.vmem("acc")
    for k in range(NP // CHUNK):
        part = pl.ds(k * CHUNK, CHUNK)
        row = local_row(pc_ref[0:1, part], pc_ref[1:2, part], pc_ref[2:3, part], me, slab)
        row = jnp.where(stay_ref[0:1, part] > 0.5, row, -1)
        col = pc_ref[1:2, part] % 128
        more = deposit(row, col, [pv_ref[c : c + 1, part] for c in range(3)], CHUNK)
        if k == 0:
            acc_ref[...] = more
        else:
            acc_ref[...] += more
    for c, x in enumerate(add_parts(acc_ref)):
        sum_ref[c * 256 : (c + 1) * 256, :] = x
    out.send("sums")
    rates = local_rate(input_blocks(inp), viscosity_blocks(inp, out), magnetic_blocks(inp, out))
    write_blocks(out.vmem("local"), rates)
    out.send("local")


def arrivals(edge_ref, cnt_ref, me, slab):
    lane = lane_iota((1, CAP))
    live = jnp.concatenate([(lane < cnt_ref[s, 0, me]).astype(i32) for s in range(SECT)], axis=1)

    def channel(q):
        return jnp.concatenate([edge_ref[s, EDGE_PART + q : EDGE_PART + q + 1, :] for s in range(SECT)], axis=1)

    velocity = [channel(c) for c in range(3)]
    theta, r, z = [channel(3 + c).astype(i32) for c in range(3)]
    row = jnp.where(live > 0, local_row(theta, r, z, me, slab), -1)
    return live, row, r % 128, velocity


def whole_azimuth_part(inp):
    recv_ref, edge_ref = inp("inner"), inp("edge")
    left, lap_factor, grad_factor, cross = azimuth_factors()
    bounds = []
    for k in range(4):
        at = EDGE_BOUND + k
        bounds.append(jnp.concatenate([edge_ref[t, at : at + 1, :] for t in range(SECT)], axis=0))

    def share(near, far, sign):
        nu, swirl = both_halves(near[1], False), both_halves(near[0], False)
        factor = nu * lap_factor - sign * swirl * grad_factor
        turn = cross * nu * pltpu.roll(sign * far[0] * grad_factor, 64, 1)
        return factor * far[0] + turn, jnp.where(left, factor * far[1], 0.0)

    begin, end = bounds[:2], bounds[2:]
    at_begin = share(begin, [pltpu.roll(x, 1, 0) for x in end], -1.0)
    at_end = share(end, [pltpu.roll(x, SECT - 1, 0) for x in begin], 1.0)
    row = row_iota((8, 128))
    out = ([], [])
    for t in range(SECT):
        folded = recv_ref[t, ROW_B : ROW_B + TH // 2, :]
        second = jnp.concatenate([folded, pltpu.roll(folded, 64, 1)], axis=0)
        for k, x in enumerate((recv_ref[t, 0:TH, :], jnp.where(left, second, 0.0))):
            out[k].append(x[:8] + jnp.where(row == 0, at_begin[k][t : t + 1], 0.0))
            out[k].append(x[8 : TH - 8])
            out[k].append(x[TH - 8 :] + jnp.where(row == 7, at_end[k][t : t + 1], 0.0))
    return jnp.concatenate(out[0], axis=0), jnp.concatenate(out[1], axis=0)


def filtered_inner(inp, me):
    part = jnp.concatenate(whole_azimuth_part(inp), axis=1)
    low, high = part[: NA // 2], part[NA // 2 :]
    basis_ref, weight_ref, basis_t_ref = inp("basis"), inp("weight"), inp("basis_t")
    out = 0.0
    for parity, x in enumerate((low + high, low - high)):
        spectrum = jnp.dot(basis_ref[parity], x, precision=HIGHEST, preferred_element_type=f32)
        weight = weight_ref[parity]
        spectrum = spectrum * jnp.concatenate([weight, weight], axis=1)
        back = jnp.dot(basis_t_ref[parity], spectrum, precision=HIGHEST, preferred_element_type=f32)
        if parity:
            back = jnp.where(me < 4, back, -back)
        out = out + back
    return out[:, :128], out[:, 128:]


def local_rate(field, nu, magnetic):
    lane = lane_iota((TH, 128))
    row = row_iota((TH, 128))
    rates = [[[None, None], [None, None]] for _ in range(3)]
    for z in range(2):
        rolled = [[(pltpu.roll(field[c][z][h], 1, 1), pltpu.roll(field[c][z][h], 127, 1)) for h in range(2)] for c in range(3)]
        for h in range(2):
            radius = lane_iota((1, 128)).astype(f32) + (h * 128 + 0.5)
            inverse = 1.0 / radius
            eddy = nu[z][h]
            u = [field[c][z][h] for c in range(3)]
            lap_ax, lap_rad, grad_rad, grad_ax, lap_th, grad_th = [], [], [], [], [], []
            for c in range(3):
                x = u[c]
                if h == 0:
                    prev_r = jnp.where(lane == 0, 0.0, rolled[c][0][0])
                    next_r = jnp.where(lane == 127, rolled[c][1][1], rolled[c][0][1])
                else:
                    prev_r = jnp.where(lane == 0, rolled[c][0][0], rolled[c][1][0])
                    next_r = jnp.where(lane == 127, 0.0, rolled[c][1][1])
                other = field[c][1 - z][h]
                prev_t = jnp.where(row == 0, 0.0, pltpu.roll(x, 1, 0))
                next_t = jnp.where(row == TH - 1, 0.0, pltpu.roll(x, TH - 1, 0))
                lap_rad.append(((radius + 0.5) * (next_r - x) - (radius - 0.5) * (x - prev_r)) * inverse)
                lap_ax.append(other - 2.0 * x)
                grad_rad.append(0.5 * (next_r - prev_r))
                grad_ax.append((0.5 if z == 0 else -0.5) * other)
                lap_th.append((next_t - 2.0 * x + prev_t) * (1.0 / (radius * radius * (DTHETA * DTHETA))))
                grad_th.append((next_t - prev_t) * (1.0 / (2.0 * DTHETA * radius)))
            b = [magnetic[c][z][h] for c in range(3)]
            slip = [-u[0], radius * (2.0 / NR) - u[1], -u[2]]
            current = [slip[1] * b[2] - slip[2] * b[1], slip[2] * b[0] - slip[0] * b[2], slip[0] * b[1] - slip[1] * b[0]]
            force = [
                current[1] * b[2] - current[2] * b[1],
                current[2] * b[0] - current[0] * b[2],
                current[0] * b[1] - current[1] * b[0],
            ]
            inverse2 = inverse * inverse
            metric = [
                u[1] * u[1] * inverse - eddy * u[0] * inverse2,
                -eddy * u[1] * inverse2 - u[0] * u[1] * inverse,
                0.0,
            ]
            coupling = [-2.0 * eddy * grad_th[1] * inverse, 2.0 * eddy * grad_th[0] * inverse, 0.0]
            for c in range(3):
                azimuth = eddy * lap_th[c] - u[1] * grad_th[c] + coupling[c]
                if h == 0:
                    azimuth = jnp.where(lane < KR, 0.0, azimuth)
                rates[c][z][h] = (
                    eddy * (lap_rad[c] + lap_ax[c])
                    - (u[0] * grad_rad[c] + u[2] * grad_ax[c])
                    + metric[c]
                    + 0.5 * force[c]
                    + azimuth
                )
    return rates


def outer_rate(filtered, field, nu, inp, me, slab):
    edge_ref, one_ref, two_ref = inp("edge"), inp("one"), inp("two")
    before_sector = (me + SECT - 1) % SECT
    after_sector = (me + 1) % SECT
    opposite = (me + SECT // 2) % SECT
    odd = slab % 2 == 1
    lane = lane_iota((TH, 128))
    row = row_iota((8, 128))
    turned = jnp.concatenate([edge_ref[opposite, 0:8, :], jnp.zeros((120, 128), f32)], axis=0).T
    rates = [[[None, None], [None, None]] for _ in range(3)]
    for z in range(2):
        for h in range(2):
            radius = lane_iota((1, 128)).astype(f32) + (h * 128 + 0.5)
            lap_factor = 1.0 / (radius * radius * (DTHETA * DTHETA))
            grad_factor = 1.0 / (2.0 * DTHETA * radius)
            cross = 2.0 * grad_factor / radius
            eddy, u = nu[z][h], [field[c][z][h] for c in range(3)]
            by_face = eddy + (0.5 if z == 0 else -0.5) * u[2]
            end = slab == (0 if z == 0 else lax.axis_size("ax") - 1)
            halos = []
            for sector, at, sign in ((before_sector, slice(0, 8), -1.0), (after_sector, slice(TH - 8, TH), 1.0)):
                f = [edge_ref[sector, (c * 2 + z) * 2 + h : (c * 2 + z) * 2 + h + 1, :] for c in range(3)]
                nu8, swirl8 = eddy[at], u[1][at]
                by_halo = nu8 * lap_factor - sign * swirl8 * grad_factor
                extra = [-sign * cross * nu8 * f[1], sign * cross * nu8 * f[0], 0.0]
                keep = row == (0 if sign < 0 else 7)
                if h == 0:
                    keep = keep & (lane_iota((8, 128)) >= KR)
                halos.append([jnp.where(keep, by_halo * f[c] + extra[c], 0.0) for c in range(3)])
            for c in range(3):
                face = pl.ds((c * 2 + h) * TH, TH)
                one, two = one_ref[face, :], two_ref[face, :]
                face = jnp.where(odd, one, two) if z == 0 else jnp.where(odd, two, one)
                rate = jnp.where(end, 0.0, face) * by_face
                if h == 0:
                    offset = (c % 2) * 64 + z * 32
                    pole = turned[TH:] if c == 2 else turned[:TH]
                    ghost = POLE_SIGNS[c] * lanes(pole, -((c % 2) * 2 + z))
                    rate = rate + jnp.where(lane < KR, lanes(filtered[c // 2], -offset), 0.0)
                    rate = rate + jnp.where(lane == 0, 0.5 * u[0] * ghost, 0.0)
                rates[c][z][h] = jnp.concatenate(
                    [rate[:8] + halos[0][c], rate[8 : TH - 8], rate[TH - 8 :] + halos[1][c]], axis=0
                )
    return rates


def viscosity_blocks(inp, out):
    nu_s = out.vmem("nu")
    nu_s[...] = inp("nu")[...].astype(f32)
    return [[nu_s[strided(0, z, h), :] for h in range(2)] for z in range(2)]


def magnetic_blocks(inp, out):
    mag_s = out.vmem("mag")
    mag_s[...] = inp("mag")[...].astype(f32)
    return [[[mag_s[strided(c, z, h), :] for h in range(2)] for z in range(2)] for c in range(3)]


def input_blocks(inp):
    vel_ref = inp("vel")
    return [[[vel_ref[strided(c, z, h), :] for h in range(2)] for z in range(2)] for c in range(3)]


def blocks(ref):
    return [[[ref[block(c, z, h), :] for h in range(2)] for z in range(2)] for c in range(3)]


def short_arrivals(edge_ref, cnt_ref, me, slab):
    lane = lane_iota((1, CAP))
    half = CAP // 2
    order = [(me + k) % SECT for k in (1, SECT - 1, 2, 3, 4, 5, 6)]

    def pick(get):
        full = [get(s, lane) for s in order[:2]]
        pairs = [
            jnp.where(lane < half, get(order[k], lane), pltpu.roll(get(order[k + 1], lane), half, 1)) for k in (2, 4)
        ]
        return jnp.concatenate(full + pairs + [jnp.where(lane < half, get(order[6], lane), 0.0)], axis=1)

    live = pick(lambda s, lane: (lane < cnt_ref[s, 0, me]).astype(f32))
    values = [pick(lambda s, lane, q=q: edge_ref[s, EDGE_PART + q : EDGE_PART + q + 1, :]) for q in range(6)]
    theta, r, z = [x.astype(i32) for x in values[3:]]
    row = jnp.where(live > 0.5, local_row(theta, r, z, me, slab), -1)
    return row, r % 128, values[:3]


def first_kernel(inp, out):
    me = lax.axis_index("az")
    slab = lax.axis_index("ax")
    row, col, velocity = short_arrivals(inp("edge"), inp("cnt"), me, slab)
    arrived = add_parts(deposit(row, col, velocity, 5 * CAP))
    filtered = filtered_inner(inp, me)
    sum_ref = inp("sums")
    total = [sum_ref[c * 256 : (c + 1) * 256, :] + arrived[c] for c in range(4)]
    nu, field = viscosity_blocks(inp, out), input_blocks(inp)
    rates = outer_rate(filtered, field, nu, inp, me, slab)
    local_ref = inp("local")
    mid_ref, rest_ref = out.vmem("mid"), out.vmem("rest")
    mid = [[[None, None], [None, None]] for _ in range(3)]
    for c in range(3):
        for z in range(2):
            for h in range(2):
                at = slice((z * 2 + h) * TH, (z * 2 + h + 1) * TH)
                x, s, n = field[c][z][h], total[c][at], total[3][at]
                u1 = x + DT * (local_ref[block(c, z, h), :] + rates[c][z][h] + 2.0 * (s - n * x))
                mid[c][z][h] = u1
                mid_ref[block(c, z, h), :] = u1
                rest_ref[block(c, z, h), :] = 0.5 * (x + u1) + DT * (0.8 * s + 0.2 * n * x - n * u1)
    out.send("mid")
    out.send("rest")
    write_message(out.vmem("inner"), out.vmem("edge"), mid, [nu[z][0] for z in range(2)], me)
    send_inner(out, ROW_EDGE)
    out.copy(out.vmem("edge"), out.hbm("msg").at[:, ROW_EDGE:, :])
    write_axial(out.vmem("one"), out.vmem("two"), mid, slab)
    out.send("one")
    out.send("two")


def take(pick, row, col, n):
    got = jnp.dot(pick, one_hot(row, 256, n), preferred_element_type=f32)
    got = got[:384] + got[384:]
    cols = row_iota((128, n)) == col
    return [jnp.sum(jnp.where(cols, got[c * 128 : (c + 1) * 128], 0.0), axis=0, keepdims=True) for c in range(3)]


def gather_kernel(inp, out):
    me = lax.axis_index("az")
    slab = lax.axis_index("ax")
    pc_ref, stay_ref, pv_ref = inp("pc"), inp("stay"), inp("pv")
    kept_ref, arr_ref = out.vmem("kept"), out.vmem("arrived")
    vel_ref, mid_ref = inp("vel"), inp("mid")
    parts = []
    for c in range(3):
        rows = []
        for z in range(2):
            for h in range(2):
                rows.append(0.08 * vel_ref[strided(c, z, h), :] + 0.1 * mid_ref[block(c, z, h), :])
        parts.append(split2(jnp.concatenate(rows, axis=0).T))
    pick = jnp.concatenate([p[0] for p in parts] + [p[1] for p in parts], axis=0)
    for k in range(NP // CHUNK):
        part = pl.ds(k * CHUNK, CHUNK)
        row = local_row(pc_ref[0:1, part], pc_ref[1:2, part], pc_ref[2:3, part], me, slab)
        stay = stay_ref[0:1, part] > 0.5
        row = jnp.where(stay, row, -1)
        got = take(pick, row, pc_ref[1:2, part] % 128, CHUNK)
        for c in range(3):
            kept_ref[c : c + 1, part] = jnp.where(stay, 0.82 * pv_ref[c : c + 1, part] + got[c], 0.0)
    out.send("kept")
    rates = local_rate(blocks(mid_ref), viscosity_blocks(inp, out), magnetic_blocks(inp, out))
    rest_ref, part_ref = inp("rest"), out.vmem("part")
    for c in range(3):
        for z in range(2):
            for h in range(2):
                part_ref[block(c, z, h), :] = rest_ref[block(c, z, h), :] + (0.5 * DT) * rates[c][z][h]
    out.send("part")
    live, row, col, velocity = arrivals(inp("edge"), inp("cnt"), me, slab)
    got = take(pick, row, col, SECT * CAP)
    for c in range(3):
        arr_ref[c, 0:1, :] = jnp.where(live > 0, 0.82 * velocity[c] + got[c], 0.0)
    out.send("arrived")


def second_kernel(inp, out):
    me = lax.axis_index("az")
    slab = lax.axis_index("ax")
    filtered = filtered_inner(inp, me)
    rates = outer_rate(filtered, blocks(inp("mid")), viscosity_blocks(inp, out), inp, me, slab)
    part_ref, new_ref = inp("part"), out.vmem("new")
    for c in range(3):
        for z in range(2):
            for h in range(2):
                new_ref[strided(c, z, h), :] = part_ref[block(c, z, h), :] + (0.5 * DT) * rates[c][z][h]
        rows = pl.ds(c * 256, 256)
        out.copy(new_ref.at[rows, :], out.hbm("new").at[rows, :])


def call(kernel, name, ins, outs, bufs, copies, flops=0, in_smem=()):
    in_names, out_names, buf_names = list(ins), list(outs), list(bufs)
    arrays = [ins[n] for n in in_names]
    n_in, n_out = len(in_names), len(out_names)

    def body(*refs):
        in_refs, refs = refs[:n_in], refs[n_in:]
        out_refs, refs = refs[:n_out], refs[n_out:]
        in_bufs, refs = refs[:n_in], refs[n_in:]
        buf_refs, (in_sems, out_sems) = refs[:-2], refs[-2:]
        out = Outputs(out_names, out_refs, dict(zip(buf_names, buf_refs)), out_sems)
        kernel(Inputs(in_names, in_refs, in_bufs, in_sems), out)
        out.finish()

    def in_shape(n):
        shape = ins[n].shape
        if n == "basis_t":
            return (2, TH, shape[2])
        return {"inner": (SECT, ROW_EDGE, 128), "edge": (SECT, shape[1] - ROW_EDGE, 128)}.get(n, shape)

    hbm = pl.BlockSpec(memory_space=pltpu.HBM)
    return pl.pallas_call(
        body,
        out_shape=[jax.ShapeDtypeStruct(*outs[n]) for n in out_names],
        in_specs=[hbm] * n_in,
        out_specs=[hbm] * n_out,
        scratch_shapes=[(pltpu.SMEM if n in in_smem else pltpu.VMEM)(in_shape(n), ins[n].dtype) for n in in_names]
        + [pltpu.VMEM(*bufs[n]) for n in buf_names]
        + [pltpu.SemaphoreType.DMA((n_in,)), pltpu.SemaphoreType.DMA((copies,))],
        compiler_params=pltpu.CompilerParams(vmem_limit_bytes=VMEM_LIMIT),
        cost_estimate=pl.CostEstimate(flops=flops, bytes_accessed=2 * 1024 * 1024, transcendentals=0),
        name=name,
    )(*arrays)


def rows_of(x):
    lead = x.shape[:-2]
    x = x.reshape(*lead, 2, 2, 128)
    return jnp.swapaxes(x, -3, -2).reshape(-1, 128)


def per_device(velocity, viscosity, bfield, particle_velocity, particle_cell, send_rows, send_counts):
    ax = lax.axis_size("ax")
    vel, nu, mag = rows_of(velocity), rows_of(viscosity), rows_of(bfield)
    pv, pc = particle_velocity, particle_cell
    tables = {"basis": jnp.asarray(BASIS), "weight": jnp.asarray(MODE_WEIGHT), "basis_t": jnp.asarray(BASIS_T)}
    swap_one = [(i, i ^ 1) for i in range(ax)]
    swap_two = []
    for a in range(SECT):
        swap_two += [(a * ax + i, a * ax + ((i + 1) ^ 1) - 1) for i in range(1, ax - 1)]
        swap_two += [(a * ax + i, (a ^ 2) * ax + i) for i in (0, ax - 1)]

    def swap(one, two):
        return lax.ppermute(one, "ax", swap_one), lax.ppermute(two, ("az", "ax"), swap_two)

    def to_all(msg):
        return lax.all_to_all(msg, "az", split_axis=0, concat_axis=0, tiled=True)

    face = ((384, 128), f32)
    field = ((768, 128), f32)
    materials = {"nu": ((256, 128), f32), "mag": field}
    msg, one, two = call(
        pack_kernel,
        "pack",
        {"vel": vel, "nu": nu, "pc": pc, "pv": pv, "rows": send_rows},
        {"msg": ((SECT, ROW_EDGE + EDGE1, 128), f32), "one": face, "two": face},
        {
            "inner": ((ROW_EDGE, 128), f32),
            "one": face,
            "two": face,
            "edge": ((SECT, EDGE1, 128), f32),
            "tmp": ((1024, 128), f32),
            "nu": ((256, 128), f32),
        },
        11,
    )
    one, two = swap(one, two)
    recv = to_all(msg)
    sums, local, stay = call(
        scatter_kernel,
        "deposit",
        {"rows": send_rows, "cnt": send_counts, "pc": pc, "pv": pv, "vel": vel, "nu": nu, "mag": mag},
        {"sums": ((1024, 128), f32), "local": field, "stay": ((1, NP), f32)},
        {"sums": ((1024, 128), f32), "acc": ((256, 896), f32), "local": field, "stay": ((1, NP), f32)} | materials,
        3,
        flops=2 * NP * 256 * 896,
        in_smem=("cnt",),
    )
    msg2, one2, two2, mid, rest = call(
        first_kernel,
        "first_section",
        {"edge": recv, "inner": recv, "cnt": send_counts, "basis": tables["basis"], "sums": sums, "nu": nu, "vel": vel}
        | tables
        | {"one": one, "two": two, "local": local},
        {"msg": ((SECT, ROW_EDGE + EDGE2, 128), f32), "one": face, "two": face, "mid": field, "rest": field},
        {
            "inner": ((ROW_EDGE, 128), f32),
            "edge": ((SECT, EDGE2, 128), f32),
            "one": face,
            "two": face,
            "mid": field,
            "rest": field,
            "nu": ((256, 128), f32),
        },
        13,
        in_smem=("cnt",),
    )
    one2, two2 = swap(one2, two2)
    recv2 = to_all(msg2)
    kept, arrived, part = call(
        gather_kernel,
        "take",
        {"vel": vel, "mid": mid, "pc": pc, "stay": stay, "pv": pv, "nu": nu, "mag": mag, "rest": rest}
        | {"edge": recv, "cnt": send_counts},
        {"kept": ((3, NP), f32), "arrived": ((3, 1, SECT * CAP), f32), "part": field},
        {"kept": ((3, NP), f32), "arrived": ((3, 1, SECT * CAP), f32), "part": field} | materials,
        3,
        flops=2 * NP * 512 * 384,
        in_smem=("cnt",),
    )
    (new,) = call(
        second_kernel,
        "second_section",
        {"edge": recv2, "inner": recv2} | tables | { "mid": mid, "nu": nu, "one": one2, "two": two2, "part": part},
        {"new": field},
        {"nu": ((256, 128), f32), "new": field},
        3,
    )
    new = jnp.swapaxes(new.reshape(3, TH, 2, 2, 128), 2, 3).reshape(3, TH, 2, NR)
    return new, kept, jnp.swapaxes(arrived, 0, 1)


def solution(mesh):
    return jax.shard_map(
        per_device,
        mesh=mesh,
        in_specs=(
            P(None, "az", "ax", None),
            P("az", "ax", None),
            P(None, "az", "ax", None),
            P(None, ("az", "ax")),
            P(None, ("az", "ax")),
            P(("az", "ax"), None, None),
            P(None, "ax", None),
        ),
        out_specs=(P(None, "az", "ax", None), P(None, ("az", "ax")), P(("az", "ax"), None, None)),
        check_vma=False,
    )
```

```python
import math

import jax
import jax.numpy as jnp
import ml_dtypes
import numpy as np
from jax import lax
from jax.experimental import pallas as pl
from jax.experimental.pallas import tpu as pltpu
from jax.sharding import PartitionSpec as P

NA = 512
NR = 256
KR = 32
SECT = 8
TH = NA // SECT
CAP = 128
NP = 8192
DTHETA = 2.0 * math.pi / NA
DT = 0.02
POLE_SIGNS = (-1.0, -1.0, 1.0)
f32 = jnp.float32
bf16 = jnp.bfloat16
i32 = jnp.int32
VMEM_LIMIT = 65408 * 1024

ROW_B = 64
ROW_EDGE = 96
EDGE_BOUND = 12
EDGE_PART = 16
EDGE1 = 24
EDGE2 = 16
CHUNK = 1024


def table_parts(x):
    parts = []
    for _ in range(3):
        parts.append(x.astype(ml_dtypes.bfloat16))
        x = x - parts[-1].astype(np.float32)
    return np.concatenate(parts, axis=-1)


def filter_tables():
    a = np.arange(NA // 2)
    even, odd, even_mode, odd_mode = [], [], [], []
    for m in range(NA // 2 + 1):
        scale = math.sqrt((1.0 if m in (0, NA // 2) else 2.0) / NA)
        phase = 2.0 * math.pi * (m * a % NA) / NA
        rows = [scale * np.cos(phase)]
        if m not in (0, NA // 2):
            rows.append(scale * np.sin(phase))
        for row in rows:
            (odd if m % 2 else even).append(row)
            (odd_mode if m % 2 else even_mode).append(m)
    basis = np.stack([np.stack(even), np.stack(odd)]).astype(np.float32)
    modes = np.stack([np.array(even_mode), np.array(odd_mode)]).astype(np.float64)
    cutoff = 4.0 * (np.arange(KR) + 0.5)
    weight = 1.0 / (1.0 + (modes[:, :, None] / cutoff) ** 4)
    weight = np.tile(weight, (1, 1, 128 // KR)).astype(np.float32)
    return table_parts(basis), table_parts(basis.transpose(0, 2, 1)), weight


BASIS, BASIS_T, MODE_WEIGHT = filter_tables()


def lane_iota(shape):
    return lax.broadcasted_iota(i32, shape, len(shape) - 1)


def row_iota(shape):
    return lax.broadcasted_iota(i32, shape, len(shape) - 2)


def strided(c, z, h):
    return pl.ds(c * 256 + h * 2 + z, TH, stride=4)


def block(c, z, h):
    return pl.ds(((c * 2 + z) * 2 + h) * TH, TH)


def lanes(x, by):
    by %= 128
    return x if by == 0 else pltpu.roll(x, by, 1)


def split2(x):
    hi = x.astype(bf16)
    return hi, (x - hi.astype(f32)).astype(bf16)


def pack_inner(field, nu):
    lane = lane_iota((TH, 128))

    def four(p, q, r, s):
        low = jnp.where(lane < 32, p, lanes(q, 32))
        high = jnp.where(lane < 96, lanes(r, 64), lanes(s, 96))
        return jnp.where(lane < 64, low, high)

    first = four(field[0][0][0], field[0][1][0], field[1][0][0], field[1][1][0])
    second = four(field[2][0][0], field[2][1][0], nu[0], nu[1])
    return first, second


def azimuth_factors():
    lane = lane_iota((1, 128))
    radius = (lane % KR).astype(f32) + 0.5
    lap = 1.0 / (radius * radius * (DTHETA * DTHETA))
    grad = 1.0 / (2.0 * DTHETA * radius)
    return lane < 64, lap, grad, jnp.where(lane < 64, -2.0, 2.0) / radius


def both_halves(x, left):
    side = lane_iota((1, 128)) < 64
    return jnp.where(side == left, x, pltpu.roll(x, 64, 1))


def azimuth_inner(first, second):
    left, lap_factor, grad_factor, cross = azimuth_factors()
    row = row_iota((TH, 128))
    nu, swirl = both_halves(second, False), both_halves(first, False)

    def differences(x):
        after = jnp.where(row == TH - 1, 0.0, pltpu.roll(x, TH - 1, 0))
        before = jnp.where(row == 0, 0.0, pltpu.roll(x, 1, 0))
        return (after - 2.0 * x + before) * lap_factor, (after - before) * grad_factor

    lap, grad = differences(first)
    part_first = nu * lap - swirl * grad + cross * nu * pltpu.roll(grad, 64, 1)
    lap, grad = differences(second)
    return part_first, jnp.where(left, nu * lap - swirl * grad, 0.0)


def write_message(inner_ref, edge_ref, field, nu, me):
    first, second = pack_inner(field, nu)
    part_first, part_second = azimuth_inner(first, second)
    inner_ref[0:TH, :] = part_first
    inner_ref[TH:, :] = part_second[: TH // 2] + pltpu.roll(part_second[TH // 2 :], 64, 1)
    turned = jnp.concatenate([first, second], axis=0).T
    up, opposite = (me + 1) % SECT, (me + SECT // 2) % SECT
    bounds = [first[0:1], second[0:1], first[TH - 1 : TH], second[TH - 1 : TH]]
    for t in range(SECT):
        for k in range(4):
            edge_ref[t, EDGE_BOUND + k : EDGE_BOUND + k + 1, :] = bounds[k]
    for c in range(3):
        for z in range(2):
            for h in range(2):
                x = field[c][z][h]
                row = (c * 2 + z) * 2 + h
                for t in range(SECT):
                    edge = jnp.where(t == up, x[TH - 1 : TH], x[0:1])
                    if row < 4:
                        edge = jnp.where(t == opposite, turned[row * 32 : row * 32 + 1], edge)
                    edge_ref[t, row : row + 1, :] = edge


def send_inner(out, rows):
    for t in range(SECT):
        out.copy(out.vmem("inner"), out.hbm("msg").at[t, 0:rows, :])


def write_axial(one_ref, two_ref, field, slab):
    odd = slab % 2 == 1
    for c in range(3):
        for h in range(2):
            rows = pl.ds((c * 2 + h) * TH, TH)
            low, high = field[c][0][h], field[c][1][h]
            one_ref[rows, :] = jnp.where(odd, low, high)
            two_ref[rows, :] = jnp.where(odd, high, low)


class Inputs:
    def __init__(self, names, refs, bufs, sems):
        self.refs = dict(zip(names, bufs))
        self.copies = {}
        for i, (name, ref, buf) in enumerate(zip(names, refs, bufs)):
            if name == "inner":
                ref = ref.at[:, 0:ROW_EDGE, :]
            if name == "edge":
                ref = ref.at[:, ROW_EDGE:, :]
            if name == "basis_t":
                own = lax.axis_index("az") % 4
                ref = ref.at[:, pl.ds(pl.multiple_of(own * TH, TH), TH), :]
            self.copies[name] = [pltpu.make_async_copy(ref, buf, sems.at[i])]
            self.copies[name][0].start()

    def __call__(self, name):
        for copy in self.copies.pop(name, ()):
            copy.wait()
        return self.refs[name]


class Outputs:
    def __init__(self, names, refs, bufs, sems):
        self.refs, self.bufs, self.sems, self.started = dict(zip(names, refs)), bufs, sems, []

    def hbm(self, name):
        return self.refs[name]

    def vmem(self, name):
        return self.bufs[name]

    def copy(self, src, dst):
        copy = pltpu.make_async_copy(src, dst, self.sems.at[len(self.started)])
        copy.start()
        self.started.append(copy)

    def send(self, name):
        self.copy(self.bufs[name], self.refs[name])

    def finish(self):
        for copy in self.started:
            copy.wait()


def pack_kernel(inp, out):
    me = lax.axis_index("az")
    tmp_ref, nu_s, edge_ref = out.vmem("tmp"), out.vmem("nu"), out.vmem("edge")
    vel_ref, nu_ref = inp("vel"), inp("nu")
    field = [[[vel_ref[strided(c, z, h), :] for h in range(2)] for z in range(2)] for c in range(3)]
    nu_s[...] = nu_ref[...].astype(f32)
    nu = [nu_s[pl.ds(z, TH, stride=4), :] for z in range(2)]
    write_message(out.vmem("inner"), edge_ref, field, nu, me)
    send_inner(out, ROW_EDGE)
    write_axial(out.vmem("one"), out.vmem("two"), field, lax.axis_index("ax"))
    out.send("one")
    out.send("two")
    pv_ref, pc_ref = inp("pv"), inp("pc")
    for i in range(64):
        tmp_ref[i * 8 : i * 8 + 3, :] = pv_ref[:, i * 128 : (i + 1) * 128]
        tmp_ref[512 + i * 8 : 512 + i * 8 + 3, :] = pc_ref[:, i * 128 : (i + 1) * 128].astype(f32)
    parts = []
    for k in range(2):
        for c in range(3):
            parts.append(jnp.concatenate(split2(tmp_ref[pl.ds(k * 512 + c, 64, stride=8), :]), axis=1))
    rows_ref = inp("rows")
    listed = [rows_ref[0, t : t + 1, :] for t in range(SECT)]
    low = jnp.concatenate([one_hot(row % 128, 128, 128) for row in listed], axis=1)
    high = [row_iota((64, 128)) == row // 128 for row in listed]
    picked = jnp.dot(
        jnp.concatenate(parts, axis=0), jnp.concatenate([low, low], axis=0), preferred_element_type=f32
    )
    for t in range(SECT):
        for q in range(6):
            value = picked[q * 64 : (q + 1) * 64, t * 128 : (t + 1) * 128]
            edge_ref[t, EDGE_PART + q : EDGE_PART + q + 1, :] = jnp.sum(
                jnp.where(high[t], value, 0.0), axis=0, keepdims=True
            )
    out.copy(edge_ref, out.hbm("msg").at[:, ROW_EDGE:, :])


def local_row(theta, r, z, me, slab):
    return ((z - 2 * slab) * 2 + r // 128) * TH + theta - me * TH


def spread(x, rows, n):
    tile = jnp.broadcast_to(x, (16, n)).astype(bf16)
    return jnp.concatenate([tile] * (rows // 16), axis=0)


def matches(index, rows, n):
    return row_iota((rows, n)).astype(f32).astype(bf16) == spread(index.astype(f32), rows, n)


def one_hot(index, rows, n):
    return jnp.where(matches(index, rows, n), jnp.ones((), bf16), jnp.zeros((), bf16))


def deposit(row, col, velocity, n):
    cols = matches(col, 128, n)
    pieces = []
    for c in range(3):
        for part in split2(velocity[c]):
            pieces.append(jnp.where(cols, spread(part.astype(f32), 128, n), jnp.zeros((), bf16)))
    pieces.append(one_hot(col, 128, n))
    return lax.dot_general(
        one_hot(row, 256, n), jnp.concatenate(pieces, axis=0), (((1,), (1,)), ((), ())), preferred_element_type=f32
    )


def add_parts(acc):
    out = [acc[:, c * 256 : c * 256 + 128] + acc[:, c * 256 + 128 : c * 256 + 256] for c in range(3)]
    out.append(acc[:, 768:896])
    return out


def write_blocks(ref, x):
    for c in range(3):
        for z in range(2):
            for h in range(2):
                ref[block(c, z, h), :] = x[c][z][h]


def write_stay(stay_ref, rows_ref, cnt_ref, me):
    lane = lane_iota((1, 128))
    lows, highs = [], []
    for t in range(SECT):
        row = rows_ref[0, t : t + 1, :]
        used = (row_iota((64, 128)) == row // 128) & (lane < cnt_ref[me, 0, t])
        highs.append(used.astype(f32).astype(bf16))
        lows.append(one_hot(row % 128, 128, 128))
    leaving = lax.dot_general(
        jnp.concatenate(highs, axis=1),
        jnp.concatenate(lows, axis=1),
        (((1,), (1,)), ((), ())),
        preferred_element_type=f32,
    )
    stay = 1.0 - leaving
    for i in range(64):
        stay_ref[0:1, i * 128 : (i + 1) * 128] = stay[i : i + 1, :]


def scatter_kernel(inp, out):
    me = lax.axis_index("az")
    slab = lax.axis_index("ax")
    stay_ref = out.vmem("stay")
    write_stay(stay_ref, inp("rows"), inp("cnt"), me)
    out.send("stay")
    pc_ref, pv_ref = inp("pc"), inp("pv")
    sum_ref, acc_ref = out.vmem("sums"), out.vmem("acc")
    for k in range(NP // CHUNK):
        part = pl.ds(k * CHUNK, CHUNK)
        row = local_row(pc_ref[0:1, part], pc_ref[1:2, part], pc_ref[2:3, part], me, slab)
        row = jnp.where(stay_ref[0:1, part] > 0.5, row, -1)
        col = pc_ref[1:2, part] % 128
        more = deposit(row, col, [pv_ref[c : c + 1, part] for c in range(3)], CHUNK)
        if k == 0:
            acc_ref[...] = more
        else:
            acc_ref[...] += more
    for c, x in enumerate(add_parts(acc_ref)):
        sum_ref[c * 256 : (c + 1) * 256, :] = x
    out.send("sums")
    rates = local_rate(input_blocks(inp), viscosity_blocks(inp, out), magnetic_blocks(inp, out))
    write_blocks(out.vmem("local"), rates)
    out.send("local")


def arrivals(edge_ref, cnt_ref, me, slab):
    lane = lane_iota((1, CAP))
    live = jnp.concatenate([(lane < cnt_ref[s, 0, me]).astype(i32) for s in range(SECT)], axis=1)

    def channel(q):
        return jnp.concatenate([edge_ref[s, EDGE_PART + q : EDGE_PART + q + 1, :] for s in range(SECT)], axis=1)

    velocity = [channel(c) for c in range(3)]
    theta, r, z = [channel(3 + c).astype(i32) for c in range(3)]
    row = jnp.where(live > 0, local_row(theta, r, z, me, slab), -1)
    return live, row, r % 128, velocity


def whole_azimuth_part(inp):
    recv_ref, edge_ref = inp("inner"), inp("edge")
    left, lap_factor, grad_factor, cross = azimuth_factors()
    bounds = []
    for k in range(4):
        at = EDGE_BOUND + k
        bounds.append(jnp.concatenate([edge_ref[t, at : at + 1, :] for t in range(SECT)], axis=0))

    def share(near, far, sign):
        nu, swirl = both_halves(near[1], False), both_halves(near[0], False)
        factor = nu * lap_factor - sign * swirl * grad_factor
        turn = cross * nu * pltpu.roll(sign * far[0] * grad_factor, 64, 1)
        return factor * far[0] + turn, jnp.where(left, factor * far[1], 0.0)

    begin, end = bounds[:2], bounds[2:]
    at_begin = share(begin, [pltpu.roll(x, 1, 0) for x in end], -1.0)
    at_end = share(end, [pltpu.roll(x, SECT - 1, 0) for x in begin], 1.0)
    row = row_iota((8, 128))
    out = ([], [])
    for t in range(SECT):
        folded = recv_ref[t, ROW_B : ROW_B + TH // 2, :]
        second = jnp.concatenate([folded, pltpu.roll(folded, 64, 1)], axis=0)
        for k, x in enumerate((recv_ref[t, 0:TH, :], jnp.where(left, second, 0.0))):
            out[k].append(x[:8] + jnp.where(row == 0, at_begin[k][t : t + 1], 0.0))
            out[k].append(x[8 : TH - 8])
            out[k].append(x[TH - 8 :] + jnp.where(row == 7, at_end[k][t : t + 1], 0.0))
    return jnp.concatenate(out[0], axis=0), jnp.concatenate(out[1], axis=0)


def table_dot(table, x):
    q = [table[:, k * 256 : (k + 1) * 256] for k in range(3)]
    hi = x.astype(bf16)
    rest = x - hi.astype(f32)
    mid = rest.astype(bf16)
    low = (rest - mid.astype(f32)).astype(bf16)
    return jnp.dot(
        jnp.concatenate([q[2], q[1], q[0], q[1], q[0], q[0]], axis=1),
        jnp.concatenate([hi, mid, low, hi, mid, hi], axis=0),
        preferred_element_type=f32,
    )


def filtered_inner(inp, me):
    part = jnp.concatenate(whole_azimuth_part(inp), axis=1)
    low, high = part[: NA // 2], part[NA // 2 :]
    basis_ref, weight_ref, basis_t_ref = inp("basis"), inp("weight"), inp("basis_t")
    out = 0.0
    for parity, x in enumerate((low + high, low - high)):
        spectrum = table_dot(basis_ref[parity], x)
        weight = weight_ref[parity]
        spectrum = spectrum * jnp.concatenate([weight, weight], axis=1)
        back = table_dot(basis_t_ref[parity], spectrum)
        if parity:
            back = jnp.where(me < 4, back, -back)
        out = out + back
    return out[:, :128], out[:, 128:]


def local_rate(field, nu, magnetic):
    lane = lane_iota((TH, 128))
    row = row_iota((TH, 128))
    rates = [[[None, None], [None, None]] for _ in range(3)]
    for z in range(2):
        rolled = [[(pltpu.roll(field[c][z][h], 1, 1), pltpu.roll(field[c][z][h], 127, 1)) for h in range(2)] for c in range(3)]
        for h in range(2):
            radius = lane_iota((1, 128)).astype(f32) + (h * 128 + 0.5)
            inverse = 1.0 / radius
            eddy = nu[z][h]
            u = [field[c][z][h] for c in range(3)]
            lap_ax, lap_rad, grad_rad, grad_ax, lap_th, grad_th = [], [], [], [], [], []
            for c in range(3):
                x = u[c]
                if h == 0:
                    prev_r = jnp.where(lane == 0, 0.0, rolled[c][0][0])
                    next_r = jnp.where(lane == 127, rolled[c][1][1], rolled[c][0][1])
                else:
                    prev_r = jnp.where(lane == 0, rolled[c][0][0], rolled[c][1][0])
                    next_r = jnp.where(lane == 127, 0.0, rolled[c][1][1])
                other = field[c][1 - z][h]
                prev_t = jnp.where(row == 0, 0.0, pltpu.roll(x, 1, 0))
                next_t = jnp.where(row == TH - 1, 0.0, pltpu.roll(x, TH - 1, 0))
                lap_rad.append(((radius + 0.5) * (next_r - x) - (radius - 0.5) * (x - prev_r)) * inverse)
                lap_ax.append(other - 2.0 * x)
                grad_rad.append(0.5 * (next_r - prev_r))
                grad_ax.append((0.5 if z == 0 else -0.5) * other)
                lap_th.append((next_t - 2.0 * x + prev_t) * (1.0 / (radius * radius * (DTHETA * DTHETA))))
                grad_th.append((next_t - prev_t) * (1.0 / (2.0 * DTHETA * radius)))
            b = [magnetic[c][z][h] for c in range(3)]
            slip = [-u[0], radius * (2.0 / NR) - u[1], -u[2]]
            current = [slip[1] * b[2] - slip[2] * b[1], slip[2] * b[0] - slip[0] * b[2], slip[0] * b[1] - slip[1] * b[0]]
            force = [
                current[1] * b[2] - current[2] * b[1],
                current[2] * b[0] - current[0] * b[2],
                current[0] * b[1] - current[1] * b[0],
            ]
            inverse2 = inverse * inverse
            metric = [
                u[1] * u[1] * inverse - eddy * u[0] * inverse2,
                -eddy * u[1] * inverse2 - u[0] * u[1] * inverse,
                0.0,
            ]
            coupling = [-2.0 * eddy * grad_th[1] * inverse, 2.0 * eddy * grad_th[0] * inverse, 0.0]
            for c in range(3):
                azimuth = eddy * lap_th[c] - u[1] * grad_th[c] + coupling[c]
                if h == 0:
                    azimuth = jnp.where(lane < KR, 0.0, azimuth)
                rates[c][z][h] = (
                    eddy * (lap_rad[c] + lap_ax[c])
                    - (u[0] * grad_rad[c] + u[2] * grad_ax[c])
                    + metric[c]
                    + 0.5 * force[c]
                    + azimuth
                )
    return rates


def outer_rate(filtered, field, nu, inp, me, slab):
    edge_ref, one_ref, two_ref = inp("edge"), inp("one"), inp("two")
    before_sector = (me + SECT - 1) % SECT
    after_sector = (me + 1) % SECT
    opposite = (me + SECT // 2) % SECT
    odd = slab % 2 == 1
    lane = lane_iota((TH, 128))
    row = row_iota((8, 128))
    turned = jnp.concatenate([edge_ref[opposite, 0:8, :], jnp.zeros((120, 128), f32)], axis=0).T
    rates = [[[None, None], [None, None]] for _ in range(3)]
    for z in range(2):
        for h in range(2):
            radius = lane_iota((1, 128)).astype(f32) + (h * 128 + 0.5)
            lap_factor = 1.0 / (radius * radius * (DTHETA * DTHETA))
            grad_factor = 1.0 / (2.0 * DTHETA * radius)
            cross = 2.0 * grad_factor / radius
            eddy, u = nu[z][h], [field[c][z][h] for c in range(3)]
            by_face = eddy + (0.5 if z == 0 else -0.5) * u[2]
            end = slab == (0 if z == 0 else lax.axis_size("ax") - 1)
            halos = []
            for sector, at, sign in ((before_sector, slice(0, 8), -1.0), (after_sector, slice(TH - 8, TH), 1.0)):
                f = [edge_ref[sector, (c * 2 + z) * 2 + h : (c * 2 + z) * 2 + h + 1, :] for c in range(3)]
                nu8, swirl8 = eddy[at], u[1][at]
                by_halo = nu8 * lap_factor - sign * swirl8 * grad_factor
                extra = [-sign * cross * nu8 * f[1], sign * cross * nu8 * f[0], 0.0]
                keep = row == (0 if sign < 0 else 7)
                if h == 0:
                    keep = keep & (lane_iota((8, 128)) >= KR)
                halos.append([jnp.where(keep, by_halo * f[c] + extra[c], 0.0) for c in range(3)])
            for c in range(3):
                face = pl.ds((c * 2 + h) * TH, TH)
                one, two = one_ref[face, :], two_ref[face, :]
                face = jnp.where(odd, one, two) if z == 0 else jnp.where(odd, two, one)
                rate = jnp.where(end, 0.0, face) * by_face
                if h == 0:
                    offset = (c % 2) * 64 + z * 32
                    pole = turned[TH:] if c == 2 else turned[:TH]
                    ghost = POLE_SIGNS[c] * lanes(pole, -((c % 2) * 2 + z))
                    rate = rate + jnp.where(lane < KR, lanes(filtered[c // 2], -offset), 0.0)
                    rate = rate + jnp.where(lane == 0, 0.5 * u[0] * ghost, 0.0)
                rates[c][z][h] = jnp.concatenate(
                    [rate[:8] + halos[0][c], rate[8 : TH - 8], rate[TH - 8 :] + halos[1][c]], axis=0
                )
    return rates


def viscosity_blocks(inp, out):
    nu_s = out.vmem("nu")
    nu_s[...] = inp("nu")[...].astype(f32)
    return [[nu_s[strided(0, z, h), :] for h in range(2)] for z in range(2)]


def magnetic_blocks(inp, out):
    mag_s = out.vmem("mag")
    mag_s[...] = inp("mag")[...].astype(f32)
    return [[[mag_s[strided(c, z, h), :] for h in range(2)] for z in range(2)] for c in range(3)]


def input_blocks(inp):
    vel_ref = inp("vel")
    return [[[vel_ref[strided(c, z, h), :] for h in range(2)] for z in range(2)] for c in range(3)]


def blocks(ref):
    return [[[ref[block(c, z, h), :] for h in range(2)] for z in range(2)] for c in range(3)]


def short_arrivals(edge_ref, cnt_ref, me, slab):
    lane = lane_iota((1, CAP))
    half = CAP // 2
    order = [(me + k) % SECT for k in (1, SECT - 1, 2, 3, 4, 5, 6)]

    def pick(get):
        full = [get(s, lane) for s in order[:2]]
        pairs = [
            jnp.where(lane < half, get(order[k], lane), pltpu.roll(get(order[k + 1], lane), half, 1)) for k in (2, 4)
        ]
        return jnp.concatenate(full + pairs + [jnp.where(lane < half, get(order[6], lane), 0.0)], axis=1)

    live = pick(lambda s, lane: (lane < cnt_ref[s, 0, me]).astype(f32))
    values = [pick(lambda s, lane, q=q: edge_ref[s, EDGE_PART + q : EDGE_PART + q + 1, :]) for q in range(6)]
    theta, r, z = [x.astype(i32) for x in values[3:]]
    row = jnp.where(live > 0.5, local_row(theta, r, z, me, slab), -1)
    return row, r % 128, values[:3]


def first_kernel(inp, out):
    me = lax.axis_index("az")
    slab = lax.axis_index("ax")
    row, col, velocity = short_arrivals(inp("edge"), inp("cnt"), me, slab)
    arrived = add_parts(deposit(row, col, velocity, 5 * CAP))
    filtered = filtered_inner(inp, me)
    sum_ref = inp("sums")
    total = [sum_ref[c * 256 : (c + 1) * 256, :] + arrived[c] for c in range(4)]
    nu, field = viscosity_blocks(inp, out), input_blocks(inp)
    rates = outer_rate(filtered, field, nu, inp, me, slab)
    local_ref = inp("local")
    mid_ref, rest_ref = out.vmem("mid"), out.vmem("rest")
    mid = [[[None, None], [None, None]] for _ in range(3)]
    for c in range(3):
        for z in range(2):
            for h in range(2):
                at = slice((z * 2 + h) * TH, (z * 2 + h + 1) * TH)
                x, s, n = field[c][z][h], total[c][at], total[3][at]
                u1 = x + DT * (local_ref[block(c, z, h), :] + rates[c][z][h] + 2.0 * (s - n * x))
                mid[c][z][h] = u1
                mid_ref[block(c, z, h), :] = u1
                rest_ref[block(c, z, h), :] = 0.5 * (x + u1) + DT * (0.8 * s + 0.2 * n * x - n * u1)
    out.send("mid")
    out.send("rest")
    write_message(out.vmem("inner"), out.vmem("edge"), mid, [nu[z][0] for z in range(2)], me)
    send_inner(out, ROW_EDGE)
    out.copy(out.vmem("edge"), out.hbm("msg").at[:, ROW_EDGE:, :])
    write_axial(out.vmem("one"), out.vmem("two"), mid, slab)
    out.send("one")
    out.send("two")


def take(pick, row, col, n):
    got = jnp.dot(pick, one_hot(row, 256, n), preferred_element_type=f32)
    got = got[:384] + got[384:]
    cols = row_iota((128, n)) == col
    return [jnp.sum(jnp.where(cols, got[c * 128 : (c + 1) * 128], 0.0), axis=0, keepdims=True) for c in range(3)]


def gather_kernel(inp, out):
    me = lax.axis_index("az")
    slab = lax.axis_index("ax")
    pc_ref, stay_ref, pv_ref = inp("pc"), inp("stay"), inp("pv")
    kept_ref, arr_ref = out.vmem("kept"), out.vmem("arrived")
    vel_ref, mid_ref = inp("vel"), inp("mid")
    parts = []
    for c in range(3):
        rows = []
        for z in range(2):
            for h in range(2):
                rows.append(0.08 * vel_ref[strided(c, z, h), :] + 0.1 * mid_ref[block(c, z, h), :])
        parts.append(split2(jnp.concatenate(rows, axis=0).T))
    pick = jnp.concatenate([p[0] for p in parts] + [p[1] for p in parts], axis=0)
    for k in range(NP // CHUNK):
        part = pl.ds(k * CHUNK, CHUNK)
        row = local_row(pc_ref[0:1, part], pc_ref[1:2, part], pc_ref[2:3, part], me, slab)
        stay = stay_ref[0:1, part] > 0.5
        row = jnp.where(stay, row, -1)
        got = take(pick, row, pc_ref[1:2, part] % 128, CHUNK)
        for c in range(3):
            kept_ref[c : c + 1, part] = jnp.where(stay, 0.82 * pv_ref[c : c + 1, part] + got[c], 0.0)
    out.send("kept")
    rates = local_rate(blocks(mid_ref), viscosity_blocks(inp, out), magnetic_blocks(inp, out))
    rest_ref, part_ref = inp("rest"), out.vmem("part")
    for c in range(3):
        for z in range(2):
            for h in range(2):
                part_ref[block(c, z, h), :] = rest_ref[block(c, z, h), :] + (0.5 * DT) * rates[c][z][h]
    out.send("part")
    live, row, col, velocity = arrivals(inp("edge"), inp("cnt"), me, slab)
    got = take(pick, row, col, SECT * CAP)
    for c in range(3):
        arr_ref[c, 0:1, :] = jnp.where(live > 0, 0.82 * velocity[c] + got[c], 0.0)
    out.send("arrived")


def second_kernel(inp, out):
    me = lax.axis_index("az")
    slab = lax.axis_index("ax")
    filtered = filtered_inner(inp, me)
    rates = outer_rate(filtered, blocks(inp("mid")), viscosity_blocks(inp, out), inp, me, slab)
    part_ref, new_ref = inp("part"), out.vmem("new")
    for c in range(3):
        for z in range(2):
            for h in range(2):
                new_ref[strided(c, z, h), :] = part_ref[block(c, z, h), :] + (0.5 * DT) * rates[c][z][h]
        rows = pl.ds(c * 256, 256)
        out.copy(new_ref.at[rows, :], out.hbm("new").at[rows, :])


def call(kernel, name, ins, outs, bufs, copies, flops=0, in_smem=()):
    in_names, out_names, buf_names = list(ins), list(outs), list(bufs)
    arrays = [ins[n] for n in in_names]
    n_in, n_out = len(in_names), len(out_names)

    def body(*refs):
        in_refs, refs = refs[:n_in], refs[n_in:]
        out_refs, refs = refs[:n_out], refs[n_out:]
        in_bufs, refs = refs[:n_in], refs[n_in:]
        buf_refs, (in_sems, out_sems) = refs[:-2], refs[-2:]
        out = Outputs(out_names, out_refs, dict(zip(buf_names, buf_refs)), out_sems)
        kernel(Inputs(in_names, in_refs, in_bufs, in_sems), out)
        out.finish()

    def in_shape(n):
        shape = ins[n].shape
        if n == "basis_t":
            return (2, TH, shape[2])
        return {"inner": (SECT, ROW_EDGE, 128), "edge": (SECT, shape[1] - ROW_EDGE, 128)}.get(n, shape)

    hbm = pl.BlockSpec(memory_space=pltpu.HBM)
    return pl.pallas_call(
        body,
        out_shape=[jax.ShapeDtypeStruct(*outs[n]) for n in out_names],
        in_specs=[hbm] * n_in,
        out_specs=[hbm] * n_out,
        scratch_shapes=[(pltpu.SMEM if n in in_smem else pltpu.VMEM)(in_shape(n), ins[n].dtype) for n in in_names]
        + [pltpu.VMEM(*bufs[n]) for n in buf_names]
        + [pltpu.SemaphoreType.DMA((n_in,)), pltpu.SemaphoreType.DMA((copies,))],
        compiler_params=pltpu.CompilerParams(vmem_limit_bytes=VMEM_LIMIT),
        cost_estimate=pl.CostEstimate(flops=flops, bytes_accessed=2 * 1024 * 1024, transcendentals=0),
        name=name,
    )(*arrays)


def rows_of(x):
    lead = x.shape[:-2]
    x = x.reshape(*lead, 2, 2, 128)
    return jnp.swapaxes(x, -3, -2).reshape(-1, 128)


def per_device(velocity, viscosity, bfield, particle_velocity, particle_cell, send_rows, send_counts):
    ax = lax.axis_size("ax")
    vel, nu, mag = rows_of(velocity), rows_of(viscosity), rows_of(bfield)
    pv, pc = particle_velocity, particle_cell
    tables = {"basis": jnp.asarray(BASIS), "weight": jnp.asarray(MODE_WEIGHT), "basis_t": jnp.asarray(BASIS_T)}
    swap_one = [(i, i ^ 1) for i in range(ax)]
    swap_two = []
    for a in range(SECT):
        swap_two += [(a * ax + i, a * ax + ((i + 1) ^ 1) - 1) for i in range(1, ax - 1)]
        swap_two += [(a * ax + i, (a ^ 2) * ax + i) for i in (0, ax - 1)]

    def swap(one, two):
        return lax.ppermute(one, "ax", swap_one), lax.ppermute(two, ("az", "ax"), swap_two)

    def to_all(msg):
        return lax.all_to_all(msg, "az", split_axis=0, concat_axis=0, tiled=True)

    face = ((384, 128), f32)
    field = ((768, 128), f32)
    materials = {"nu": ((256, 128), f32), "mag": field}
    msg, one, two = call(
        pack_kernel,
        "pack",
        {"vel": vel, "nu": nu, "pc": pc, "pv": pv, "rows": send_rows},
        {"msg": ((SECT, ROW_EDGE + EDGE1, 128), f32), "one": face, "two": face},
        {
            "inner": ((ROW_EDGE, 128), f32),
            "one": face,
            "two": face,
            "edge": ((SECT, EDGE1, 128), f32),
            "tmp": ((1024, 128), f32),
            "nu": ((256, 128), f32),
        },
        11,
    )
    one, two = swap(one, two)
    recv = to_all(msg)
    sums, local, stay = call(
        scatter_kernel,
        "deposit",
        {"rows": send_rows, "cnt": send_counts, "pc": pc, "pv": pv, "vel": vel, "nu": nu, "mag": mag},
        {"sums": ((1024, 128), f32), "local": field, "stay": ((1, NP), f32)},
        {"sums": ((1024, 128), f32), "acc": ((256, 896), f32), "local": field, "stay": ((1, NP), f32)} | materials,
        3,
        flops=2 * NP * 256 * 896,
        in_smem=("cnt",),
    )
    msg2, one2, two2, mid, rest = call(
        first_kernel,
        "first_section",
        {"edge": recv, "inner": recv, "cnt": send_counts, "basis": tables["basis"], "sums": sums, "nu": nu, "vel": vel}
        | tables
        | {"one": one, "two": two, "local": local},
        {"msg": ((SECT, ROW_EDGE + EDGE2, 128), f32), "one": face, "two": face, "mid": field, "rest": field},
        {
            "inner": ((ROW_EDGE, 128), f32),
            "edge": ((SECT, EDGE2, 128), f32),
            "one": face,
            "two": face,
            "mid": field,
            "rest": field,
            "nu": ((256, 128), f32),
        },
        13,
        in_smem=("cnt",),
    )
    one2, two2 = swap(one2, two2)
    recv2 = to_all(msg2)
    kept, arrived, part = call(
        gather_kernel,
        "take",
        {"vel": vel, "mid": mid, "pc": pc, "stay": stay, "pv": pv, "nu": nu, "mag": mag, "rest": rest}
        | {"edge": recv, "cnt": send_counts},
        {"kept": ((3, NP), f32), "arrived": ((3, 1, SECT * CAP), f32), "part": field},
        {"kept": ((3, NP), f32), "arrived": ((3, 1, SECT * CAP), f32), "part": field} | materials,
        3,
        flops=2 * NP * 512 * 384,
        in_smem=("cnt",),
    )
    (new,) = call(
        second_kernel,
        "second_section",
        {"edge": recv2, "inner": recv2} | tables | { "mid": mid, "nu": nu, "one": one2, "two": two2, "part": part},
        {"new": field},
        {"nu": ((256, 128), f32), "new": field},
        3,
    )
    new = jnp.swapaxes(new.reshape(3, TH, 2, 2, 128), 2, 3).reshape(3, TH, 2, NR)
    return new, kept, jnp.swapaxes(arrived, 0, 1)


def solution(mesh):
    return jax.shard_map(
        per_device,
        mesh=mesh,
        in_specs=(
            P(None, "az", "ax", None),
            P("az", "ax", None),
            P(None, "az", "ax", None),
            P(None, ("az", "ax")),
            P(None, ("az", "ax")),
            P(("az", "ax"), None, None),
            P(None, "ax", None),
        ),
        out_specs=(P(None, "az", "ax", None), P(None, ("az", "ax")), P(("az", "ax"), None, None)),
        check_vma=False,
    )
```
